128 devices in a mesh: dp: 16 (over y, x), expert: 8 (over z, core).
Axes of the slice: x: 4, y: 4, z: 4, core: 2. Of those that a mesh axis runs over, the one named last changes fastest.
Arguments:
- tokens: bfloat16 [24576, 1536], P(('dp', 'expert')), may hold values from -6 to 6
- cotangent: bfloat16 [24576, 1536], P(('dp', 'expert')), may hold values from -6 to 6
- seq_lengths: int32 [16, 3], P('dp'), may hold values from 1 to 1024, 1536 in all within a row
- position_map: int32 [16, 1536], P('dp'), may hold values from 0 to 1535, each once within a row
- routes: int32 [24576, 8], P(('dp', 'expert')), may hold values from 0 to 39, all different within a row
- turn_order: int32 [128, 1536], P(('dp', 'expert')), may hold values from 0 to 1535, each once within a row
- norm_gain: float32 [1536], replicated, may hold values from 0.5 to 1.5
- ffn_gain: float32 [1536], replicated, may hold values from 0.5 to 1.5
- w_query: bfloat16 [1536, 1536], P('dp'), may hold values from -0.15625 to 0.15625
- key_weight: bfloat16 [1536, 512], P('dp'), may hold values from -0.15625 to 0.15625
- value_weight: bfloat16 [1536, 512], P('dp'), may hold values from -0.15625 to 0.15625
- w_out: bfloat16 [1536, 1536], P('dp'), may hold values from -2.5 to 2.5
- w_router: bfloat16 [1536, 40], replicated, may hold values from -0.078125 to 0.078125
- w_gate_up: bfloat16 [40, 1536, 1024], P('expert'), may hold values from -0.15625 to 0.15625
- w_down: bfloat16 [40, 512, 1536], P('expert'), may hold values from -1 to 1
Outputs:
- output: bfloat16 [24576, 1536], P(('dp', 'expert'))
- d_tokens: bfloat16 [24576, 1536], P(('dp', 'expert'))
- grad_norm_gain: float32 [1536], replicated
- grad_ffn_gain: float32 [1536], replicated
- grad_query: float32 [1536, 1536], P('dp')
- grad_key: float32 [1536, 512], P('dp')
- grad_value: float32 [1536, 512], P('dp')
- grad_out: float32 [1536, 1536], P('dp')
- grad_router: float32 [1536, 40], replicated
- grad_gate_up: float32 [40, 1536, 1024], P('expert', 'dp')
- grad_down: float32 [40, 512, 1536], P('expert', None, 'dp')
The draws below stay inside these ranges and needn't reach their ends.
Inputs may be any that keep to these rules, and one draw needn't show every extreme that they name: `routes`: each row names 8 different experts. `turn_order`: each row is an ordering of the 1536 pairs of one device, pair t * 8 + k. `position_map`: each row is a permutation. `seq_lengths`: each row sums to 1536; its largest is 1024.
All inputs are finite; a program needn't handle non-finite values.
Results may differ from the reference program's by a relative error of at most 0.025.
Values may be sent and summed in bfloat16 or wider, within the bound.
No kernel may reach another device: no remote copies, remote signals or barrier semaphores. Data moves between devices by JAX's collectives and lax.ppermute only.
A program may use at most 256 MiB of HBM per device.

```python
import math
import jax
import jax.numpy as jnp
import numpy as np
from jax import lax

MODEL_WIDTH = 1536
QUERY_HEADS = 24
KEY_VALUE_HEADS = 8
HEAD_SIZE = 64
FF = 512
TOP = 8
SEQS = 3
EXPERTS = 40
GROUP_TOKENS = 1536
TOK_DEV = 192
TOKENS = 24576
LONGEST = 1024
CAP = 43
N_DP = 16
N_EXPERT = 8
DEVICES = 128


def steps_of(key, extent, split, smallest, top_value):
    factor_of = 1.0
    for axis_at, shards_of in split:
        heights = jax.random.uniform(jax.random.fold_in(jax.random.fold_in(key, 6), axis_at), (shards_of,), jnp.float32, smallest / len(split), top_value / len(split))
        factor_of = factor_of * jnp.repeat(jnp.exp(heights), extent[axis_at] // shards_of).reshape((-1,) + (1,) * (len(extent) - 1 - axis_at))
    return factor_of


def distinct(key, rows, count, top, lift):
    order = jax.random.permutation(jax.random.fold_in(key, 1), count)
    pull = order
    for power in range(3):
        pull = pull * pull // count
    pull = pull * lift // count
    chance = jax.random.randint(jax.random.fold_in(key, 2), (rows, count), 0, 4096) + pull
    sure = jax.random.permutation(jax.random.fold_in(key, 3), rows)[jnp.arange(count) % rows]
    chance = jnp.where(jnp.arange(rows)[:, None] == sure[None, :], 1 << 14, chance)
    merit = chance * count + jnp.arange(count)
    return lax.top_k(merit.astype(jnp.int32), top)[1].astype(jnp.int32)


def length_profile(count, total, reach, slope):
    weights = [(1 << 20) // math.isqrt(grade ** slope) + 1 for grade in range(2, count + 1)]
    surplus, holding = total - reach - (count - 1), [1] * (count - 1)
    while surplus > 0:
        movable = [i for i in range(count - 1) if holding[i] < reach]
        pool, budget = sum([weights[i] for i in movable]), surplus
        for i in movable:
            extra = min(reach - holding[i], max(1, budget * weights[i] // pool), surplus)
            holding[i] = holding[i] + extra
            surplus = surplus - extra
    return np.array([reach] + holding)


def ragged(rng, number_of, total, most, skew):
    if number_of == 2:
        one = jax.random.randint(rng, (), max(1, total - most), min(most, total - 1) + 1)
        return jnp.stack([one, total - one])
    tallies = jnp.asarray(length_profile(number_of, total, most, skew), jnp.int32)
    couples = (number_of - 1) // 2
    source_of, taker = tallies[1:1 + 2 * couples:2], tallies[2:2 + 2 * couples:2]
    room = jnp.minimum(source_of - 1, most - taker)
    passed = jax.random.randint(jax.random.fold_in(rng, 1), (couples,), 0, 1 << 20) % (room + 1)
    tallies = tallies.at[1:1 + 2 * couples:2].set(source_of - passed).at[2:2 + 2 * couples:2].set(taker + passed)
    return tallies[jax.random.permutation(jax.random.fold_in(rng, 2), number_of)]


def scatter_about(key, dims, spread, bound, split=(), kind=jnp.bfloat16):
    entries = jax.random.normal(key, dims, jnp.float32) * spread
    if len(split) > 0:
        entries = steps_of(key, dims, split, -0.22, 0.18) * entries
    return jnp.clip(entries, min=-bound, max=bound).astype(kind)


def setup_inputs(seed: int = 0) -> dict:
    splits = jax.random.split(jax.random.key(seed), 16)
    tokens = scatter_about(splits[0], (TOKENS, MODEL_WIDTH), 1.0, 6.0, ((0, 128),))
    cotangent = scatter_about(splits[1], (TOKENS, MODEL_WIDTH), 1.0, 6.0, ((0, 128),))
    seq_lengths = jax.vmap(lambda own: ragged(own, SEQS, GROUP_TOKENS, LONGEST, 1))(jax.random.split(splits[2], N_DP)).reshape((N_DP, SEQS)).astype(jnp.int32)
    position_map = jax.vmap(lambda own: jax.random.permutation(own, GROUP_TOKENS))(jax.random.split(splits[3], N_DP)).reshape((N_DP, GROUP_TOKENS)).astype(jnp.int32)
    routes = distinct(splits[4], TOKENS, EXPERTS, TOP, 1638)
    turn_order = jax.vmap(lambda own: jax.random.permutation(own, TOK_DEV * TOP))(jax.random.split(splits[5], DEVICES)).reshape((DEVICES, TOK_DEV * TOP)).astype(jnp.int32)
    norm_gain = jnp.clip(1.0 + 0.1 * jax.random.normal(splits[6], (MODEL_WIDTH,), jnp.float32), 0.5, 1.5)
    ffn_gain = jnp.clip(1.0 + 0.1 * jax.random.normal(splits[7], (MODEL_WIDTH,), jnp.float32), 0.5, 1.5)
    w_query = scatter_about(splits[8], (MODEL_WIDTH, QUERY_HEADS * HEAD_SIZE), MODEL_WIDTH ** -0.5, 0.15625, ((0, 16),))
    key_weight = scatter_about(splits[9], (MODEL_WIDTH, KEY_VALUE_HEADS * HEAD_SIZE), MODEL_WIDTH ** -0.5, 0.15625, ((0, 16),))
    value_weight = scatter_about(splits[10], (MODEL_WIDTH, KEY_VALUE_HEADS * HEAD_SIZE), MODEL_WIDTH ** -0.5, 0.15625, ((0, 16),))
    w_out = scatter_about(splits[11], (QUERY_HEADS * HEAD_SIZE, MODEL_WIDTH), (max(1, QUERY_HEADS * HEAD_SIZE // 256)) ** -0.5, 2.5, ((0, 16),))
    w_router = scatter_about(splits[12], (MODEL_WIDTH, EXPERTS), (4 * MODEL_WIDTH) ** -0.5, 0.078125)
    w_gate_up = scatter_about(splits[13], (EXPERTS, MODEL_WIDTH, 2 * FF), MODEL_WIDTH ** -0.5, 0.15625, ((0, 8),))
    w_down = scatter_about(splits[14], (EXPERTS, FF, MODEL_WIDTH), (max(1, FF // 16)) ** -0.5, 1.0, ((0, 8),))
    return {"tokens": tokens, "cotangent": cotangent, "seq_lengths": seq_lengths, "position_map": position_map, "routes": routes, "turn_order": turn_order, "norm_gain": norm_gain, "ffn_gain": ffn_gain, "w_query": w_query, "key_weight": key_weight, "value_weight": value_weight, "w_out": w_out, "w_router": w_router, "w_gate_up": w_gate_up, "w_down": w_down}


@jax.custom_vjp
def lower_precision(v):
    return lax.optimization_barrier(v.astype(jnp.bfloat16)).astype(jnp.float32)

@jax.custom_vjp
def low_back(v):
    return v

def low_keep(v):
    return (lower_precision(v), None)

def low_pass(kept, grad):
    return (grad,)

def back_keep(v):
    return (v, None)

def back_low(kept, grad):
    return (lower_precision(grad),)
lower_precision.defvjp(low_keep, low_pass)
low_back.defvjp(back_keep, back_low)
EXACT = lax.Precision.HIGHEST
EPSILON = 1e-06
MASKED = -1e+30

def matmul(left, right):
    return jnp.dot(left, right, precision=EXACT, preferred_element_type=jnp.float32)

def normed(values, gain):
    return values * lax.rsqrt(lax.optimization_barrier(jnp.mean(values * values, axis=-1, keepdims=True)) + EPSILON) * gain

def rotary(position, half_dim):
    frequency = 10000.0 ** (-(jnp.arange(half_dim, dtype=jnp.float32) * 2.0) / (2.0 * half_dim))
    angles = position.astype(jnp.float32)[:, None] * frequency[None, :]
    rotary_cosine = jnp.cos(angles)
    rotary_sine = jnp.sin(angles)
    return (jnp.concatenate([rotary_cosine, rotary_cosine], -1), jnp.concatenate([rotary_sine, rotary_sine], -1))

def apply_rotary(values, rotary_cosine, rotary_sine):
    half_dim = values.shape[-1] // 2
    turned = jnp.concatenate([-values[..., half_dim:], values[..., :half_dim]], -1)
    return values * rotary_cosine[:, None, :] + turned * rotary_sine[:, None, :]

def stream_info(lengths, stream):
    starts = (jnp.cumsum(lengths) - lengths).astype(jnp.int32)
    sequence = lax.optimization_barrier(jnp.sum((stream[:, None] >= starts[None, 1:]).astype(jnp.int32), axis=1)).astype(jnp.int32)
    chosen = sequence[:, None] == jnp.arange(lengths.shape[0], dtype=jnp.int32)[None, :]
    seq_begin = lax.optimization_barrier(jnp.sum(jnp.where(chosen, starts[None, :], 0), axis=1)).astype(jnp.int32)
    return (sequence, (stream - seq_begin).astype(jnp.int32))

def slot_table(route_rows, order, experts, capacity):
    flat_routes = route_rows.reshape(-1).astype(jnp.int32)
    turn_expert = flat_routes[order]
    onehot = (turn_expert[:, None] == jnp.arange(experts, dtype=jnp.int32)[None, :]).astype(jnp.int32)
    before = (jnp.cumsum(onehot, axis=0) - onehot).astype(jnp.int32)
    slot_turn = lax.optimization_barrier(jnp.sum(before * onehot, axis=1)).astype(jnp.int32)
    slot_pair = jnp.zeros_like(flat_routes).at[order].set(slot_turn)
    kept_pair = slot_pair < capacity
    destination = jnp.where(kept_pair, flat_routes * capacity + slot_pair, experts * capacity)
    return (destination.astype(jnp.int32), kept_pair)

def pick_rows(table, index):
    return table[index]

def fill_slots(destination, token_ids):
    return jnp.full((EXPERTS * CAP,), -1, jnp.int32).at[destination].set(token_ids, mode='drop')

def device_slots(route_rows, order):
    return slot_table(route_rows, order, EXPERTS, CAP)

def reference(tokens, cotangent, seq_lengths, position_map, routes, turn_order, norm_gain, ffn_gain, w_query, key_weight, value_weight, w_out, w_router, w_gate_up, w_down):
    pairs = TOK_DEV * TOP
    route_groups = routes.reshape(N_DP, GROUP_TOKENS, TOP)
    order_groups = turn_order.reshape(N_DP, N_EXPERT, pairs)
    token_ids = (jnp.arange(N_EXPERT, dtype=jnp.int32)[:, None] * TOK_DEV + jnp.arange(pairs, dtype=jnp.int32)[None, :] // TOP).astype(jnp.int32)
    score_scale = HEAD_SIZE ** (-0.5)

    def layer(token_rows, gain_one, gain_two, query_w, key_w, value_w, out_w, router_w, gate_up_w, down_w):

        def one_group(inputs):
            rows_in, route_rows, orders, lengths, stream = inputs
            sequence, position = stream_info(lengths, stream)
            visible = (sequence[:, None] == sequence[None, :]) & (position[None, :] <= position[:, None])
            rotary_cosine, rotary_sine = rotary(position, HEAD_SIZE // 2)
            normal_one = lower_precision(normed(rows_in, gain_one))
            query = low_back(matmul(normal_one, query_w))
            key = low_back(matmul(normal_one, key_w))
            value_matrix = low_back(matmul(normal_one, value_w))
            rotated_query = lower_precision(apply_rotary(query.reshape(GROUP_TOKENS, QUERY_HEADS, HEAD_SIZE), rotary_cosine, rotary_sine))
            rotated_key = lower_precision(apply_rotary(key.reshape(GROUP_TOKENS, KEY_VALUE_HEADS, HEAD_SIZE), rotary_cosine, rotary_sine))
            value_lower_precision = lower_precision(value_matrix.reshape(GROUP_TOKENS, KEY_VALUE_HEADS, HEAD_SIZE))
            query_head_rows = rotated_query.reshape(GROUP_TOKENS, KEY_VALUE_HEADS, QUERY_HEADS // KEY_VALUE_HEADS, HEAD_SIZE).transpose(1, 0, 2, 3)

            def attend(parts):
                query_head, key_head, value_head = parts
                scores = low_back(jnp.einsum('trd,sd->rts', query_head, key_head, precision=EXACT) * score_scale)
                scores = jnp.where(visible[None], scores, MASKED)
                attn_probs = jax.nn.softmax(scores, axis=-1)
                return jnp.einsum('rts,sd->trd', lower_precision(attn_probs), value_head, precision=EXACT)
            mixed = lax.map(jax.checkpoint(attend), (query_head_rows, rotated_key.transpose(1, 0, 2), value_lower_precision.transpose(1, 0, 2)))
            attended = mixed.transpose(1, 0, 2, 3).reshape(GROUP_TOKENS, QUERY_HEADS * HEAD_SIZE)
            attended = lower_precision(low_back(attended))
            hidden_one = rows_in + low_back(matmul(attended, out_w))
            normal_two = lower_precision(normed(hidden_one, gain_two))
            logits = matmul(normal_two, router_w)
            gates = jax.nn.softmax(jnp.take_along_axis(logits, route_rows, axis=1), axis=1)
            destination, kept_pair = jax.vmap(device_slots)(route_rows.reshape(N_EXPERT, TOK_DEV, TOP), orders)
            filled = jax.vmap(fill_slots)(destination, token_ids)
            expert_rows = jnp.where(filled[..., None] >= 0, normal_two[jnp.maximum(filled, 0)], 0.0)
            expert_rows = expert_rows.reshape(N_EXPERT, EXPERTS, CAP, MODEL_WIDTH).transpose(1, 0, 2, 3).reshape(EXPERTS, N_EXPERT * CAP, MODEL_WIDTH)
            expert_rows = low_back(expert_rows)
            gate_up = low_back(jnp.einsum('erd,edf->erf', expert_rows, gate_up_w, precision=EXACT))
            hidden = lower_precision(jax.nn.silu(gate_up[..., :FF]) * gate_up[..., FF:])
            expert_out = lower_precision(low_back(jnp.einsum('erf,efd->erd', hidden, down_w, precision=EXACT)))
            expert_out = expert_out.reshape(EXPERTS, N_EXPERT, CAP, MODEL_WIDTH).transpose(1, 0, 2, 3).reshape(N_EXPERT, EXPERTS * CAP, MODEL_WIDTH)
            safe_dest = jnp.minimum(destination, EXPERTS * CAP - 1)
            pair_rows = jax.vmap(pick_rows)(expert_out, safe_dest)
            pair_weight = gates.reshape(N_EXPERT, pairs) * kept_pair.astype(jnp.float32)
            mixture = lax.optimization_barrier(jnp.sum((pair_rows * pair_weight[..., None]).reshape(N_EXPERT, TOK_DEV, TOP, MODEL_WIDTH), axis=2))
            return hidden_one + mixture.reshape(GROUP_TOKENS, MODEL_WIDTH)
        grouped = lax.map(jax.checkpoint(one_group), (token_rows.reshape(N_DP, GROUP_TOKENS, MODEL_WIDTH), route_groups, order_groups, seq_lengths, position_map))
        return grouped.reshape(N_DP * GROUP_TOKENS, MODEL_WIDTH)
    floats = [array.astype(jnp.float32) for array in (tokens, norm_gain, ffn_gain, w_query, key_weight, value_weight, w_out, w_router, w_gate_up, w_down)]
    result, pullback = jax.vjp(layer, floats[0], floats[1], floats[2], floats[3], floats[4], floats[5], floats[6], floats[7], floats[8], floats[9])
    grads = pullback(cotangent.astype(jnp.float32))
    return (result.astype(jnp.bfloat16), grads[0].astype(jnp.bfloat16), grads[1], grads[2], grads[3], grads[4], grads[5], grads[6], grads[7], grads[8], grads[9])
```

```python
import functools

import jax
import jax.numpy as jnp
from jax import lax
from jax.experimental import pallas as pl
from jax.experimental.pallas import tpu as pltpu
from jax.sharding import PartitionSpec as P

MODEL_WIDTH = 1536
QUERY_HEADS = 24
KEY_VALUE_HEADS = 8
HEAD_SIZE = 64
FF = 512
TOP = 8
EXPERTS = 40

EPSILON = 1e-06
MASKED = -1e30
EXACT = lax.Precision.HIGHEST
F32 = jnp.float32
BF16 = jnp.bfloat16

ROWS = 192
BLOCKS = 8
GROUP = ROWS * BLOCKS
TILE = 256
TILES = GROUP // TILE
GROUPED = QUERY_HEADS // KEY_VALUE_HEADS
QUERY_COLS = GROUPED * HEAD_SIZE
HEAD_COLS = QUERY_COLS + 2 * HEAD_SIZE
STACK = GROUPED * TILE
CAP = 43
SLOTS = 48
LOCAL_EXPERTS = EXPERTS // BLOCKS
EXPERT_ROWS = BLOCKS * SLOTS


def dot(left, right, dims=((1,), (0,))):
    return lax.dot_general(left, right, (dims, ((), ())), preferred_element_type=F32)


def whole(shape):
    return pl.BlockSpec(shape, lambda *_: (0,) * len(shape))


class Group:
    def __init__(self, devices):
        self.count = devices
        self.along = devices // 2
        index = lax.axis_index("expert")
        self.z = index // 2
        self.core = index % 2

    def send(self, value, shift, flip=0):
        steps = [
            (z * 2 + c, ((z + shift) % self.along) * 2 + (c ^ flip))
            for z in range(self.along)
            for c in range(2)
        ]
        return lax.ppermute(value, "expert", steps)

    def swap(self, value):
        return self.send(value, 0, 1)

    def gather(self, value):
        along = [value] + [self.send(value, -kz) for kz in range(1, self.along)]
        blocks = []
        for piece in along:
            blocks += [piece, self.swap(piece)]
        return blocks, along[1:]

    def exchange(self, blocks):
        pairs = blocks.reshape((self.along, 2) + blocks.shape[1:])
        pairs = jnp.stack([pairs[:, 0], self.swap(pairs[:, 1])], 1)
        return [pairs[0]] + [
            self.send(pairs[self.along - kz], self.along - kz) for kz in range(1, self.along)
        ]

    def exchange_pairs(self, pairs):
        other = [self.swap(pair[1:]) for pair in pairs]
        pairs = [jnp.concatenate([pair[:1], o], 0) for pair, o in zip(pairs, other)]
        return [pairs[0]] + [
            self.send(pairs[self.along - kz], self.along - kz) for kz in range(1, self.along)
        ]

    def sum_scatter(self, blocks):
        pairs = blocks.reshape((self.along, 2) + blocks.shape[1:])
        other = self.swap(pairs[:, 1])
        both = pairs[:, 0].astype(F32) + other.astype(F32)
        terms = [both[0]]
        for kz in range(1, self.along):
            terms.append(self.send(both[kz].astype(BF16), kz))
        return terms

    def to_natural(self, stack):
        pairs = stack.reshape((self.along, 2) + stack.shape[1:])
        pairs = jnp.where(self.core == 1, pairs[:, ::-1], pairs)
        pairs = lax.dynamic_slice_in_dim(
            jnp.concatenate([pairs, pairs], 0), self.along - self.z, self.along, 0
        )
        return pairs.reshape(stack.shape)

    def to_blocks(self, stack):
        pairs = stack.reshape((self.along, 2) + stack.shape[1:])
        pairs = lax.dynamic_slice_in_dim(
            jnp.concatenate([pairs, pairs], 0), self.z, self.along, 0
        )
        return jnp.where(self.core == 1, pairs[:, ::-1], pairs).reshape(stack.shape)


def after(value, *events):
    return lax.optimization_barrier((value, events))[0]


def gather_dp(value, count):
    side = 4
    if count != side * side:
        return lax.all_gather(value, "dp", axis=0, tiled=True)
    index = lax.axis_index("dp")
    y, x = index // side, index % side

    def send(piece, up, right):
        steps = [
            (v * side + u, ((v + up) % side) * side + (u + right) % side)
            for v in range(side)
            for u in range(side)
        ]
        return lax.ppermute(piece, "dp", steps)

    def natural(stack, at, axis):
        return lax.dynamic_slice_in_dim(
            jnp.concatenate([stack, stack], axis), side - at, side, axis
        )

    row = jnp.stack([value] + [send(value, 0, -k) for k in range(1, side)], 0)
    row = natural(row, x, 0)
    full = jnp.stack([row] + [send(row, -k, 0) for k in range(1, side)], 0)
    return natural(full, y, 0).reshape((-1,) + value.shape[1:])


def sum_over(value, axis, count):
    step = 1
    while step < count:
        value = value + lax.ppermute(value, axis, [(i, i ^ step) for i in range(count)])
        step *= 2
    return value


def rotary(position):
    half = HEAD_SIZE // 2
    frequency = 10000.0 ** (-(jnp.arange(half, dtype=F32) * 2.0) / (2.0 * half))
    angles = position.astype(F32)[:, None] * frequency[None, :]
    cosine = jnp.cos(angles)
    sine = jnp.sin(angles)
    return (
        jnp.concatenate([cosine] * 4, -1),
        jnp.concatenate([-sine, sine, -sine, sine], -1),
    )


def stream_starts(lengths, stream):
    starts = jnp.cumsum(lengths) - lengths
    sequence = jnp.sum((stream[:, None] >= starts[None, 1:]).astype(jnp.int32), axis=1)
    chosen = sequence[:, None] == jnp.arange(lengths.shape[0], dtype=jnp.int32)[None, :]
    return jnp.sum(jnp.where(chosen, starts[None, :], 0), axis=1)


def slot_table(route_rows, order):
    rows = route_rows.shape[0]
    pairs = rows * TOP
    turns = jnp.arange(pairs, dtype=jnp.int32)
    turn = jnp.sum(jnp.where(order[None, :] == turns[:, None], turns[None, :], 0), axis=1)
    turn = turn.reshape(rows, TOP)
    hits = jnp.arange(EXPERTS, dtype=jnp.int32)[:, None, None] == route_rows[None]
    used = jnp.any(hits, axis=2)
    turn_of = jnp.sum(jnp.where(hits, turn[None], 0), axis=2)
    earlier = used[:, None, :] & (turn_of[:, None, :] < turn_of[:, :, None])
    slot = jnp.sum(earlier.astype(jnp.int32), axis=2)
    return jnp.where(used, slot, -1)


def turn(values, cosine, signed_sine):
    lane = lax.broadcasted_iota(jnp.int32, values.shape, 1) % HEAD_SIZE
    half = HEAD_SIZE // 2
    width = values.shape[1]
    other = jnp.where(
        lane < half,
        pltpu.roll(values, width - half, 1),
        pltpu.roll(values, half, 1),
    )
    return values * cosine + other * signed_sine


def visible_keys(tile, key_tile, begin):
    key_at = lax.broadcasted_iota(jnp.int32, (TILE, STACK), 0) + key_tile * TILE
    query_at = lax.broadcasted_iota(jnp.int32, (TILE, STACK), 1) % TILE + tile * TILE
    return (key_at >= begin) & (key_at <= query_at)


def attend_kernel(
    first_ref,
    *refs,
):
    normal_refs, refs = refs[:BLOCKS], refs[BLOCKS:]
    (
    weight_ref,
    cosine_ref,
    sine_ref,
    stream_ref,
    begin_ref,
    out_ref,
    query_ref,
    key_ref,
    value_ref,
    total_ref,
    turned_ref,
    heads,
    place,
    ) = refs
    for b in range(BLOCKS):
        rows = pl.ds(b * ROWS, ROWS)
        cosine = cosine_ref[rows, :]
        sine = sine_ref[rows, :]
        made = dot(normal_refs[b][...], weight_ref[...])
        one = turn(made[:, :128], cosine, sine)
        two = turn(made[:, 128:256], cosine, sine)
        heads[rows, :] = jnp.concatenate([one, two, made[:, 256:]], 1).astype(BF16)
    for i in range(TILES):
        rows = pl.ds(i * TILE, TILE)
        at = lax.broadcasted_iota(jnp.int32, (TILE, GROUP), 0) + i * TILE
        chosen = (stream_ref[...] == at).astype(F32).astype(BF16)
        place[rows, :] = chosen
        ordered = dot(chosen, heads[...])
        for h in range(GROUPED):
            part = ordered[:, h * HEAD_SIZE : (h + 1) * HEAD_SIZE] * (HEAD_SIZE**-0.5)
            query_ref[i, pl.ds(h * TILE, TILE), :] = part.astype(BF16)
        key_ref[rows, :] = ordered[:, QUERY_COLS : QUERY_COLS + HEAD_SIZE].astype(BF16)
        value_ref[rows, :] = ordered[:, QUERY_COLS + HEAD_SIZE :].astype(BF16)
    for i in range(TILES):
        query = query_ref[i]
        begin = begin_ref[i]

        def step(j, carry, query=query, begin=begin, i=i):
            top, total, mixed = carry
            rows = pl.ds(pl.multiple_of(j * TILE, TILE), TILE)
            scores = dot(key_ref[rows, :], query, ((1,), (1,)))
            scores = jnp.where(visible_keys(i, j, begin), scores, MASKED)
            new_top = jnp.maximum(top, jnp.max(scores, axis=0, keepdims=True))
            weight = jnp.exp(scores - new_top)
            fade = jnp.exp(top - new_top)
            total = total * fade + jnp.sum(weight, axis=0, keepdims=True)
            mixed = mixed * fade + dot(value_ref[rows, :], weight.astype(BF16), ((0,), (0,)))
            return new_top, total, mixed

        top, total, mixed = lax.fori_loop(
            first_ref[i],
            i + 1,
            step,
            (
                jnp.full((1, STACK), MASKED, F32),
                jnp.zeros((1, STACK), F32),
                jnp.zeros((HEAD_SIZE, STACK), F32),
            ),
        )
        total_ref[i] = top + jnp.log(total)
        mixed = mixed / total
        for h in range(GROUPED):
            turned_ref[pl.ds(h * HEAD_SIZE, HEAD_SIZE), pl.ds(i * TILE, TILE)] = mixed[
                :, h * TILE : (h + 1) * TILE
            ].astype(BF16)
    out_ref[...] = dot(turned_ref[...], place[...]).T.astype(BF16)


def attend(first, normals, weight, cosine, sine, stream, begin):
    return pl.pallas_call(
        attend_kernel,
        out_shape=(
            jax.ShapeDtypeStruct((GROUP, QUERY_COLS), BF16),
            jax.ShapeDtypeStruct((TILES, STACK, HEAD_SIZE), BF16),
            jax.ShapeDtypeStruct((GROUP, HEAD_SIZE), BF16),
            jax.ShapeDtypeStruct((GROUP, HEAD_SIZE), BF16),
            jax.ShapeDtypeStruct((TILES, 1, STACK), F32),
            jax.ShapeDtypeStruct((QUERY_COLS, GROUP), BF16),
        ),
        in_specs=[pl.BlockSpec(memory_space=pltpu.SMEM)]
        + [pl.BlockSpec(memory_space=pltpu.VMEM)] * (BLOCKS + 5),
        out_specs=tuple([pl.BlockSpec(memory_space=pltpu.VMEM)] * 6),
        scratch_shapes=[pltpu.VMEM((GROUP, HEAD_COLS), BF16), pltpu.VMEM((GROUP, GROUP), BF16)],
        compiler_params=pltpu.CompilerParams(vmem_limit_bytes=56 * 2**20),
        name="attend",
    )(first, *normals, weight, cosine, sine, stream, begin)


def attend_back_kernel(
    first_ref,
    grad_ref,
    query_ref,
    key_ref,
    value_ref,
    total_ref,
    turned_ref,
    cosine_ref,
    sine_ref,
    stream_row_ref,
    stream_ref,
    begin_ref,
    *refs,
):
    out_refs, (whole_ref, grad_key, grad_value, grad_heads) = refs[:4], refs[4:]
    grad_key[...] = jnp.zeros_like(grad_key)
    grad_value[...] = jnp.zeros_like(grad_value)
    for i in range(TILES):
        query = query_ref[i]
        begin = begin_ref[i]
        total = total_ref[i]
        at = lax.broadcasted_iota(jnp.int32, (TILE, GROUP), 0) + i * TILE
        chosen = (stream_row_ref[...] == at).astype(F32).astype(BF16)
        grad = dot(chosen, grad_ref[...])
        grad_turned = grad.T
        product = grad_turned * turned_ref[:, pl.ds(i * TILE, TILE)].astype(F32)
        inner = jnp.concatenate(
            [
                jnp.sum(product[h * HEAD_SIZE : (h + 1) * HEAD_SIZE], axis=0, keepdims=True)
                for h in range(GROUPED)
            ],
            1,
        )
        grad = jnp.concatenate(
            [grad[:, h * HEAD_SIZE : (h + 1) * HEAD_SIZE] for h in range(GROUPED)], 0
        ).astype(BF16)

        def step(j, grad_query, query=query, begin=begin, total=total, inner=inner, grad=grad, i=i):
            rows = pl.ds(pl.multiple_of(j * TILE, TILE), TILE)
            key = key_ref[rows, :]
            scores = dot(key, query, ((1,), (1,)))
            scores = jnp.where(visible_keys(i, j, begin), scores, MASKED)
            weight = jnp.exp(scores - total)
            grad_weight = dot(value_ref[rows, :], grad, ((1,), (1,)))
            grad_scores = (weight * (grad_weight - inner)).astype(BF16)
            grad_value[rows, :] += dot(weight.astype(BF16), grad)
            grad_key[rows, :] += dot(grad_scores, query)
            return grad_query + dot(key, grad_scores, ((0,), (0,)))

        grad_query = lax.fori_loop(
            first_ref[i], i + 1, step, jnp.zeros((HEAD_SIZE, STACK), F32)
        )
        grad_query = grad_query * (HEAD_SIZE**-0.5)
        for h in range(GROUPED):
            grad_heads[pl.ds(i * TILE, TILE), h * HEAD_SIZE : (h + 1) * HEAD_SIZE] = grad_query[
                :, h * TILE : (h + 1) * TILE
            ].T.astype(F32)
    grad_heads[:, QUERY_COLS : QUERY_COLS + HEAD_SIZE] = grad_key[...]
    ready = []
    for i in range(TILES):
        rows = pl.ds(i * TILE, TILE)
        cosine = cosine_ref[rows, :]
        sine = -sine_ref[rows, :]
        one = turn(grad_heads[rows, :128], cosine, sine)
        two = turn(grad_heads[rows, 128:256], cosine, sine)
        ready.append(jnp.concatenate([one, two, grad_value[rows, :]], 1).astype(BF16))
    ready = jnp.concatenate(ready, 0)
    for b in range(BLOCKS):
        rows = pl.ds(b * ROWS, ROWS)
        at = lax.broadcasted_iota(jnp.int32, (ROWS, GROUP), 1)
        chosen = (stream_ref[rows, :] == at).astype(F32).astype(BF16)
        found = dot(chosen, ready).astype(BF16)
        out_refs[b // 2][b % 2] = found
        whole_ref[b] = found


def attend_back(*operands):
    return pl.pallas_call(
        attend_back_kernel,
        out_shape=tuple([jax.ShapeDtypeStruct((2, ROWS, HEAD_COLS), BF16)] * 4)
        + (jax.ShapeDtypeStruct((BLOCKS, ROWS, HEAD_COLS), BF16),),
        in_specs=[pl.BlockSpec(memory_space=pltpu.SMEM)]
        + [pl.BlockSpec(memory_space=pltpu.VMEM)] * 11,
        out_specs=tuple([pl.BlockSpec(memory_space=pltpu.VMEM)] * 5),
        scratch_shapes=[
            pltpu.VMEM((GROUP, HEAD_SIZE), F32),
            pltpu.VMEM((GROUP, HEAD_SIZE), F32),
            pltpu.VMEM((GROUP, 4 * HEAD_SIZE), F32),
        ],
        compiler_params=pltpu.CompilerParams(vmem_limit_bytes=56 * 2**20),
        name="attend_back",
    )(*operands)


def project_kernel(place_ref, *refs):
    pairs, (weight_ref, inputs_ref, gain_ref, hidden_ref, scale_ref, normal_ref) = (
        refs[:4],
        refs[4:],
    )
    z, core = place_ref[0], place_ref[1]
    hidden = inputs_ref[...].astype(F32)
    for kz in range(4):
        for kc in range(2):
            device = ((z + kz) % 4) * 2 + (core + kc) % 2
            rows = pl.ds(pl.multiple_of(device * QUERY_COLS, QUERY_COLS), QUERY_COLS)
            hidden = hidden + dot(pairs[kz][kc], weight_ref[rows, :])
    hidden_ref[...] = hidden
    scale = lax.rsqrt(jnp.mean(hidden * hidden, axis=-1, keepdims=True) + EPSILON)
    scale_ref[...] = scale
    normal_ref[...] = (hidden * scale * gain_ref[...]).astype(BF16)


def project(place, pairs, weight, inputs, gain):
    return pl.pallas_call(
        project_kernel,
        out_shape=(
            jax.ShapeDtypeStruct((ROWS, MODEL_WIDTH), F32),
            jax.ShapeDtypeStruct((ROWS, 1), F32),
            jax.ShapeDtypeStruct((ROWS, MODEL_WIDTH), BF16),
        ),
        in_specs=[pl.BlockSpec(memory_space=pltpu.SMEM)]
        + [pl.BlockSpec(memory_space=pltpu.VMEM)] * 7,
        out_specs=tuple([pl.BlockSpec(memory_space=pltpu.VMEM)] * 3),
        compiler_params=pltpu.CompilerParams(vmem_limit_bytes=40 * 2**20),
        name="project",
    )(place, *pairs, weight, inputs, gain)


def attention_weight_kernel(*refs):
    normals, attended, branch = refs[:BLOCKS], refs[BLOCKS : 2 * BLOCKS], refs[2 * BLOCKS : -2]
    heads_ref, out_ref = refs[-2:]
    parts, shard = out_ref.shape[:2]
    wide = 384
    for p in range(0, MODEL_WIDTH, wide):
        cols = slice(p, p + wide)
        one = two = None
        for b in range(BLOCKS):
            term = dot(normals[b][:, cols], heads_ref[b], ((0,), (0,)))
            one = term if b == 0 else one + term
            term = dot(attended[b][:, cols], branch[b // 2][b % 2], ((0,), (0,)))
            two = term if b == 0 else two + term
        for q in range(wide // shard) if shard <= wide else ():
            rows = slice(q * shard, (q + 1) * shard)
            out_ref[p // shard + q, :, :HEAD_COLS] = one[rows].astype(BF16)
            out_ref[p // shard + q, :, HEAD_COLS:] = two[rows].astype(BF16)
        if shard > wide:
            at = pl.ds(p % shard, wide)
            out_ref[p // shard, at, :HEAD_COLS] = one.astype(BF16)
            out_ref[p // shard, at, HEAD_COLS:] = two.astype(BF16)


def attention_weights(normals, attended, branch, heads, parts):
    return pl.pallas_call(
        attention_weight_kernel,
        out_shape=jax.ShapeDtypeStruct(
            (parts, MODEL_WIDTH // parts, HEAD_COLS + QUERY_COLS), BF16
        ),
        in_specs=[pl.BlockSpec(memory_space=pltpu.VMEM)] * (2 * BLOCKS + 5),
        out_specs=pl.BlockSpec(memory_space=pltpu.VMEM),
        compiler_params=pltpu.CompilerParams(vmem_limit_bytes=40 * 2**20),
        name="attention_weights",
    )(*normals, *attended, *branch, heads)


PER_STEP = 2
GATHER_STEPS = 1
EXPERT_STEPS = GATHER_STEPS + LOCAL_EXPERTS


def slots_hit(slot_ref, block):
    slot = lax.broadcasted_iota(jnp.int32, (SLOTS, ROWS), 0)
    slot = jnp.where(slot < CAP, slot, -2)
    return [slot_ref[block, e : e + 1, :] == slot for e in range(LOCAL_EXPERTS)]


def expert_kernel(device_ref, slot_ref, all_slots_ref, router_ref, *refs):
    normal_refs, refs = refs[:BLOCKS], refs[BLOCKS:]
    grad_refs, refs = refs[:BLOCKS], refs[BLOCKS:]
    (
        weight_one_ref,
        weight_two_ref,
        mixed_ref,
        grad_mixed_ref,
        grad_gate_ref,
        rows_ref,
        hidden_ref,
        grad_out_ref,
        grad_hidden_ref,
        own_gates_ref,
        held,
        grad_held,
        gates,
        grad_gates,
    ) = refs
    step = pl.program_id(0)

    @pl.when(step < GATHER_STEPS)
    def _():
        begin = device_ref[0] * LOCAL_EXPERTS
        expert_at = lax.broadcasted_iota(jnp.int32, (EXPERTS, ROWS), 0)
        for block in range(BLOCKS):
            used = all_slots_ref[block] >= 0
            logits = dot(router_ref[...], normal_refs[block][...], ((1,), (1,)))
            logits = jnp.where(used, logits, MASKED)
            gate = jnp.exp(logits - jnp.max(logits, axis=0, keepdims=True))
            gate = jnp.where(used, gate, 0.0)
            gate = gate / jnp.sum(gate, axis=0, keepdims=True)
            if block == 0:
                own_gates_ref[...] = gate
            hits = slots_hit(slot_ref, block)
            spread = []
            for e in range(LOCAL_EXPERTS):
                row = jnp.sum(
                    jnp.where(expert_at == begin + e, gate, 0.0), axis=0, keepdims=True
                )
                spread.append(jnp.sum(jnp.where(hits[e], row, 0.0), axis=1, keepdims=True))
            chosen = jnp.concatenate(hits, 0).astype(F32).astype(BF16)
            rows = dot(chosen, normal_refs[block][...]).astype(BF16)
            grads = dot(chosen, grad_refs[block][...]).astype(BF16)
            for e in range(LOCAL_EXPERTS):
                part = slice(e * SLOTS, (e + 1) * SLOTS)
                held[e, block] = rows[part]
                grad_held[e, block] = grads[part]
                gates[e, block] = spread[e]

    @pl.when((step >= GATHER_STEPS) & (step < EXPERT_STEPS))
    def _():
        e = step - GATHER_STEPS
        blocked = (BLOCKS, SLOTS, MODEL_WIDTH)
        rows = held[e].reshape(EXPERT_ROWS, MODEL_WIDTH)
        rows_ref[0] = rows
        made = dot(rows, weight_one_ref[0])
        gate_part = made[:, :FF]
        up_part = made[:, FF:]
        sigmoid_gate = jax.nn.sigmoid(gate_part)
        activation = gate_part * sigmoid_gate
        hidden = (activation * up_part).astype(BF16)
        hidden_ref[0] = hidden
        out = dot(hidden, weight_two_ref[0]).astype(BF16).astype(F32)
        gate = gates[e].reshape(EXPERT_ROWS, 1)
        grads = grad_held[e].reshape(EXPERT_ROWS, MODEL_WIDTH).astype(F32)
        grad_gates[e] = jnp.sum(out * grads, axis=1, keepdims=True).reshape(BLOCKS, SLOTS, 1)
        held[e] = (out * gate).astype(BF16).reshape(blocked)
        grad_out = (grads * gate).astype(BF16)
        grad_out_ref[0] = grad_out
        grad_hidden = dot(grad_out, weight_two_ref[0], ((1,), (1,)))
        grad_gate = (
            grad_hidden * up_part * sigmoid_gate * (1.0 + gate_part * (1.0 - sigmoid_gate))
        )
        grad_up = grad_hidden * activation
        grad_made = jnp.concatenate([grad_gate, grad_up], 1).astype(BF16)
        grad_hidden_ref[0] = grad_made
        grad_rows = dot(grad_made, weight_one_ref[0], ((1,), (1,))).astype(BF16)
        grad_held[e] = grad_rows.reshape(blocked)

    @pl.when(step >= EXPERT_STEPS)
    def _():
        for b in range(PER_STEP):
            block = (step - EXPERT_STEPS) * PER_STEP + b
            hits = slots_hit(slot_ref, block)
            for e in range(LOCAL_EXPERTS):
                grad_gate_ref[block, e : e + 1, :] = jnp.sum(
                    jnp.where(hits[e], grad_gates[e, block], 0.0), axis=0, keepdims=True
                )
            chosen = jnp.concatenate(hits, 0).astype(F32).astype(BF16)
            mixed = jnp.concatenate([held[e, block] for e in range(LOCAL_EXPERTS)], 0)
            mixed_ref[b] = dot(chosen, mixed, ((0,), (0,))).astype(BF16)
            mixed = jnp.concatenate([grad_held[e, block] for e in range(LOCAL_EXPERTS)], 0)
            grad_mixed_ref[b] = dot(chosen, mixed, ((0,), (0,))).astype(BF16)


def expert_layer(device, slots, all_slots, router, normals, grads, weight_one, weight_two):
    steps = EXPERT_STEPS + BLOCKS // PER_STEP

    def working(s):
        return (jnp.clip(s - GATHER_STEPS, 0, LOCAL_EXPERTS - 1), 0, 0)

    def ending(s):
        return (jnp.maximum(s - EXPERT_STEPS, 0), 0, 0)

    def kept(shape):
        return pl.BlockSpec(shape, lambda s: (0,) * len(shape), pipeline_mode=pl.Buffered(1))

    table = (BLOCKS, LOCAL_EXPERTS, ROWS)
    row_block = (PER_STEP, ROWS, MODEL_WIDTH)
    return pl.pallas_call(
        expert_kernel,
        grid=(steps,),
        out_shape=(
            jax.ShapeDtypeStruct((BLOCKS, ROWS, MODEL_WIDTH), BF16),
            jax.ShapeDtypeStruct((BLOCKS, ROWS, MODEL_WIDTH), BF16),
            jax.ShapeDtypeStruct(table, F32),
            jax.ShapeDtypeStruct((LOCAL_EXPERTS, EXPERT_ROWS, MODEL_WIDTH), BF16),
            jax.ShapeDtypeStruct((LOCAL_EXPERTS, EXPERT_ROWS, FF), BF16),
            jax.ShapeDtypeStruct((LOCAL_EXPERTS, EXPERT_ROWS, MODEL_WIDTH), BF16),
            jax.ShapeDtypeStruct((LOCAL_EXPERTS, EXPERT_ROWS, 2 * FF), BF16),
            jax.ShapeDtypeStruct((EXPERTS, ROWS), F32),
        ),
        in_specs=[
            pl.BlockSpec(memory_space=pltpu.SMEM),
            kept(table),
            kept((BLOCKS, EXPERTS, ROWS)),
            kept((EXPERTS, MODEL_WIDTH)),
        ]
        + [kept((ROWS, MODEL_WIDTH))] * (2 * BLOCKS)
        + [
            pl.BlockSpec((1, MODEL_WIDTH, 2 * FF), working),
            pl.BlockSpec((1, FF, MODEL_WIDTH), working),
        ],
        out_specs=(
            pl.BlockSpec(row_block, ending),
            pl.BlockSpec(row_block, ending),
            whole(table),
            pl.BlockSpec((1, EXPERT_ROWS, MODEL_WIDTH), working),
            pl.BlockSpec((1, EXPERT_ROWS, FF), working),
            pl.BlockSpec((1, EXPERT_ROWS, MODEL_WIDTH), working),
            pl.BlockSpec((1, EXPERT_ROWS, 2 * FF), working),
            whole((EXPERTS, ROWS)),
        ),
        scratch_shapes=[
            pltpu.VMEM((LOCAL_EXPERTS, BLOCKS, SLOTS, MODEL_WIDTH), BF16),
            pltpu.VMEM((LOCAL_EXPERTS, BLOCKS, SLOTS, MODEL_WIDTH), BF16),
            pltpu.VMEM((LOCAL_EXPERTS, BLOCKS, SLOTS, 1), F32),
            pltpu.VMEM((LOCAL_EXPERTS, BLOCKS, SLOTS, 1), F32),
        ],
        compiler_params=pltpu.CompilerParams(vmem_limit_bytes=60 * 2**20),
        name="expert_layer",
    )(device, slots, all_slots, router, *normals, *grads, weight_one, weight_two)


def expert_weight_kernel(rows_ref, grad_made_ref, hidden_ref, grad_out_ref, out_ref):
    parts = out_ref.shape[0]
    wide = out_ref.shape[2]
    together = 4 if parts % 4 == 0 else 1
    for p in range(0, parts, together):
        cols = slice(p * wide, (p + together) * wide)
        one = dot(rows_ref[0][:, cols], grad_made_ref[0], ((0,), (0,)))
        two = dot(grad_out_ref[0][:, cols], hidden_ref[0], ((0,), (0,)))
        for q in range(together):
            part = slice(q * wide, (q + 1) * wide)
            out_ref[p + q, 0, :, : 2 * FF] = one[part].astype(BF16)
            out_ref[p + q, 0, :, 2 * FF :] = two[part].astype(BF16)


def expert_weights(rows, grad_made, hidden, grad_out, parts):
    out = (parts, LOCAL_EXPERTS, MODEL_WIDTH // parts, 3 * FF)

    def expert(e):
        return (e, 0, 0)

    return pl.pallas_call(
        expert_weight_kernel,
        grid=(LOCAL_EXPERTS,),
        out_shape=jax.ShapeDtypeStruct(out, BF16),
        in_specs=[
            pl.BlockSpec((1, EXPERT_ROWS, MODEL_WIDTH), expert),
            pl.BlockSpec((1, EXPERT_ROWS, 2 * FF), expert),
            pl.BlockSpec((1, EXPERT_ROWS, FF), expert),
            pl.BlockSpec((1, EXPERT_ROWS, MODEL_WIDTH), expert),
        ],
        out_specs=pl.BlockSpec((out[0], 1, out[2], out[3]), lambda e: (0, e, 0, 0)),
        compiler_params=pltpu.CompilerParams(vmem_limit_bytes=60 * 2**20),
        name="expert_weights",
    )(rows, grad_made, hidden, grad_out)


def norm_back(grad_normed, values, scale, gain):
    weighted = grad_normed * gain
    grad_gain = jnp.sum(grad_normed * values * scale, axis=0)
    inner = jnp.mean(weighted * values, axis=-1, keepdims=True)
    return (scale * weighted - values * scale * scale * scale * inner, grad_gain)


def local(
    n_dp,
    tokens,
    cotangent,
    seq_lengths,
    position_map,
    routes,
    turn_order,
    norm_gain,
    ffn_gain,
    w_query,
    key_weight,
    value_weight,
    w_out,
    w_router,
    w_gate_up,
    w_down,
):
    group = Group(BLOCKS)
    index = lax.axis_index("expert")
    shard = w_query.shape[0]

    inputs_wide = tokens.astype(F32)
    scale_one = lax.rsqrt(jnp.mean(inputs_wide * inputs_wide, axis=-1, keepdims=True) + EPSILON)
    normal_one = (inputs_wide * scale_one * norm_gain).astype(BF16)
    normals, normals_here = group.gather(normal_one)

    by_heads = jnp.concatenate(
        [
            w_query.reshape(shard, BLOCKS, QUERY_COLS),
            key_weight.reshape(shard, BLOCKS, HEAD_SIZE),
            value_weight.reshape(shard, BLOCKS, HEAD_SIZE),
        ],
        2,
    )
    own_heads = lax.dynamic_index_in_dim(by_heads, index, 1, keepdims=False)
    own_heads = gather_dp(own_heads, n_dp)
    out_full = lax.all_gather(w_out, "dp", axis=0, tiled=True)
    heads_full = lax.all_gather(
        by_heads.reshape(shard, BLOCKS * HEAD_COLS), "dp", axis=0, tiled=True
    )

    lengths = seq_lengths[0]
    stream = group.to_blocks(position_map[0].reshape(BLOCKS, ROWS)).reshape(GROUP)
    ordered = jnp.arange(GROUP, dtype=jnp.int32)
    begin_ordered = stream_starts(lengths, ordered)
    cosine, sine = rotary(stream - stream_starts(lengths, stream))
    cosine_ordered, sine_ordered = rotary(ordered - begin_ordered)
    first = begin_ordered[::TILE] // TILE
    begin = jnp.tile(begin_ordered.reshape(TILES, 1, TILE), (1, 1, GROUPED))
    stream_row = stream[None, :]

    own_slots = slot_table(routes, turn_order[0]).astype(F32)
    own_slots, cotangent_late = after((own_slots, cotangent), *normals_here)
    slots, _ = group.gather(own_slots)
    slots = jnp.stack(slots, 0).astype(jnp.int32)
    grads, grads_here = group.gather(cotangent_late)

    mixed, query, key, value, log_total, turned = attend(
        first, normals, own_heads, cosine, sine, stream_row, begin
    )
    attended = group.exchange(mixed.reshape(BLOCKS, ROWS, QUERY_COLS))
    hidden_one, scale_two, normal_two = project(
        jnp.stack([group.z, group.core]), attended, out_full, tokens, ffn_gain[None]
    )
    normals_two, normals_two_here = group.gather(normal_two)

    attended = group.to_natural(jnp.stack(attended, 0).reshape(BLOCKS, ROWS, QUERY_COLS))
    attended = jnp.transpose(attended, (1, 0, 2)).reshape(ROWS, QUERY_HEADS * HEAD_SIZE)
    attended_all, attended_here = group.gather(after(attended, *normals_two_here))

    own_slots = lax.dynamic_slice_in_dim(slots, index * LOCAL_EXPERTS, LOCAL_EXPERTS, 1)
    mixture, grad_mixture, grad_gates, rows, hidden, grad_rows, grad_made, own_gates = expert_layer(
        index[None], own_slots, slots, w_router.T, normals_two, grads, w_gate_up, w_down
    )
    grad_terms = group.sum_scatter(grad_mixture)
    expert_grads = expert_weights(rows, grad_made, hidden, grad_rows, n_dp)
    expert_grads = lax.psum_scatter(expert_grads, "dp", scatter_dimension=0, tiled=True)[0]
    grad_gate_up = expert_grads[:, :, : 2 * FF].astype(F32)
    grad_down = jnp.transpose(expert_grads[:, :, 2 * FF :], (0, 2, 1)).astype(F32)

    grad_output = cotangent.astype(F32)
    grad_gates = jnp.stack(group.exchange(grad_gates), 0)
    grad_gates = group.to_natural(grad_gates.reshape(BLOCKS, LOCAL_EXPERTS, ROWS)).reshape(
        EXPERTS, ROWS
    )
    grad_logits = own_gates * (grad_gates - jnp.sum(own_gates * grad_gates, axis=0, keepdims=True))
    router_wide = w_router.astype(F32)
    grad_normal_two = sum(term.astype(F32) for term in grad_terms)
    grad_normal_two = grad_normal_two + lax.dot_general(
        grad_logits,
        router_wide,
        (((0,), (1,)), ((), ())),
        precision=EXACT,
        preferred_element_type=F32,
    )
    grad_hidden_one, local_ffn_gain = norm_back(grad_normal_two, hidden_one, scale_two, ffn_gain)
    grad_hidden_one = grad_hidden_one + grad_output
    grad_branch = grad_hidden_one.astype(BF16)
    attended_grad = dot(grad_branch, out_full, ((1,), (1,))).astype(BF16)

    def by_device(values):
        return group.to_blocks(
            jnp.transpose(values.reshape(ROWS, BLOCKS, QUERY_COLS), (1, 0, 2))
        )

    attended_grad = group.exchange(by_device(attended_grad))
    branch, mixture, local_ffn_gain, grad_logits = after(
        (grad_branch, mixture, local_ffn_gain, grad_logits), *attended_grad[1:]
    )
    branch_all = group.exchange(by_device(branch))
    mixture_terms = group.sum_scatter(mixture)
    *head_blocks, head_grads = attend_back(
        first,
        jnp.stack(attended_grad, 0).reshape(GROUP, QUERY_COLS),
        query,
        key,
        value,
        log_total,
        turned,
        cosine_ordered,
        sine_ordered,
        stream_row,
        stream[:, None],
        begin,
    )
    own_grads = group.exchange_pairs(head_blocks)
    own_grads = group.to_natural(jnp.stack(own_grads, 0).reshape(BLOCKS, ROWS, HEAD_COLS))
    own_grads = jnp.transpose(own_grads, (1, 0, 2)).reshape(ROWS, BLOCKS * HEAD_COLS)
    grad_normal_one = dot(own_grads, heads_full, ((1,), (1,)))
    grad_inputs, local_norm_gain = norm_back(grad_normal_one, inputs_wide, scale_one, norm_gain)
    d_tokens = (grad_inputs + grad_hidden_one).astype(BF16)
    output = (hidden_one + sum(term.astype(F32) for term in mixture_terms)).astype(BF16)

    local_grads = attention_weights(normals, attended_all, branch_all, head_grads, n_dp)
    parts = lax.all_to_all(local_grads, "dp", split_axis=0, concat_axis=0, tiled=True)
    parts = jnp.sum(parts.astype(F32), axis=0)
    parts, _ = group.gather(parts.astype(BF16))
    parts = jnp.transpose(group.to_natural(jnp.stack(parts, 0)), (1, 0, 2)).astype(F32)
    grad_query = parts[:, :, :QUERY_COLS].reshape(shard, -1)
    grad_key = parts[:, :, QUERY_COLS : QUERY_COLS + HEAD_SIZE].reshape(shard, -1)
    grad_value = parts[:, :, QUERY_COLS + HEAD_SIZE : HEAD_COLS].reshape(shard, -1)
    grad_out = parts[:, :, HEAD_COLS:].reshape(shard, -1)

    local_router = jnp.dot(
        grad_logits, normal_two.astype(F32), precision=EXACT, preferred_element_type=F32
    )
    local_router = jnp.concatenate([local_router, local_ffn_gain[None]], 0)
    local_router = group.to_blocks(
        jnp.transpose(local_router.reshape(EXPERTS + 1, BLOCKS, ROWS), (1, 0, 2))
    )
    own_router = jnp.sum(jnp.concatenate(group.exchange(local_router), 0), axis=0)
    own_router = sum_over(own_router, "dp", n_dp)
    parts, _ = group.gather(own_router)
    parts = jnp.transpose(group.to_natural(jnp.stack(parts, 0)), (0, 2, 1))
    parts = parts.reshape(MODEL_WIDTH, EXPERTS + 1)

    return (
        output,
        d_tokens,
        sum_over(sum_over(local_norm_gain, "expert", BLOCKS), "dp", n_dp),
        parts[:, EXPERTS],
        grad_query,
        grad_key,
        grad_value,
        grad_out,
        parts[:, :EXPERTS],
        grad_gate_up,
        grad_down,
    )


def solution(mesh):
    placed = (
        P(("dp", "expert"), None),
        P(("dp", "expert"), None),
        P("dp", None),
        P("dp", None),
        P(("dp", "expert"), None),
        P(("dp", "expert"), None),
        P(),
        P(),
        P("dp", None),
        P("dp", None),
        P("dp", None),
        P("dp", None),
        P(),
        P("expert", None, None),
        P("expert", None, None),
    )
    return jax.shard_map(
        functools.partial(local, mesh.shape["dp"]),
        mesh=mesh,
        in_specs=placed,
        out_specs=(
            P(("dp", "expert"), None),
            P(("dp", "expert"), None),
            P(),
            P(),
            P("dp", None),
            P("dp", None),
            P("dp", None),
            P("dp", None),
            P(),
            P("expert", "dp", None),
            P("expert", None, "dp"),
        ),
        check_vma=False,
    )
```

```python
import functools

import jax
import jax.numpy as jnp
from jax import lax
from jax.experimental import pallas as pl
from jax.experimental.pallas import tpu as pltpu
from jax.sharding import PartitionSpec as P

MODEL_WIDTH = 1536
QUERY_HEADS = 24
KEY_VALUE_HEADS = 8
HEAD_SIZE = 64
FF = 512
TOP = 8
EXPERTS = 40

EPSILON = 1e-06
MASKED = -1e30
EXACT = lax.Precision.HIGHEST
F32 = jnp.float32
BF16 = jnp.bfloat16

ROWS = 192
BLOCKS = 8
GROUP = ROWS * BLOCKS
TILE = 256
TILES = GROUP // TILE
GROUPED = QUERY_HEADS // KEY_VALUE_HEADS
QUERY_COLS = GROUPED * HEAD_SIZE
HEAD_COLS = QUERY_COLS + 2 * HEAD_SIZE
STACK = GROUPED * TILE
CAP = 43
SLOTS = 48
LOCAL_EXPERTS = EXPERTS // BLOCKS
EXPERT_ROWS = BLOCKS * SLOTS
EXTRA = 16
TABLE_ROWS = EXPERTS * ROWS // MODEL_WIDTH
GATE_COLS = 256


def work(microseconds):
    return pl.CostEstimate(flops=int(microseconds * 1e9), bytes_accessed=0, transcendentals=0)


def dot(left, right, dims=((1,), (0,))):
    return lax.dot_general(left, right, (dims, ((), ())), preferred_element_type=F32)


def whole(shape):
    return pl.BlockSpec(shape, lambda *_: (0,) * len(shape))


class Group:
    def __init__(self, devices):
        self.count = devices
        self.along = devices // 2
        index = lax.axis_index("expert")
        self.z = index // 2
        self.core = index % 2

    def send(self, value, shift, flip=0):
        steps = [
            (z * 2 + c, ((z + shift) % self.along) * 2 + (c ^ flip))
            for z in range(self.along)
            for c in range(2)
        ]
        return lax.ppermute(value, "expert", steps)

    def swap(self, value):
        return self.send(value, 0, 1)

    def along_z(self, value):
        return [value] + [self.send(value, -kz) for kz in range(1, self.along)]

    def both_cores(self, along):
        blocks = []
        for piece in along:
            blocks += [piece, self.swap(piece)]
        return blocks

    def gather_small(self, value):
        along = jnp.stack(self.along_z(value), 0)
        return self.to_natural(jnp.stack([along, self.swap(along)], 1).reshape((-1,) + value.shape))

    def exchange(self, blocks):
        pairs = blocks.reshape((self.along, 2) + blocks.shape[1:])
        return self.exchange_pairs(pairs[:, 0], pairs[:, 1])

    def exchange_pairs(self, mine, other):
        pairs = jnp.stack([mine, self.swap(other)], 1)
        return [pairs[0]] + [
            self.send(pairs[self.along - kz], self.along - kz) for kz in range(1, self.along)
        ]

    def sum_cores(self, mine, other):
        both = [mine[kz].astype(F32) + other[kz].astype(F32) for kz in range(self.along)]
        return [both[0]] + [one.astype(BF16) for one in both[1:]]

    def scatter_along_z(self, terms):
        return [terms[0]] + [self.send(terms[kz], kz) for kz in range(1, self.along)]

    def to_natural(self, stack):
        pairs = stack.reshape((self.along, 2) + stack.shape[1:])
        pairs = jnp.where(self.core == 1, pairs[:, ::-1], pairs)
        pairs = lax.dynamic_slice_in_dim(
            jnp.concatenate([pairs, pairs], 0), self.along - self.z, self.along, 0
        )
        return pairs.reshape(stack.shape)

    def to_blocks(self, stack):
        pairs = stack.reshape((self.along, 2) + stack.shape[1:])
        pairs = lax.dynamic_slice_in_dim(
            jnp.concatenate([pairs, pairs], 0), self.z, self.along, 0
        )
        return jnp.where(self.core == 1, pairs[:, ::-1], pairs).reshape(stack.shape)


def after(value, *events):
    return lax.optimization_barrier((value, events))[0]


def gather_dp(value, count, pass_on=lambda row: row):
    side = 4
    if count != side * side:
        return lax.all_gather(value, "dp", axis=0, tiled=True)
    index = lax.axis_index("dp")
    y, x = index // side, index % side

    def send(piece, up, right):
        steps = [
            (v * side + u, ((v + up) % side) * side + (u + right) % side)
            for v in range(side)
            for u in range(side)
        ]
        return lax.ppermute(piece, "dp", steps)

    def natural(stack, at, axis):
        return lax.dynamic_slice_in_dim(
            jnp.concatenate([stack, stack], axis), side - at, side, axis
        )

    row = jnp.stack([value] + [send(value, 0, -k) for k in range(1, side)], 0)
    row = pass_on(natural(row, x, 0))
    full = jnp.stack([row] + [send(row, -k, 0) for k in range(1, side)], 0)
    return natural(full, y, 0).reshape((-1,) + value.shape[1:])


def sum_over(value, axis, count):
    step = 1
    while step < count:
        value = value + lax.ppermute(value, axis, [(i, i ^ step) for i in range(count)])
        step *= 2
    return value


def rotary(position):
    half = HEAD_SIZE // 2
    frequency = 10000.0 ** (-(jnp.arange(half, dtype=F32) * 2.0) / (2.0 * half))
    angles = position.astype(F32)[:, None] * frequency[None, :]
    cosine = jnp.cos(angles)
    sine = jnp.sin(angles)
    return (
        jnp.concatenate([cosine] * 4, -1),
        jnp.concatenate([-sine, sine, -sine, sine], -1),
    )


def stream_starts(lengths, stream):
    starts = jnp.cumsum(lengths) - lengths
    sequence = jnp.sum((stream[:, None] >= starts[None, 1:]).astype(jnp.int32), axis=1)
    chosen = sequence[:, None] == jnp.arange(lengths.shape[0], dtype=jnp.int32)[None, :]
    return jnp.sum(jnp.where(chosen, starts[None, :], 0), axis=1)


def slot_table(route_rows, order):
    rows = route_rows.shape[0]
    pairs = rows * TOP
    turns = jnp.arange(pairs, dtype=jnp.int32)
    turn = jnp.sum(jnp.where(order[None, :] == turns[:, None], turns[None, :], 0), axis=1)
    turn = turn.reshape(rows, TOP)
    hits = jnp.arange(EXPERTS, dtype=jnp.int32)[:, None, None] == route_rows[None]
    used = jnp.any(hits, axis=2)
    turn_of = jnp.sum(jnp.where(hits, turn[None], 0), axis=2)
    earlier = used[:, None, :] & (turn_of[:, None, :] < turn_of[:, :, None])
    slot = jnp.sum(earlier.astype(jnp.int32), axis=2)
    return jnp.where(used, slot, -1)


def turn(values, cosine, signed_sine):
    lane = lax.broadcasted_iota(jnp.int32, values.shape, 1) % HEAD_SIZE
    half = HEAD_SIZE // 2
    width = values.shape[1]
    other = jnp.where(
        lane < half,
        pltpu.roll(values, width - half, 1),
        pltpu.roll(values, half, 1),
    )
    return values * cosine + other * signed_sine


def visible_keys(tile, key_tile, begin):
    key_at = lax.broadcasted_iota(jnp.int32, (TILE, STACK), 0) + key_tile * TILE
    query_at = lax.broadcasted_iota(jnp.int32, (TILE, STACK), 1) % TILE + tile * TILE
    return (key_at >= begin) & (key_at <= query_at)


def attend_kernel(
    first_ref,
    *refs,
):
    normal_refs, refs = refs[:BLOCKS], refs[BLOCKS:]
    (
    weight_ref,
    cosine_ref,
    sine_ref,
    stream_ref,
    begin_ref,
    out_ref,
    other_ref,
    query_ref,
    key_ref,
    value_ref,
    total_ref,
    turned_ref,
    heads,
    place,
    ) = refs
    for b in range(BLOCKS):
        rows = pl.ds(b * ROWS, ROWS)
        cosine = cosine_ref[rows, :]
        sine = sine_ref[rows, :]
        made = dot(normal_refs[b][...], weight_ref[...])
        one = turn(made[:, :128], cosine, sine)
        two = turn(made[:, 128:256], cosine, sine)
        heads[rows, :] = jnp.concatenate([one, two, made[:, 256:]], 1).astype(BF16)
    for i in range(TILES):
        rows = pl.ds(i * TILE, TILE)
        at = lax.broadcasted_iota(jnp.int32, (TILE, GROUP), 0) + i * TILE
        chosen = (stream_ref[...] == at).astype(F32).astype(BF16)
        place[rows, :] = chosen
        ordered = dot(chosen, heads[...])
        for h in range(GROUPED):
            part = ordered[:, h * HEAD_SIZE : (h + 1) * HEAD_SIZE] * (HEAD_SIZE**-0.5)
            query_ref[i, pl.ds(h * TILE, TILE), :] = part.astype(BF16)
        key_ref[rows, :] = ordered[:, QUERY_COLS : QUERY_COLS + HEAD_SIZE].astype(BF16)
        value_ref[rows, :] = ordered[:, QUERY_COLS + HEAD_SIZE :].astype(BF16)
    for i in range(TILES):
        query = query_ref[i]
        begin = begin_ref[i]

        def step(j, carry, query=query, begin=begin, i=i):
            top, total, mixed = carry
            rows = pl.ds(pl.multiple_of(j * TILE, TILE), TILE)
            scores = dot(key_ref[rows, :], query, ((1,), (1,)))
            scores = jnp.where(visible_keys(i, j, begin), scores, MASKED)
            new_top = jnp.maximum(top, jnp.max(scores, axis=0, keepdims=True))
            weight = jnp.exp(scores - new_top)
            fade = jnp.exp(top - new_top)
            total = total * fade + jnp.sum(weight, axis=0, keepdims=True)
            mixed = mixed * fade + dot(value_ref[rows, :], weight.astype(BF16), ((0,), (0,)))
            return new_top, total, mixed

        top, total, mixed = lax.fori_loop(
            first_ref[i],
            i + 1,
            step,
            (
                jnp.full((1, STACK), MASKED, F32),
                jnp.zeros((1, STACK), F32),
                jnp.zeros((HEAD_SIZE, STACK), F32),
            ),
        )
        total_ref[i] = top + jnp.log(total)
        mixed = mixed / total
        for h in range(GROUPED):
            turned_ref[pl.ds(h * HEAD_SIZE, HEAD_SIZE), pl.ds(i * TILE, TILE)] = mixed[
                :, h * TILE : (h + 1) * TILE
            ].astype(BF16)
    mixed = dot(turned_ref[...], place[...]).T.astype(BF16)
    for b in range(BLOCKS):
        (out_ref, other_ref)[b % 2][b // 2] = mixed[b * ROWS : (b + 1) * ROWS]


def attend(first, normals, weight, cosine, sine, stream, begin):
    return pl.pallas_call(
        attend_kernel,
        out_shape=(
            jax.ShapeDtypeStruct((BLOCKS // 2, ROWS, QUERY_COLS), BF16),
            jax.ShapeDtypeStruct((BLOCKS // 2, ROWS, QUERY_COLS), BF16),
            jax.ShapeDtypeStruct((TILES, STACK, HEAD_SIZE), BF16),
            jax.ShapeDtypeStruct((GROUP, HEAD_SIZE), BF16),
            jax.ShapeDtypeStruct((GROUP, HEAD_SIZE), BF16),
            jax.ShapeDtypeStruct((TILES, 1, STACK), F32),
            jax.ShapeDtypeStruct((QUERY_COLS, GROUP), BF16),
        ),
        in_specs=[pl.BlockSpec(memory_space=pltpu.SMEM)]
        + [pl.BlockSpec(memory_space=pltpu.VMEM)] * (BLOCKS + 5),
        out_specs=tuple([pl.BlockSpec(memory_space=pltpu.VMEM)] * 7),
        scratch_shapes=[pltpu.VMEM((GROUP, HEAD_COLS), BF16), pltpu.VMEM((GROUP, GROUP), BF16)],
        compiler_params=pltpu.CompilerParams(vmem_limit_bytes=56 * 2**20),
        cost_estimate=work(20),
        name="attend",
    )(first, *normals, weight, cosine, sine, stream, begin)


def attend_back_kernel(
    first_ref,
    grad_0_ref,
    grad_1_ref,
    grad_2_ref,
    grad_3_ref,
    query_ref,
    key_ref,
    value_ref,
    total_ref,
    turned_ref,
    cosine_ref,
    sine_ref,
    stream_row_ref,
    stream_ref,
    begin_ref,
    *refs,
):
    out_refs, (whole_ref, grad_key, grad_value, grad_heads) = refs[:2], refs[2:]
    pairs = (grad_0_ref, grad_1_ref, grad_2_ref, grad_3_ref)
    grads = jnp.concatenate([pair[kc] for pair in pairs for kc in range(2)], 0)
    grad_key[...] = jnp.zeros_like(grad_key)
    grad_value[...] = jnp.zeros_like(grad_value)
    for i in range(TILES):
        query = query_ref[i]
        begin = begin_ref[i]
        total = total_ref[i]
        at = lax.broadcasted_iota(jnp.int32, (TILE, GROUP), 0) + i * TILE
        chosen = (stream_row_ref[...] == at).astype(F32).astype(BF16)
        grad = dot(chosen, grads)
        grad_turned = grad.T
        product = grad_turned * turned_ref[:, pl.ds(i * TILE, TILE)].astype(F32)
        inner = jnp.concatenate(
            [
                jnp.sum(product[h * HEAD_SIZE : (h + 1) * HEAD_SIZE], axis=0, keepdims=True)
                for h in range(GROUPED)
            ],
            1,
        )
        grad = jnp.concatenate(
            [grad[:, h * HEAD_SIZE : (h + 1) * HEAD_SIZE] for h in range(GROUPED)], 0
        ).astype(BF16)

        def step(j, grad_query, query=query, begin=begin, total=total, inner=inner, grad=grad, i=i):
            rows = pl.ds(pl.multiple_of(j * TILE, TILE), TILE)
            key = key_ref[rows, :]
            scores = dot(key, query, ((1,), (1,)))
            scores = jnp.where(visible_keys(i, j, begin), scores, MASKED)
            weight = jnp.exp(scores - total)
            grad_weight = dot(value_ref[rows, :], grad, ((1,), (1,)))
            grad_scores = (weight * (grad_weight - inner)).astype(BF16)
            grad_value[rows, :] += dot(weight.astype(BF16), grad)
            grad_key[rows, :] += dot(grad_scores, query)
            return grad_query + dot(key, grad_scores, ((0,), (0,)))

        grad_query = lax.fori_loop(
            first_ref[i], i + 1, step, jnp.zeros((HEAD_SIZE, STACK), F32)
        )
        grad_query = grad_query * (HEAD_SIZE**-0.5)
        for h in range(GROUPED):
            grad_heads[pl.ds(i * TILE, TILE), h * HEAD_SIZE : (h + 1) * HEAD_SIZE] = grad_query[
                :, h * TILE : (h + 1) * TILE
            ].T.astype(F32)
    grad_heads[:, QUERY_COLS : QUERY_COLS + HEAD_SIZE] = grad_key[...]
    ready = []
    for i in range(TILES):
        rows = pl.ds(i * TILE, TILE)
        cosine = cosine_ref[rows, :]
        sine = -sine_ref[rows, :]
        one = turn(grad_heads[rows, :128], cosine, sine)
        two = turn(grad_heads[rows, 128:256], cosine, sine)
        ready.append(jnp.concatenate([one, two, grad_value[rows, :]], 1).astype(BF16))
    ready = jnp.concatenate(ready, 0)
    for b in range(BLOCKS):
        rows = pl.ds(b * ROWS, ROWS)
        at = lax.broadcasted_iota(jnp.int32, (ROWS, GROUP), 1)
        chosen = (stream_ref[rows, :] == at).astype(F32).astype(BF16)
        found = dot(chosen, ready).astype(BF16)
        out_refs[b % 2][b // 2] = found
        whole_ref[b] = found


def attend_back(*operands):
    return pl.pallas_call(
        attend_back_kernel,
        out_shape=tuple([jax.ShapeDtypeStruct((4, ROWS, HEAD_COLS), BF16)] * 2)
        + (jax.ShapeDtypeStruct((BLOCKS, ROWS, HEAD_COLS), BF16),),
        in_specs=[pl.BlockSpec(memory_space=pltpu.SMEM)]
        + [pl.BlockSpec(memory_space=pltpu.VMEM)] * 14,
        out_specs=tuple([pl.BlockSpec(memory_space=pltpu.VMEM)] * 3),
        scratch_shapes=[
            pltpu.VMEM((GROUP, HEAD_SIZE), F32),
            pltpu.VMEM((GROUP, HEAD_SIZE), F32),
            pltpu.VMEM((GROUP, 4 * HEAD_SIZE), F32),
        ],
        compiler_params=pltpu.CompilerParams(vmem_limit_bytes=56 * 2**20),
        cost_estimate=work(22),
        name="attend_back",
    )(*operands)


def project_kernel(place_ref, *refs):
    pairs, (weight_ref, inputs_ref, gain_ref, hidden_ref, scale_ref, normal_ref) = (
        refs[:4],
        refs[4:],
    )
    z, core = place_ref[0], place_ref[1]
    hidden = inputs_ref[...].astype(F32)
    for kz in range(4):
        for kc in range(2):
            device = ((z + kz) % 4) * 2 + (core + kc) % 2
            rows = pl.ds(pl.multiple_of(device * QUERY_COLS, QUERY_COLS), QUERY_COLS)
            hidden = hidden + dot(pairs[kz][kc], weight_ref[rows, :])
    hidden_ref[...] = hidden
    scale = lax.rsqrt(jnp.mean(hidden * hidden, axis=-1, keepdims=True) + EPSILON)
    scale_ref[...] = scale
    normal_ref[...] = (hidden * scale * gain_ref[...]).astype(BF16)


def project(place, pairs, weight, inputs, gain):
    return pl.pallas_call(
        project_kernel,
        out_shape=(
            jax.ShapeDtypeStruct((ROWS, MODEL_WIDTH), F32),
            jax.ShapeDtypeStruct((ROWS, 1), F32),
            jax.ShapeDtypeStruct((ROWS, MODEL_WIDTH), BF16),
        ),
        in_specs=[pl.BlockSpec(memory_space=pltpu.SMEM)]
        + [pl.BlockSpec(memory_space=pltpu.VMEM)] * 7,
        out_specs=tuple([pl.BlockSpec(memory_space=pltpu.VMEM)] * 3),
        compiler_params=pltpu.CompilerParams(vmem_limit_bytes=40 * 2**20),
        cost_estimate=work(3),
        name="project",
    )(place, *pairs, weight, inputs, gain)


def branch_kernel(place_ref, *refs):
    terms, refs = refs[:4], refs[4:]
    (
        hidden_ref,
        scale_ref,
        gain_ref,
        cotangent_ref,
        gates_ref,
        router_ref,
        weight_ref,
        grad_hidden_ref,
        grad_ref,
        grad_other_ref,
        branch_ref,
        branch_other_ref,
        grad_logits_ref,
        grad_gain_ref,
    ) = refs
    total = terms[0][...]
    for term in terms[1:]:
        total = total + term[...].astype(F32)
    spread = total[ROWS : ROWS + BLOCKS] + total[ROWS + BLOCKS :]
    grad_gates = jnp.concatenate(
        [spread[:, e * GATE_COLS : e * GATE_COLS + ROWS] for e in range(LOCAL_EXPERTS)], 0
    )
    gates = gates_ref[...]
    grad_logits = gates * (grad_gates - jnp.sum(gates * grad_gates, axis=0, keepdims=True))
    grad_logits_ref[...] = grad_logits
    grad_normal = total[:ROWS] + lax.dot_general(
        grad_logits,
        router_ref[...].astype(F32),
        (((0,), (0,)), ((), ())),
        precision=EXACT,
        preferred_element_type=F32,
    )
    hidden, scale = hidden_ref[...], scale_ref[...]
    weighted = grad_normal * gain_ref[...]
    grad_gain_ref[...] = jnp.sum(grad_normal * hidden * scale, axis=0, keepdims=True)
    inner = jnp.mean(weighted * hidden, axis=-1, keepdims=True)
    grad_hidden = scale * weighted - hidden * (scale * scale * scale * inner)
    grad_hidden = grad_hidden + cotangent_ref[...].astype(F32)
    grad_hidden_ref[...] = grad_hidden
    branch = grad_hidden.astype(BF16)
    parts = [branch[:, n * QUERY_COLS : (n + 1) * QUERY_COLS] for n in range(BLOCKS)]
    z, core = place_ref[0], place_ref[1]
    for kz in range(4):
        for kc in range(2):
            device = ((z + kz) % 4) * 2 + (core + kc) % 2
            rows = pl.ds(pl.multiple_of(device * QUERY_COLS, QUERY_COLS), QUERY_COLS)
            grad = dot(branch, weight_ref[rows, :], ((1,), (1,)))
            (grad_ref, grad_other_ref)[kc][kz] = grad.astype(BF16)
            part = parts[0].astype(F32)
            for n in range(1, BLOCKS):
                part = jnp.where(device == n, parts[n].astype(F32), part)
            (branch_ref, branch_other_ref)[kc][kz] = part.astype(BF16)


def branch_back(place, terms, *operands):
    block = jax.ShapeDtypeStruct((BLOCKS // 2, ROWS, QUERY_COLS), BF16)
    return pl.pallas_call(
        branch_kernel,
        out_shape=(
            jax.ShapeDtypeStruct((ROWS, MODEL_WIDTH), F32),
            block,
            block,
            block,
            block,
            jax.ShapeDtypeStruct((EXPERTS, ROWS), F32),
            jax.ShapeDtypeStruct((1, MODEL_WIDTH), F32),
        ),
        in_specs=[pl.BlockSpec(memory_space=pltpu.SMEM)]
        + [pl.BlockSpec(memory_space=pltpu.VMEM)] * 11,
        out_specs=tuple([pl.BlockSpec(memory_space=pltpu.VMEM)] * 7),
        compiler_params=pltpu.CompilerParams(vmem_limit_bytes=48 * 2**20),
        cost_estimate=work(8),
        name="branch_back",
    )(place, *terms, *operands)


def attention_weight_kernel(*refs):
    normals, attended, messages = refs[:BLOCKS], refs[BLOCKS : 2 * BLOCKS], refs[2 * BLOCKS : -2]
    heads_ref, out_ref = refs[-2:]
    branch = []
    for message in messages:
        begin = message.shape[1] - 2 * QUERY_COLS
        both = message[:, begin:]
        branch += [both[:, :QUERY_COLS], both[:, QUERY_COLS:]]
    parts, shard = out_ref.shape[:2]
    wide = 384
    for p in range(0, MODEL_WIDTH, wide):
        cols = slice(p, p + wide)
        one = two = None
        for b in range(BLOCKS):
            term = dot(normals[b][:, cols], heads_ref[b], ((0,), (0,)))
            one = term if b == 0 else one + term
            term = dot(attended[b][:, cols], branch[b], ((0,), (0,)))
            two = term if b == 0 else two + term
        for q in range(wide // shard) if shard <= wide else ():
            rows = slice(q * shard, (q + 1) * shard)
            out_ref[p // shard + q, :, :HEAD_COLS] = one[rows].astype(BF16)
            out_ref[p // shard + q, :, HEAD_COLS:] = two[rows].astype(BF16)
        if shard > wide:
            at = pl.ds(p % shard, wide)
            out_ref[p // shard, at, :HEAD_COLS] = one.astype(BF16)
            out_ref[p // shard, at, HEAD_COLS:] = two.astype(BF16)


def attention_weights(normals, attended, branch, heads, parts):
    return pl.pallas_call(
        attention_weight_kernel,
        out_shape=jax.ShapeDtypeStruct(
            (parts, MODEL_WIDTH // parts, HEAD_COLS + QUERY_COLS), BF16
        ),
        in_specs=[pl.BlockSpec(memory_space=pltpu.VMEM)] * (2 * BLOCKS + 5),
        out_specs=pl.BlockSpec(memory_space=pltpu.VMEM),
        compiler_params=pltpu.CompilerParams(vmem_limit_bytes=40 * 2**20),
        cost_estimate=work(9),
        name="attention_weights",
    )(*normals, *attended, *branch, heads)


PER_STEP = 2
GATHER_STEPS = 1
EXPERT_STEPS = GATHER_STEPS + LOCAL_EXPERTS


def slots_hit(slot_ref, block):
    slot = lax.broadcasted_iota(jnp.int32, (SLOTS, ROWS), 0)
    slot = jnp.where(slot < CAP, slot, -2)
    return [slot_ref[block, e : e + 1, :] == slot for e in range(LOCAL_EXPERTS)]


def expert_kernel(device_ref, slot_ref, all_slots_ref, router_ref, *refs):
    normal_refs, refs = refs[:BLOCKS], refs[BLOCKS:]
    grad_refs, refs = refs[:BLOCKS], refs[BLOCKS:]
    (
        weight_one_ref,
        weight_two_ref,
        mixed_ref,
        mixed_other_ref,
        grad_mixed_ref,
        grad_mixed_other_ref,
        rows_ref,
        hidden_ref,
        grad_out_ref,
        grad_hidden_ref,
        own_gates_ref,
        held,
        grad_held,
        gates,
        grad_gates,
    ) = refs
    step = pl.program_id(0)

    @pl.when(step < GATHER_STEPS)
    def _():
        device = device_ref[0]
        expert_at = lax.broadcasted_iota(jnp.int32, (EXPERTS, ROWS), 0)
        for block in range(BLOCKS):
            used = all_slots_ref[block] >= 0
            logits = dot(router_ref[...], normal_refs[block][...], ((1,), (1,)))
            logits = jnp.where(used, logits, MASKED)
            gate = jnp.exp(logits - jnp.max(logits, axis=0, keepdims=True))
            gate = jnp.where(used, gate, 0.0)
            gate = gate / jnp.sum(gate, axis=0, keepdims=True)
            if block == 0:
                own_gates_ref[...] = gate
            hits = slots_hit(slot_ref, block)
            spread = []
            for e in range(LOCAL_EXPERTS):
                row = jnp.sum(
                    jnp.where(expert_at == e * BLOCKS + device, gate, 0.0), axis=0, keepdims=True
                )
                spread.append(jnp.sum(jnp.where(hits[e], row, 0.0), axis=1, keepdims=True))
            chosen = jnp.concatenate(hits, 0).astype(F32).astype(BF16)
            rows = dot(chosen, normal_refs[block][...]).astype(BF16)
            grads = dot(chosen, grad_refs[block][:ROWS, :]).astype(BF16)
            for e in range(LOCAL_EXPERTS):
                part = slice(e * SLOTS, (e + 1) * SLOTS)
                held[e, block] = rows[part]
                grad_held[e, block] = grads[part]
                gates[e, block] = spread[e]

    @pl.when((step >= GATHER_STEPS) & (step < EXPERT_STEPS))
    def _():
        e = step - GATHER_STEPS
        blocked = (BLOCKS, SLOTS, MODEL_WIDTH)
        rows = held[e].reshape(EXPERT_ROWS, MODEL_WIDTH)
        rows_ref[0] = rows
        made = dot(rows, weight_one_ref[0])
        gate_part = made[:, :FF]
        up_part = made[:, FF:]
        sigmoid_gate = jax.nn.sigmoid(gate_part)
        activation = gate_part * sigmoid_gate
        hidden = (activation * up_part).astype(BF16)
        hidden_ref[0] = hidden
        out = dot(hidden, weight_two_ref[0]).astype(BF16).astype(F32)
        gate = gates[e].reshape(EXPERT_ROWS, 1)
        grads = grad_held[e].reshape(EXPERT_ROWS, MODEL_WIDTH).astype(F32)
        grad_gates[e] = jnp.sum(out * grads, axis=1, keepdims=True).reshape(BLOCKS, SLOTS, 1)
        held[e] = (out * gate).astype(BF16).reshape(blocked)
        grad_out = (grads * gate).astype(BF16)
        grad_out_ref[0] = grad_out
        grad_hidden = dot(grad_out, weight_two_ref[0], ((1,), (1,)))
        grad_gate = (
            grad_hidden * up_part * sigmoid_gate * (1.0 + gate_part * (1.0 - sigmoid_gate))
        )
        grad_up = grad_hidden * activation
        grad_made = jnp.concatenate([grad_gate, grad_up], 1).astype(BF16)
        grad_hidden_ref[0] = grad_made
        grad_rows = dot(grad_made, weight_one_ref[0], ((1,), (1,))).astype(BF16)
        grad_held[e] = grad_rows.reshape(blocked)

    @pl.when(step >= EXPERT_STEPS)
    def _():
        for b in range(PER_STEP):
            block = (step - EXPERT_STEPS) * PER_STEP + b
            hits = slots_hit(slot_ref, block)
            parts = []
            for e in range(LOCAL_EXPERTS):
                part = jnp.where(hits[e], grad_gates[e, block], 0.0)
                parts.append(jnp.sum(part, axis=0, keepdims=True))
                parts.append(jnp.zeros((1, GATE_COLS - ROWS), F32))
            parts.append(jnp.zeros((1, MODEL_WIDTH - LOCAL_EXPERTS * GATE_COLS), F32))
            row = jnp.concatenate(parts, 1)
            at = lax.broadcasted_iota(jnp.int32, (BLOCKS, MODEL_WIDTH), 0)
            row = jnp.where(at == device_ref[0], row, 0.0)
            high = row.astype(BF16).astype(F32)
            row = jnp.concatenate([high, row - high], 0).astype(BF16)
            chosen = jnp.concatenate(hits, 0).astype(F32).astype(BF16)
            mixed = jnp.concatenate([held[e, block] for e in range(LOCAL_EXPERTS)], 0)
            to = (mixed_ref, mixed_other_ref)[b]
            to[0] = dot(chosen, mixed, ((0,), (0,))).astype(BF16)
            mixed = jnp.concatenate([grad_held[e, block] for e in range(LOCAL_EXPERTS)], 0)
            to = (grad_mixed_ref, grad_mixed_other_ref)[b]
            to[0, :ROWS, :] = dot(chosen, mixed, ((0,), (0,))).astype(BF16)
            to[0, ROWS:, :] = row


def expert_layer(device, slots, all_slots, router, normals, grads, weight_one, weight_two):
    steps = EXPERT_STEPS + BLOCKS // PER_STEP

    def working(s):
        return (jnp.clip(s - GATHER_STEPS, 0, LOCAL_EXPERTS - 1), 0, 0)

    def ending(s):
        return (jnp.maximum(s - EXPERT_STEPS, 0), 0, 0)

    def kept(shape):
        return pl.BlockSpec(shape, lambda s: (0,) * len(shape), pipeline_mode=pl.Buffered(1))

    table = (BLOCKS, LOCAL_EXPERTS, ROWS)
    row_block = (1, ROWS, MODEL_WIDTH)
    return pl.pallas_call(
        expert_kernel,
        grid=(steps,),
        out_shape=(
            jax.ShapeDtypeStruct((BLOCKS // 2, ROWS, MODEL_WIDTH), BF16),
            jax.ShapeDtypeStruct((BLOCKS // 2, ROWS, MODEL_WIDTH), BF16),
            jax.ShapeDtypeStruct((BLOCKS // 2, ROWS + EXTRA, MODEL_WIDTH), BF16),
            jax.ShapeDtypeStruct((BLOCKS // 2, ROWS + EXTRA, MODEL_WIDTH), BF16),
            jax.ShapeDtypeStruct((LOCAL_EXPERTS, EXPERT_ROWS, MODEL_WIDTH), BF16),
            jax.ShapeDtypeStruct((LOCAL_EXPERTS, EXPERT_ROWS, FF), BF16),
            jax.ShapeDtypeStruct((LOCAL_EXPERTS, EXPERT_ROWS, MODEL_WIDTH), BF16),
            jax.ShapeDtypeStruct((LOCAL_EXPERTS, EXPERT_ROWS, 2 * FF), BF16),
            jax.ShapeDtypeStruct((EXPERTS, ROWS), F32),
        ),
        in_specs=[
            pl.BlockSpec(memory_space=pltpu.SMEM),
            kept(table),
            kept((BLOCKS, EXPERTS, ROWS)),
            kept((EXPERTS, MODEL_WIDTH)),
        ]
        + [kept((ROWS, MODEL_WIDTH))] * BLOCKS
        + [kept((ROWS + EXTRA, MODEL_WIDTH))] * BLOCKS
        + [
            pl.BlockSpec((1, MODEL_WIDTH, 2 * FF), working),
            pl.BlockSpec((1, FF, MODEL_WIDTH), working),
        ],
        out_specs=(
            pl.BlockSpec(row_block, ending),
            pl.BlockSpec(row_block, ending),
            pl.BlockSpec((1, ROWS + EXTRA, MODEL_WIDTH), ending),
            pl.BlockSpec((1, ROWS + EXTRA, MODEL_WIDTH), ending),
            pl.BlockSpec((1, EXPERT_ROWS, MODEL_WIDTH), working),
            pl.BlockSpec((1, EXPERT_ROWS, FF), working),
            pl.BlockSpec((1, EXPERT_ROWS, MODEL_WIDTH), working),
            pl.BlockSpec((1, EXPERT_ROWS, 2 * FF), working),
            whole((EXPERTS, ROWS)),
        ),
        scratch_shapes=[
            pltpu.VMEM((LOCAL_EXPERTS, BLOCKS, SLOTS, MODEL_WIDTH), BF16),
            pltpu.VMEM((LOCAL_EXPERTS, BLOCKS, SLOTS, MODEL_WIDTH), BF16),
            pltpu.VMEM((LOCAL_EXPERTS, BLOCKS, SLOTS, 1), F32),
            pltpu.VMEM((LOCAL_EXPERTS, BLOCKS, SLOTS, 1), F32),
        ],
        compiler_params=pltpu.CompilerParams(vmem_limit_bytes=60 * 2**20),
        cost_estimate=work(38),
        name="expert_layer",
    )(device, slots, all_slots, router, *normals, *grads, weight_one, weight_two)


def expert_weight_kernel(left_ref, right_ref, *refs):
    out_ref = refs[-1]
    parts, _, wide, _ = out_ref.shape
    together = 4 if parts % 4 == 0 else 1
    for p in range(0, parts, together):
        cols = slice(p * wide, (p + together) * wide)
        made = dot(left_ref[0][:, cols], right_ref[0], ((0,), (0,)))
        for q in range(together):
            out_ref[p + q, 0] = made[q * wide : (q + 1) * wide].astype(BF16)


def expert_weights(left, right, parts, column, so_far=None):
    shape = (parts, LOCAL_EXPERTS, MODEL_WIDTH // parts, 3 * FF)
    columns = right.shape[2]
    given = [left, right] + ([] if so_far is None else [so_far])
    return pl.pallas_call(
        expert_weight_kernel,
        grid=(LOCAL_EXPERTS,),
        out_shape=jax.ShapeDtypeStruct(shape, BF16),
        in_specs=[
            pl.BlockSpec((1, EXPERT_ROWS, MODEL_WIDTH), lambda e: (e, 0, 0)),
            pl.BlockSpec((1, EXPERT_ROWS, columns), lambda e: (e, 0, 0)),
        ]
        + [pl.BlockSpec(memory_space=pl.ANY)] * (len(given) - 2),
        out_specs=pl.BlockSpec(
            (parts, 1, shape[2], columns), lambda e: (0, e, 0, column // columns)
        ),
        input_output_aliases={} if so_far is None else {2: 0},
        compiler_params=pltpu.CompilerParams(vmem_limit_bytes=60 * 2**20),
        cost_estimate=work(7 * columns / FF),
        name="expert_weights",
    )(*given)


def norm_back(grad_normed, values, scale, gain):
    weighted = grad_normed * gain
    grad_gain = jnp.sum(grad_normed * values * scale, axis=0)
    inner = jnp.mean(weighted * values, axis=-1, keepdims=True)
    return (scale * weighted - values * scale * scale * scale * inner, grad_gain)


def local(
    n_dp,
    tokens,
    cotangent,
    seq_lengths,
    position_map,
    routes,
    turn_order,
    norm_gain,
    ffn_gain,
    w_query,
    key_weight,
    value_weight,
    w_out,
    w_router,
    w_gate_up,
    w_down,
):
    group = Group(BLOCKS)
    index = lax.axis_index("expert")
    shard = w_query.shape[0]

    inputs_wide = tokens.astype(F32)
    scale_one = lax.rsqrt(jnp.mean(inputs_wide * inputs_wide, axis=-1, keepdims=True) + EPSILON)
    normal_one = (inputs_wide * scale_one * norm_gain).astype(BF16)
    by_heads = jnp.concatenate(
        [
            w_query.reshape(shard, BLOCKS, QUERY_COLS),
            key_weight.reshape(shard, BLOCKS, HEAD_SIZE),
            value_weight.reshape(shard, BLOCKS, HEAD_SIZE),
        ],
        2,
    )
    own_heads = lax.dynamic_index_in_dim(by_heads, index, 1, keepdims=False)
    along = group.along_z(normal_one)
    tables = (position_map, seq_lengths, routes, turn_order)
    held = list(tables)

    def pass_on(row):
        row, held[:] = lax.optimization_barrier((row, tables))
        return row

    own_heads = gather_dp(own_heads, n_dp, pass_on)
    position_map, seq_lengths, routes, turn_order = held
    own_heads, along = lax.optimization_barrier((own_heads, along))
    normals = group.both_cores(along)
    out_full = lax.all_gather(w_out, "dp", axis=0, tiled=True)
    heads_full = lax.all_gather(
        by_heads.reshape(shard, BLOCKS * HEAD_COLS), "dp", axis=0, tiled=True
    )

    lengths = seq_lengths[0]
    stream = group.to_blocks(position_map[0].reshape(BLOCKS, ROWS)).reshape(GROUP)
    ordered = jnp.arange(GROUP, dtype=jnp.int32)
    begin_ordered = stream_starts(lengths, ordered)
    cosine, sine = rotary(stream - stream_starts(lengths, stream))
    cosine_ordered, sine_ordered = rotary(ordered - begin_ordered)
    first = begin_ordered[::TILE] // TILE
    begin = jnp.tile(begin_ordered.reshape(TILES, 1, TILE), (1, 1, GROUPED))
    stream_row = stream[None, :]

    own_slots = slot_table(routes, turn_order[0]).reshape(BLOCKS, LOCAL_EXPERTS, ROWS)
    own_slots = jnp.transpose(own_slots, (1, 0, 2)).astype(BF16).reshape(TABLE_ROWS, MODEL_WIDTH)
    grads = jnp.concatenate(
        [cotangent, own_slots, jnp.zeros((EXTRA - TABLE_ROWS, MODEL_WIDTH), BF16)], 0
    )
    grads = group.along_z(after(grads, *normals))
    made = attend(first, normals, own_heads, cosine, sine, stream_row, begin)
    made, grads = lax.optimization_barrier((made, grads))
    mixed, other, query, key, value, log_total, turned = made

    attended = group.exchange_pairs(mixed, other)
    grads = group.both_cores(grads)
    attended, grads = lax.optimization_barrier((attended, grads))
    place = jnp.stack([group.z, group.core])
    hidden_one, scale_two, normal_two = project(place, attended, out_full, tokens, ffn_gain[None])
    along = group.along_z(normal_two)
    slots = jnp.stack([block[ROWS : ROWS + TABLE_ROWS] for block in grads], 0)
    slots = slots.reshape(BLOCKS, EXPERTS, ROWS).astype(jnp.int32)
    own_slots = lax.dynamic_index_in_dim(
        slots.reshape(BLOCKS, LOCAL_EXPERTS, BLOCKS, ROWS), index, 2, keepdims=False
    )
    normals_two = group.both_cores(along)

    attended = group.to_natural(jnp.stack(attended, 0).reshape(BLOCKS, ROWS, QUERY_COLS))
    attended = jnp.transpose(attended, (1, 0, 2)).reshape(ROWS, QUERY_HEADS * HEAD_SIZE)
    attended_all = group.along_z(after(attended, *normals_two))

    router = w_router.T.reshape(BLOCKS, LOCAL_EXPERTS, MODEL_WIDTH)
    router = jnp.transpose(router, (1, 0, 2)).reshape(EXPERTS, MODEL_WIDTH)
    made = expert_layer(
        index[None], own_slots, slots, router, normals_two, grads, w_gate_up, w_down
    )
    made, attended_all = lax.optimization_barrier((made, attended_all))
    mixture, mixture_other, grad_mixture, grad_mixture_other = made[:4]
    rows, hidden, grad_rows, grad_made, own_gates = made[4:]
    other = group.swap(grad_mixture_other)
    expert_grads = expert_weights(grad_rows, hidden, n_dp, 2 * FF)
    other, expert_grads = lax.optimization_barrier((other, expert_grads))
    grad_terms = group.sum_cores(grad_mixture, other)
    grad_terms, expert_grads = lax.optimization_barrier((grad_terms, expert_grads))
    grad_terms = group.scatter_along_z(grad_terms)
    expert_grads = expert_weights(rows, grad_made, n_dp, 0, expert_grads)
    expert_grads, grad_terms = lax.optimization_barrier((expert_grads, grad_terms))
    expert_grads = lax.psum_scatter(expert_grads, "dp", scatter_dimension=0, tiled=True)[0]
    grad_gate_up = expert_grads[:, :, : 2 * FF].astype(F32)
    grad_down = jnp.transpose(expert_grads[:, :, 2 * FF :], (0, 2, 1)).astype(F32)

    grad_hidden_one, mine, other, branch, branch_other, grad_logits, local_ffn_gain = branch_back(
        place,
        grad_terms,
        hidden_one,
        scale_two,
        ffn_gain[None],
        cotangent,
        own_gates,
        router,
        out_full,
    )
    mixture_other = after(mixture_other, mine)
    attended_grad = group.exchange_pairs(mine, other)
    branch_other = group.swap(branch_other)
    mixture_other = group.swap(mixture_other)
    terms = group.sum_cores(mixture, mixture_other)
    branch_own = jnp.concatenate([branch[0], branch_other[0]], 1)
    messages = [
        jnp.concatenate([terms[kz], branch[kz], branch_other[kz]], 1) for kz in range(1, 4)
    ]
    attended_grad, messages, mixture, attended_all = lax.optimization_barrier(
        (attended_grad, messages, terms[0], attended_all)
    )
    messages = [group.send(messages[3 - kz], 4 - kz) for kz in range(1, 4)]
    head_grads = attend_back(
        first,
        *attended_grad,
        query,
        key,
        value,
        log_total,
        turned,
        cosine_ordered,
        sine_ordered,
        stream_row,
        stream[:, None],
        begin,
    )
    head_grads, messages, attended_all, grad_logits, local_ffn_gain = lax.optimization_barrier(
        (head_grads, messages, attended_all, grad_logits, local_ffn_gain)
    )
    mine, other, head_grads = head_grads
    own_grads = group.exchange_pairs(mine, other)
    attended_all = group.both_cores(attended_all)
    own_grads = group.to_natural(jnp.stack(own_grads, 0).reshape(BLOCKS, ROWS, HEAD_COLS))
    own_grads = jnp.transpose(own_grads, (1, 0, 2)).reshape(ROWS, BLOCKS * HEAD_COLS)
    grad_normal_one = dot(own_grads, heads_full, ((1,), (1,)))
    grad_inputs, local_norm_gain = norm_back(grad_normal_one, inputs_wide, scale_one, norm_gain)
    d_tokens = (grad_inputs + grad_hidden_one).astype(BF16)
    mixture = mixture + sum(message[:, :MODEL_WIDTH].astype(F32) for message in messages)
    output = (hidden_one + mixture).astype(BF16)

    local_grads = attention_weights(
        normals, attended_all, [branch_own] + messages, head_grads, n_dp
    )
    local_grads, grad_logits, local_ffn_gain = lax.optimization_barrier(
        (local_grads, grad_logits, local_ffn_gain)
    )
    parts = lax.all_to_all(local_grads, "dp", split_axis=0, concat_axis=0, tiled=True)
    parts = jnp.sum(parts.astype(F32), axis=0)
    parts = jnp.transpose(group.gather_small(parts.astype(BF16)), (1, 0, 2)).astype(F32)
    grad_query = parts[:, :, :QUERY_COLS].reshape(shard, -1)
    grad_key = parts[:, :, QUERY_COLS : QUERY_COLS + HEAD_SIZE].reshape(shard, -1)
    grad_value = parts[:, :, QUERY_COLS + HEAD_SIZE : HEAD_COLS].reshape(shard, -1)
    grad_out = parts[:, :, HEAD_COLS:].reshape(shard, -1)

    local_router = jnp.dot(
        grad_logits, normal_two.astype(F32), precision=EXACT, preferred_element_type=F32
    )
    local_router = jnp.concatenate([local_router, local_ffn_gain], 0)
    local_router = group.to_blocks(
        jnp.transpose(local_router.reshape(EXPERTS + 1, BLOCKS, ROWS), (1, 0, 2))
    )
    own_router = sum(pair[0] + pair[1] for pair in group.exchange(local_router))
    own_router = sum_over(own_router, "dp", n_dp)
    parts = jnp.transpose(group.gather_small(own_router), (0, 2, 1))
    parts = parts.reshape(MODEL_WIDTH, EXPERTS + 1)
    grad_router = parts[:, :EXPERTS].reshape(MODEL_WIDTH, LOCAL_EXPERTS, BLOCKS)
    grad_router = jnp.transpose(grad_router, (0, 2, 1)).reshape(MODEL_WIDTH, EXPERTS)

    return (
        output,
        d_tokens,
        sum_over(sum_over(local_norm_gain, "expert", BLOCKS), "dp", n_dp),
        parts[:, EXPERTS],
        grad_query,
        grad_key,
        grad_value,
        grad_out,
        grad_router,
        grad_gate_up,
        grad_down,
    )


def solution(mesh):
    placed = (
        P(("dp", "expert"), None),
        P(("dp", "expert"), None),
        P("dp", None),
        P("dp", None),
        P(("dp", "expert"), None),
        P(("dp", "expert"), None),
        P(),
        P(),
        P("dp", None),
        P("dp", None),
        P("dp", None),
        P("dp", None),
        P(),
        P("expert", None, None),
        P("expert", None, None),
    )
    return jax.shard_map(
        functools.partial(local, mesh.shape["dp"]),
        mesh=mesh,
        in_specs=placed,
        out_specs=(
            P(("dp", "expert"), None),
            P(("dp", "expert"), None),
            P(),
            P(),
            P("dp", None),
            P("dp", None),
            P("dp", None),
            P("dp", None),
            P(),
            P("expert", "dp", None),
            P("expert", None, "dp"),
        ),
        check_vma=False,
    )
```

```python
import functools

import jax
import jax.numpy as jnp
from jax import lax
from jax.experimental import pallas as pl
from jax.experimental.pallas import tpu as pltpu
from jax.sharding import PartitionSpec as P

MODEL_WIDTH = 1536
QUERY_HEADS = 24
KEY_VALUE_HEADS = 8
HEAD_SIZE = 64
FF = 512
TOP = 8
EXPERTS = 40

EPSILON = 1e-06
MASKED = -1e30
EXACT = lax.Precision.HIGHEST
F32 = jnp.float32
BF16 = jnp.bfloat16

ROWS = 192
BLOCKS = 8
GROUP = ROWS * BLOCKS
TILE = 256
TILES = GROUP // TILE
GROUPED = QUERY_HEADS // KEY_VALUE_HEADS
QUERY_COLS = GROUPED * HEAD_SIZE
HEAD_COLS = QUERY_COLS + 2 * HEAD_SIZE
STACK = GROUPED * TILE
CAP = 43
SLOTS = 48
LOCAL_EXPERTS = EXPERTS // BLOCKS
EXPERT_ROWS = BLOCKS * SLOTS
SMALL = 48
HALF = (HEAD_COLS + QUERY_COLS) // 2
EXTRA = 16
TABLE_ROWS = EXPERTS * ROWS // MODEL_WIDTH
GATE_COLS = 256


def work(microseconds):
    return pl.CostEstimate(flops=int(microseconds * 1e9), bytes_accessed=0, transcendentals=0)


def dot(left, right, dims=((1,), (0,))):
    return lax.dot_general(left, right, (dims, ((), ())), preferred_element_type=F32)


def whole(shape):
    return pl.BlockSpec(shape, lambda *_: (0,) * len(shape))


class Group:
    def __init__(self, devices):
        self.count = devices
        self.along = devices // 2
        index = lax.axis_index("expert")
        self.z = index // 2
        self.core = index % 2

    def send(self, value, shift, flip=0):
        steps = [
            (z * 2 + c, ((z + shift) % self.along) * 2 + (c ^ flip))
            for z in range(self.along)
            for c in range(2)
        ]
        return lax.ppermute(value, "expert", steps)

    def swap(self, value):
        return self.send(value, 0, 1)

    def along_z(self, value):
        return [value] + [self.send(value, -kz) for kz in range(1, self.along)]

    def both_cores(self, along):
        blocks = []
        for piece in along:
            blocks += [piece, self.swap(piece)]
        return blocks

    def gather_small(self, value):
        along = jnp.stack(self.along_z(value), 0)
        return self.to_natural(jnp.stack([along, self.swap(along)], 1).reshape((-1,) + value.shape))

    def exchange(self, blocks):
        pairs = blocks.reshape((self.along, 2) + blocks.shape[1:])
        return self.exchange_pairs(pairs[:, 0], pairs[:, 1])

    def exchange_pairs(self, mine, other):
        pairs = jnp.stack([mine, self.swap(other)], 1)
        return [pairs[0]] + [
            self.send(pairs[self.along - kz], self.along - kz) for kz in range(1, self.along)
        ]

    def sum_cores(self, mine, other):
        both = [mine[kz].astype(F32) + other[kz].astype(F32) for kz in range(self.along)]
        return [both[0]] + [one.astype(BF16) for one in both[1:]]

    def scatter_along_z(self, terms):
        return [terms[0]] + [self.send(terms[kz], kz) for kz in range(1, self.along)]

    def to_natural(self, stack):
        pairs = stack.reshape((self.along, 2) + stack.shape[1:])
        pairs = jnp.where(self.core == 1, pairs[:, ::-1], pairs)
        pairs = lax.dynamic_slice_in_dim(
            jnp.concatenate([pairs, pairs], 0), self.along - self.z, self.along, 0
        )
        return pairs.reshape(stack.shape)

    def to_blocks(self, stack):
        pairs = stack.reshape((self.along, 2) + stack.shape[1:])
        pairs = lax.dynamic_slice_in_dim(
            jnp.concatenate([pairs, pairs], 0), self.z, self.along, 0
        )
        return jnp.where(self.core == 1, pairs[:, ::-1], pairs).reshape(stack.shape)


def after(value, *events):
    return lax.optimization_barrier((value, events))[0]


SIDE = 4


def send_dp(value, up, right):
    steps = [
        (y * SIDE + x, ((y + up) % SIDE) * SIDE + (x + right) % SIDE)
        for y in range(SIDE)
        for x in range(SIDE)
    ]
    return lax.ppermute(value, "dp", steps)


def stack_kernel(*refs):
    for i, ref in enumerate(refs[:-1]):
        refs[-1][i] = ref[...]


def stack(pieces):
    return pl.pallas_call(
        stack_kernel,
        out_shape=jax.ShapeDtypeStruct((len(pieces),) + pieces[0].shape, pieces[0].dtype),
        in_specs=[pl.BlockSpec(memory_space=pltpu.VMEM)] * len(pieces),
        out_specs=pl.BlockSpec(memory_space=pltpu.VMEM),
        cost_estimate=work(1),
        name="stack",
    )(*pieces)


def in_halves(value):
    high = value.astype(BF16)
    return jnp.concatenate([high, (value - high.astype(F32)).astype(BF16)], 0)


def from_halves(value):
    rows = value.shape[-2] // 2
    return value[..., :rows, :].astype(F32) + value[..., rows:, :].astype(F32)


def rotary(position):
    half = HEAD_SIZE // 2
    frequency = 10000.0 ** (-(jnp.arange(half, dtype=F32) * 2.0) / (2.0 * half))
    angles = position.astype(F32)[:, None] * frequency[None, :]
    cosine = jnp.cos(angles)
    sine = jnp.sin(angles)
    return (
        jnp.concatenate([cosine] * 4, -1),
        jnp.concatenate([-sine, sine, -sine, sine], -1),
    )


def stream_starts(lengths, stream):
    starts = jnp.cumsum(lengths) - lengths
    sequence = jnp.sum((stream[:, None] >= starts[None, 1:]).astype(jnp.int32), axis=1)
    chosen = sequence[:, None] == jnp.arange(lengths.shape[0], dtype=jnp.int32)[None, :]
    return jnp.sum(jnp.where(chosen, starts[None, :], 0), axis=1)


def slot_table(route_rows, order):
    rows = route_rows.shape[0]
    pairs = rows * TOP
    turns = jnp.arange(pairs, dtype=jnp.int32)
    turn = jnp.sum(jnp.where(order[None, :] == turns[:, None], turns[None, :], 0), axis=1)
    turn = turn.reshape(rows, TOP)
    hits = jnp.arange(EXPERTS, dtype=jnp.int32)[:, None, None] == route_rows[None]
    used = jnp.any(hits, axis=2)
    turn_of = jnp.sum(jnp.where(hits, turn[None], 0), axis=2)
    earlier = used[:, None, :] & (turn_of[:, None, :] < turn_of[:, :, None])
    slot = jnp.sum(earlier.astype(jnp.int32), axis=2)
    return jnp.where(used, slot, -1)


def turn(values, cosine, signed_sine):
    lane = lax.broadcasted_iota(jnp.int32, values.shape, 1) % HEAD_SIZE
    half = HEAD_SIZE // 2
    width = values.shape[1]
    other = jnp.where(
        lane < half,
        pltpu.roll(values, width - half, 1),
        pltpu.roll(values, half, 1),
    )
    return values * cosine + other * signed_sine


def visible_keys(tile, key_tile, begin):
    key_at = lax.broadcasted_iota(jnp.int32, (TILE, STACK), 0) + key_tile * TILE
    query_at = lax.broadcasted_iota(jnp.int32, (TILE, STACK), 1) % TILE + tile * TILE
    return (key_at >= begin) & (key_at <= query_at)


def attend_kernel(
    first_ref,
    *refs,
):
    normal_refs, refs = refs[:BLOCKS], refs[BLOCKS:]
    weight_refs, refs = refs[:SIDE], refs[SIDE:]
    (
    cosine_ref,
    sine_ref,
    stream_ref,
    begin_ref,
    slots_ref,
    out_ref,
    other_ref,
    query_ref,
    key_ref,
    value_ref,
    total_ref,
    turned_ref,
    heads,
    place,
    weights,
    ) = refs
    y, x = first_ref[TILES], first_ref[TILES + 1]
    for ky in range(SIDE):
        for kx in range(SIDE):
            weights[((y + ky) % SIDE) * SIDE + (x + kx) % SIDE] = weight_refs[ky][kx]
    weight = weights[...].reshape(MODEL_WIDTH, HEAD_COLS)
    for b in range(BLOCKS):
        rows = pl.ds(b * ROWS, ROWS)
        cosine = cosine_ref[rows, :]
        sine = sine_ref[rows, :]
        made = dot(normal_refs[b][...], weight)
        one = turn(made[:, :128], cosine, sine)
        two = turn(made[:, 128:256], cosine, sine)
        heads[rows, :] = jnp.concatenate([one, two, made[:, 256:]], 1).astype(BF16)
    for i in range(TILES):
        rows = pl.ds(i * TILE, TILE)
        at = lax.broadcasted_iota(jnp.int32, (TILE, GROUP), 0) + i * TILE
        chosen = (stream_ref[...] == at).astype(F32).astype(BF16)
        place[rows, :] = chosen
        ordered = dot(chosen, heads[...])
        for h in range(GROUPED):
            part = ordered[:, h * HEAD_SIZE : (h + 1) * HEAD_SIZE] * (HEAD_SIZE**-0.5)
            query_ref[i, pl.ds(h * TILE, TILE), :] = part.astype(BF16)
        key_ref[rows, :] = ordered[:, QUERY_COLS : QUERY_COLS + HEAD_SIZE].astype(BF16)
        value_ref[rows, :] = ordered[:, QUERY_COLS + HEAD_SIZE :].astype(BF16)
    for i in range(TILES):
        query = query_ref[i]
        begin = begin_ref[i]

        def step(j, carry, query=query, begin=begin, i=i):
            top, total, mixed = carry
            rows = pl.ds(pl.multiple_of(j * TILE, TILE), TILE)
            scores = dot(key_ref[rows, :], query, ((1,), (1,)))
            scores = jnp.where(visible_keys(i, j, begin), scores, MASKED)
            new_top = jnp.maximum(top, jnp.max(scores, axis=0, keepdims=True))
            weight = jnp.exp(scores - new_top)
            fade = jnp.exp(top - new_top)
            total = total * fade + jnp.sum(weight, axis=0, keepdims=True)
            mixed = mixed * fade + dot(value_ref[rows, :], weight.astype(BF16), ((0,), (0,)))
            return new_top, total, mixed

        top, total, mixed = lax.fori_loop(
            first_ref[i],
            i + 1,
            step,
            (
                jnp.full((1, STACK), MASKED, F32),
                jnp.zeros((1, STACK), F32),
                jnp.zeros((HEAD_SIZE, STACK), F32),
            ),
        )
        total_ref[i] = top + jnp.log(total)
        mixed = mixed / total
        for h in range(GROUPED):
            turned_ref[pl.ds(h * HEAD_SIZE, HEAD_SIZE), pl.ds(i * TILE, TILE)] = mixed[
                :, h * TILE : (h + 1) * TILE
            ].astype(BF16)
    mixed = dot(turned_ref[...], place[...]).T.astype(BF16)
    for b in range(BLOCKS):
        to = (out_ref, other_ref)[b % 2]
        to[b // 2, :ROWS, :] = mixed[b * ROWS : (b + 1) * ROWS]
        to[b // 2, ROWS:, :] = slots_ref[...]


def attend(first, normals, weights, cosine, sine, stream, begin, slots):
    return pl.pallas_call(
        attend_kernel,
        out_shape=(
            jax.ShapeDtypeStruct((BLOCKS // 2, ROWS + SMALL, QUERY_COLS), BF16),
            jax.ShapeDtypeStruct((BLOCKS // 2, ROWS + SMALL, QUERY_COLS), BF16),
            jax.ShapeDtypeStruct((TILES, STACK, HEAD_SIZE), BF16),
            jax.ShapeDtypeStruct((GROUP, HEAD_SIZE), BF16),
            jax.ShapeDtypeStruct((GROUP, HEAD_SIZE), BF16),
            jax.ShapeDtypeStruct((TILES, 1, STACK), F32),
            jax.ShapeDtypeStruct((QUERY_COLS, GROUP), BF16),
        ),
        in_specs=[pl.BlockSpec(memory_space=pltpu.SMEM)]
        + [pl.BlockSpec(memory_space=pltpu.VMEM)] * (BLOCKS + SIDE + 5),
        out_specs=tuple([pl.BlockSpec(memory_space=pltpu.VMEM)] * 7),
        scratch_shapes=[
            pltpu.VMEM((GROUP, HEAD_COLS), BF16),
            pltpu.VMEM((GROUP, GROUP), BF16),
            pltpu.VMEM((SIDE * SIDE, MODEL_WIDTH // SIDE**2, HEAD_COLS), BF16),
        ],
        compiler_params=pltpu.CompilerParams(vmem_limit_bytes=60 * 2**20),
        cost_estimate=work(20),
        name="attend",
    )(first, *normals, *weights, cosine, sine, stream, begin, slots)


def attend_back_kernel(
    first_ref,
    grad_0_ref,
    grad_1_ref,
    grad_2_ref,
    grad_3_ref,
    query_ref,
    key_ref,
    value_ref,
    total_ref,
    turned_ref,
    cosine_ref,
    sine_ref,
    stream_row_ref,
    stream_ref,
    begin_ref,
    *refs,
):
    out_refs, (whole_ref, grad_key, grad_value, grad_heads) = refs[:2], refs[2:]
    pairs = (grad_0_ref, grad_1_ref, grad_2_ref, grad_3_ref)
    grads = jnp.concatenate([pair[kc] for pair in pairs for kc in range(2)], 0)
    grad_key[...] = jnp.zeros_like(grad_key)
    grad_value[...] = jnp.zeros_like(grad_value)
    for i in range(TILES):
        query = query_ref[i]
        begin = begin_ref[i]
        total = total_ref[i]
        at = lax.broadcasted_iota(jnp.int32, (TILE, GROUP), 0) + i * TILE
        chosen = (stream_row_ref[...] == at).astype(F32).astype(BF16)
        grad = dot(chosen, grads)
        grad_turned = grad.T
        product = grad_turned * turned_ref[:, pl.ds(i * TILE, TILE)].astype(F32)
        inner = jnp.concatenate(
            [
                jnp.sum(product[h * HEAD_SIZE : (h + 1) * HEAD_SIZE], axis=0, keepdims=True)
                for h in range(GROUPED)
            ],
            1,
        )
        grad = jnp.concatenate(
            [grad[:, h * HEAD_SIZE : (h + 1) * HEAD_SIZE] for h in range(GROUPED)], 0
        ).astype(BF16)

        def step(j, grad_query, query=query, begin=begin, total=total, inner=inner, grad=grad, i=i):
            rows = pl.ds(pl.multiple_of(j * TILE, TILE), TILE)
            key = key_ref[rows, :]
            scores = dot(key, query, ((1,), (1,)))
            scores = jnp.where(visible_keys(i, j, begin), scores, MASKED)
            weight = jnp.exp(scores - total)
            grad_weight = dot(value_ref[rows, :], grad, ((1,), (1,)))
            grad_scores = (weight * (grad_weight - inner)).astype(BF16)
            grad_value[rows, :] += dot(weight.astype(BF16), grad)
            grad_key[rows, :] += dot(grad_scores, query)
            return grad_query + dot(key, grad_scores, ((0,), (0,)))

        grad_query = lax.fori_loop(
            first_ref[i], i + 1, step, jnp.zeros((HEAD_SIZE, STACK), F32)
        )
        grad_query = grad_query * (HEAD_SIZE**-0.5)
        for h in range(GROUPED):
            grad_heads[pl.ds(i * TILE, TILE), h * HEAD_SIZE : (h + 1) * HEAD_SIZE] = grad_query[
                :, h * TILE : (h + 1) * TILE
            ].T.astype(F32)
    grad_heads[:, QUERY_COLS : QUERY_COLS + HEAD_SIZE] = grad_key[...]
    ready = []
    for i in range(TILES):
        rows = pl.ds(i * TILE, TILE)
        cosine = cosine_ref[rows, :]
        sine = -sine_ref[rows, :]
        one = turn(grad_heads[rows, :128], cosine, sine)
        two = turn(grad_heads[rows, 128:256], cosine, sine)
        ready.append(jnp.concatenate([one, two, grad_value[rows, :]], 1).astype(BF16))
    ready = jnp.concatenate(ready, 0)
    for b in range(BLOCKS):
        rows = pl.ds(b * ROWS, ROWS)
        at = lax.broadcasted_iota(jnp.int32, (ROWS, GROUP), 1)
        chosen = (stream_ref[rows, :] == at).astype(F32).astype(BF16)
        found = dot(chosen, ready).astype(BF16)
        out_refs[b % 2][b // 2] = found
        whole_ref[b] = found


def attend_back(*operands):
    return pl.pallas_call(
        attend_back_kernel,
        out_shape=tuple([jax.ShapeDtypeStruct((4, ROWS, HEAD_COLS), BF16)] * 2)
        + (jax.ShapeDtypeStruct((BLOCKS, ROWS, HEAD_COLS), BF16),),
        in_specs=[pl.BlockSpec(memory_space=pltpu.SMEM)]
        + [pl.BlockSpec(memory_space=pltpu.VMEM)] * 14,
        out_specs=tuple([pl.BlockSpec(memory_space=pltpu.VMEM)] * 3),
        scratch_shapes=[
            pltpu.VMEM((GROUP, HEAD_SIZE), F32),
            pltpu.VMEM((GROUP, HEAD_SIZE), F32),
            pltpu.VMEM((GROUP, 4 * HEAD_SIZE), F32),
        ],
        compiler_params=pltpu.CompilerParams(vmem_limit_bytes=60 * 2**20),
        cost_estimate=work(22),
        name="attend_back",
    )(*operands)


def project_kernel(place_ref, *refs):
    pairs, (weight_ref, inputs_ref, gain_ref, hidden_ref, scale_ref, normal_ref) = (
        refs[:4],
        refs[4:],
    )
    z, core = place_ref[0], place_ref[1]
    hidden = inputs_ref[...].astype(F32)
    for kz in range(4):
        for kc in range(2):
            device = ((z + kz) % 4) * 2 + (core + kc) % 2
            rows = pl.ds(pl.multiple_of(device * QUERY_COLS, QUERY_COLS), QUERY_COLS)
            hidden = hidden + dot(pairs[kz][kc, :ROWS, :], weight_ref[rows, :])
    hidden_ref[...] = hidden
    scale = lax.rsqrt(jnp.mean(hidden * hidden, axis=-1, keepdims=True) + EPSILON)
    scale_ref[...] = scale
    normal_ref[...] = (hidden * scale * gain_ref[...]).astype(BF16)


def project(place, pairs, weight, inputs, gain):
    return pl.pallas_call(
        project_kernel,
        out_shape=(
            jax.ShapeDtypeStruct((ROWS, MODEL_WIDTH), F32),
            jax.ShapeDtypeStruct((ROWS, 1), F32),
            jax.ShapeDtypeStruct((ROWS, MODEL_WIDTH), BF16),
        ),
        in_specs=[pl.BlockSpec(memory_space=pltpu.SMEM)]
        + [pl.BlockSpec(memory_space=pltpu.VMEM)] * 7,
        out_specs=tuple([pl.BlockSpec(memory_space=pltpu.VMEM)] * 3),
        compiler_params=pltpu.CompilerParams(vmem_limit_bytes=60 * 2**20),
        cost_estimate=work(3),
        name="project",
    )(place, *pairs, weight, inputs, gain)


def branch_kernel(place_ref, *refs):
    terms, refs = refs[:4], refs[4:]
    (
        hidden_ref,
        scale_ref,
        gain_ref,
        cotangent_ref,
        gates_ref,
        router_ref,
        weight_ref,
        grad_hidden_ref,
        grad_ref,
        grad_other_ref,
        branch_ref,
        branch_other_ref,
        grad_logits_ref,
        grad_gain_ref,
    ) = refs
    total = terms[0][...]
    for term in terms[1:]:
        total = total + term[...].astype(F32)
    spread = total[ROWS : ROWS + BLOCKS] + total[ROWS + BLOCKS :]
    grad_gates = jnp.concatenate(
        [spread[:, e * GATE_COLS : e * GATE_COLS + ROWS] for e in range(LOCAL_EXPERTS)], 0
    )
    gates = gates_ref[...]
    grad_logits = gates * (grad_gates - jnp.sum(gates * grad_gates, axis=0, keepdims=True))
    grad_logits_ref[...] = grad_logits
    grad_normal = total[:ROWS] + lax.dot_general(
        grad_logits,
        router_ref[...].astype(F32),
        (((0,), (0,)), ((), ())),
        precision=EXACT,
        preferred_element_type=F32,
    )
    hidden, scale = hidden_ref[...], scale_ref[...]
    weighted = grad_normal * gain_ref[...]
    grad_gain_ref[...] = jnp.sum(grad_normal * hidden * scale, axis=0, keepdims=True)
    inner = jnp.mean(weighted * hidden, axis=-1, keepdims=True)
    grad_hidden = scale * weighted - hidden * (scale * scale * scale * inner)
    grad_hidden = grad_hidden + cotangent_ref[...].astype(F32)
    grad_hidden_ref[...] = grad_hidden
    branch = grad_hidden.astype(BF16)
    parts = [branch[:, n * QUERY_COLS : (n + 1) * QUERY_COLS] for n in range(BLOCKS)]
    z, core = place_ref[0], place_ref[1]
    for kz in range(4):
        for kc in range(2):
            device = ((z + kz) % 4) * 2 + (core + kc) % 2
            rows = pl.ds(pl.multiple_of(device * QUERY_COLS, QUERY_COLS), QUERY_COLS)
            grad = dot(branch, weight_ref[rows, :], ((1,), (1,)))
            (grad_ref, grad_other_ref)[kc][kz] = grad.astype(BF16)
            part = parts[0].astype(F32)
            for n in range(1, BLOCKS):
                part = jnp.where(device == n, parts[n].astype(F32), part)
            (branch_ref, branch_other_ref)[kc][kz] = part.astype(BF16)


def branch_back(place, terms, *operands):
    block = jax.ShapeDtypeStruct((BLOCKS // 2, ROWS, QUERY_COLS), BF16)
    return pl.pallas_call(
        branch_kernel,
        out_shape=(
            jax.ShapeDtypeStruct((ROWS, MODEL_WIDTH), F32),
            block,
            block,
            block,
            block,
            jax.ShapeDtypeStruct((EXPERTS, ROWS), F32),
            jax.ShapeDtypeStruct((1, MODEL_WIDTH), F32),
        ),
        in_specs=[pl.BlockSpec(memory_space=pltpu.SMEM)]
        + [pl.BlockSpec(memory_space=pltpu.VMEM)] * 11,
        out_specs=tuple([pl.BlockSpec(memory_space=pltpu.VMEM)] * 7),
        compiler_params=pltpu.CompilerParams(vmem_limit_bytes=60 * 2**20),
        cost_estimate=work(8),
        name="branch_back",
    )(place, *terms, *operands)


def attention_weight_kernel(place_ref, *refs):
    normals, attended, messages = refs[:BLOCKS], refs[BLOCKS : 2 * BLOCKS], refs[2 * BLOCKS : -10]
    heads_ref, out_refs, made = refs[-10], refs[-9:-1], refs[-1]
    branch = []
    for message in messages:
        branch += [message[:, :QUERY_COLS], message[:, QUERY_COLS:]]
    shard = made.shape[1]
    wide = 4 * shard
    for p in range(0, MODEL_WIDTH, wide):
        cols = slice(p, p + wide)
        one = two = None
        for b in range(BLOCKS):
            term = dot(normals[b][:, cols], heads_ref[b], ((0,), (0,)))
            one = term if b == 0 else one + term
            term = dot(attended[b][:, cols], branch[b], ((0,), (0,)))
            two = term if b == 0 else two + term
        for q in range(4):
            rows = slice(q * shard, (q + 1) * shard)
            made[p // shard + q, :, :HEAD_COLS] = one[rows].astype(BF16)
            made[p // shard + q, :, HEAD_COLS:] = two[rows].astype(BF16)
    y, x = place_ref[TILES], place_ref[TILES + 1]
    for kx in range(SIDE):
        for ky in range(SIDE):
            part = made[((y + ky) % SIDE) * SIDE + (x + kx) % SIDE]
            out_refs[kx][ky] = part[:, :HALF]
            out_refs[SIDE + ky][kx] = part[:, HALF:]


def attention_weights(place, normals, attended, branch, heads):
    rows = MODEL_WIDTH // SIDE**2
    shape = (SIDE, rows, HALF)
    return pl.pallas_call(
        attention_weight_kernel,
        out_shape=tuple([jax.ShapeDtypeStruct(shape, BF16)] * (2 * SIDE)),
        in_specs=[pl.BlockSpec(memory_space=pltpu.SMEM)]
        + [pl.BlockSpec(memory_space=pltpu.VMEM)] * (2 * BLOCKS + 5),
        out_specs=tuple([pl.BlockSpec(memory_space=pltpu.VMEM)] * (2 * SIDE)),
        scratch_shapes=[pltpu.VMEM((SIDE * SIDE, rows, 2 * HALF), BF16)],
        compiler_params=pltpu.CompilerParams(vmem_limit_bytes=60 * 2**20),
        cost_estimate=work(9),
        name="attention_weights",
    )(place, *normals, *attended, *branch, heads)


def finish_kernel(place_ref, *refs):
    pairs, refs = refs[:4], refs[4:]
    (
        weight_ref,
        tokens_ref,
        gain_ref,
        grad_hidden_ref,
        grad_logits_ref,
        normal_ref,
        grad_gain_ref,
        out_ref,
        small_ref,
        small_other_ref,
    ) = refs
    z, core = place_ref[0], place_ref[1]
    at = [((z + kz) % 4) * 2 + (core + kc) % 2 for kz in range(4) for kc in range(2)]
    parts = [pairs[b // 2][b % 2].astype(F32) for b in range(BLOCKS)]
    natural = []
    for n in range(BLOCKS):
        part = parts[0]
        for b in range(1, BLOCKS):
            part = jnp.where(at[b] == n, parts[b], part)
        natural.append(part)
    natural = jnp.concatenate(natural, 1).astype(BF16)
    grad_normal = dot(natural, weight_ref[...], ((1,), (1,)))
    inputs = tokens_ref[...].astype(F32)
    scale = lax.rsqrt(jnp.mean(inputs * inputs, axis=-1, keepdims=True) + EPSILON)
    weighted = grad_normal * gain_ref[...]
    grad_gain = jnp.sum(grad_normal * inputs * scale, axis=0, keepdims=True)
    inner = jnp.mean(weighted * inputs, axis=-1, keepdims=True)
    grad_inputs = scale * weighted - inputs * (scale * scale * scale * inner)
    out_ref[...] = (grad_inputs + grad_hidden_ref[...]).astype(BF16)
    router = lax.dot_general(
        grad_logits_ref[...],
        normal_ref[...].astype(F32),
        (((1,), (0,)), ((), ())),
        precision=EXACT,
        preferred_element_type=F32,
    )
    rest = jnp.zeros((SMALL - EXPERTS - 2, MODEL_WIDTH), F32)
    small = jnp.concatenate([router, grad_gain_ref[...], grad_gain, rest], 0)
    parts = [small[:, n * ROWS : (n + 1) * ROWS] for n in range(BLOCKS)]
    for b in range(BLOCKS):
        part = parts[0]
        for n in range(1, BLOCKS):
            part = jnp.where(at[b] == n, parts[n], part)
        (small_ref, small_other_ref)[b % 2][b // 2] = part


def finish(place, pairs, *operands):
    small = jax.ShapeDtypeStruct((BLOCKS // 2, SMALL, ROWS), F32)
    return pl.pallas_call(
        finish_kernel,
        out_shape=(jax.ShapeDtypeStruct((ROWS, MODEL_WIDTH), BF16), small, small),
        in_specs=[pl.BlockSpec(memory_space=pltpu.SMEM)]
        + [pl.BlockSpec(memory_space=pltpu.VMEM)] * 11,
        out_specs=tuple([pl.BlockSpec(memory_space=pltpu.VMEM)] * 3),
        compiler_params=pltpu.CompilerParams(vmem_limit_bytes=60 * 2**20),
        cost_estimate=work(9),
        name="finish",
    )(place, *pairs, *operands)


PER_STEP = 2
GATHER_STEPS = 1
EXPERT_STEPS = GATHER_STEPS + LOCAL_EXPERTS


def slots_hit(slot_ref, block):
    slot = lax.broadcasted_iota(jnp.int32, (SLOTS, ROWS), 0)
    slot = jnp.where(slot < CAP, slot, -2)
    return [slot_ref[block, e : e + 1, :] == slot for e in range(LOCAL_EXPERTS)]


def expert_kernel(device_ref, slot_ref, all_slots_ref, router_ref, *refs):
    normal_refs, refs = refs[:BLOCKS], refs[BLOCKS:]
    grad_refs, refs = refs[:BLOCKS], refs[BLOCKS:]
    (
        weight_one_ref,
        weight_two_ref,
        mixed_ref,
        mixed_other_ref,
        grad_mixed_ref,
        grad_mixed_other_ref,
        weights_ref,
        own_gates_ref,
        held,
        grad_held,
        gates,
        grad_gates,
    ) = refs
    step = pl.program_id(0)

    @pl.when(step < GATHER_STEPS)
    def _():
        device = device_ref[0]
        expert_at = lax.broadcasted_iota(jnp.int32, (EXPERTS, ROWS), 0)
        for block in range(BLOCKS):
            used = all_slots_ref[block] >= 0
            logits = dot(router_ref[...], normal_refs[block][...], ((1,), (1,)))
            logits = jnp.where(used, logits, MASKED)
            gate = jnp.exp(logits - jnp.max(logits, axis=0, keepdims=True))
            gate = jnp.where(used, gate, 0.0)
            gate = gate / jnp.sum(gate, axis=0, keepdims=True)
            if block == 0:
                own_gates_ref[...] = gate
            hits = slots_hit(slot_ref, block)
            spread = []
            for e in range(LOCAL_EXPERTS):
                row = jnp.sum(
                    jnp.where(expert_at == e * BLOCKS + device, gate, 0.0), axis=0, keepdims=True
                )
                spread.append(jnp.sum(jnp.where(hits[e], row, 0.0), axis=1, keepdims=True))
            chosen = jnp.concatenate(hits, 0).astype(F32).astype(BF16)
            rows = dot(chosen, normal_refs[block][...]).astype(BF16)
            grads = dot(chosen, grad_refs[block][...]).astype(BF16)
            for e in range(LOCAL_EXPERTS):
                part = slice(e * SLOTS, (e + 1) * SLOTS)
                held[e, block] = rows[part]
                grad_held[e, block] = grads[part]
                gates[e, block] = spread[e]

    @pl.when((step >= GATHER_STEPS) & (step < EXPERT_STEPS))
    def _():
        e = step - GATHER_STEPS
        blocked = (BLOCKS, SLOTS, MODEL_WIDTH)
        rows = held[e].reshape(EXPERT_ROWS, MODEL_WIDTH)
        made = dot(rows, weight_one_ref[0])
        gate_part = made[:, :FF]
        up_part = made[:, FF:]
        sigmoid_gate = jax.nn.sigmoid(gate_part)
        activation = gate_part * sigmoid_gate
        hidden = (activation * up_part).astype(BF16)
        out = dot(hidden, weight_two_ref[0]).astype(BF16).astype(F32)
        gate = gates[e].reshape(EXPERT_ROWS, 1)
        grads = grad_held[e].reshape(EXPERT_ROWS, MODEL_WIDTH).astype(F32)
        grad_gates[e] = jnp.sum(out * grads, axis=1, keepdims=True).reshape(BLOCKS, SLOTS, 1)
        held[e] = (out * gate).astype(BF16).reshape(blocked)
        grad_out = (grads * gate).astype(BF16)
        grad_hidden = dot(grad_out, weight_two_ref[0], ((1,), (1,)))
        grad_gate = (
            grad_hidden * up_part * sigmoid_gate * (1.0 + gate_part * (1.0 - sigmoid_gate))
        )
        grad_up = grad_hidden * activation
        grad_made = jnp.concatenate([grad_gate, grad_up], 1).astype(BF16)
        grad_rows = dot(grad_made, weight_one_ref[0], ((1,), (1,))).astype(BF16)
        grad_held[e] = grad_rows.reshape(blocked)
        parts, _, wide, _ = weights_ref.shape
        for p in range(0, parts, 4):
            cols = slice(p * wide, (p + 4) * wide)
            one = dot(rows[:, cols], grad_made, ((0,), (0,))).astype(BF16)
            two = dot(grad_out[:, cols], hidden, ((0,), (0,))).astype(BF16)
            for q in range(4):
                weights_ref[p + q, 0, :, : 2 * FF] = one[q * wide : (q + 1) * wide]
                weights_ref[p + q, 0, :, 2 * FF :] = two[q * wide : (q + 1) * wide]

    @pl.when(step >= EXPERT_STEPS)
    def _():
        for b in range(PER_STEP):
            block = (step - EXPERT_STEPS) * PER_STEP + b
            hits = slots_hit(slot_ref, block)
            parts = []
            for e in range(LOCAL_EXPERTS):
                part = jnp.where(hits[e], grad_gates[e, block], 0.0)
                parts.append(jnp.sum(part, axis=0, keepdims=True))
                parts.append(jnp.zeros((1, GATE_COLS - ROWS), F32))
            parts.append(jnp.zeros((1, MODEL_WIDTH - LOCAL_EXPERTS * GATE_COLS), F32))
            row = jnp.concatenate(parts, 1)
            at = lax.broadcasted_iota(jnp.int32, (BLOCKS, MODEL_WIDTH), 0)
            row = jnp.where(at == device_ref[0], row, 0.0)
            high = row.astype(BF16).astype(F32)
            row = jnp.concatenate([high, row - high], 0).astype(BF16)
            chosen = jnp.concatenate(hits, 0).astype(F32).astype(BF16)
            mixed = jnp.concatenate([held[e, block] for e in range(LOCAL_EXPERTS)], 0)
            to = (mixed_ref, mixed_other_ref)[b]
            to[0] = dot(chosen, mixed, ((0,), (0,))).astype(BF16)
            mixed = jnp.concatenate([grad_held[e, block] for e in range(LOCAL_EXPERTS)], 0)
            to = (grad_mixed_ref, grad_mixed_other_ref)[b]
            to[0, :ROWS, :] = dot(chosen, mixed, ((0,), (0,))).astype(BF16)
            to[0, ROWS:, :] = row


def expert_layer(device, slots, all_slots, router, normals, grads, weight_one, weight_two):
    steps = EXPERT_STEPS + BLOCKS // PER_STEP

    def working(s):
        return (jnp.clip(s - GATHER_STEPS, 0, LOCAL_EXPERTS - 1), 0, 0)

    def ending(s):
        return (jnp.maximum(s - EXPERT_STEPS, 0), 0, 0)

    def kept(shape):
        return pl.BlockSpec(shape, lambda s: (0,) * len(shape), pipeline_mode=pl.Buffered(1))

    table = (BLOCKS, LOCAL_EXPERTS, ROWS)
    row_block = (1, ROWS, MODEL_WIDTH)
    return pl.pallas_call(
        expert_kernel,
        grid=(steps,),
        out_shape=(
            jax.ShapeDtypeStruct((BLOCKS // 2, ROWS, MODEL_WIDTH), BF16),
            jax.ShapeDtypeStruct((BLOCKS // 2, ROWS, MODEL_WIDTH), BF16),
            jax.ShapeDtypeStruct((BLOCKS // 2, ROWS + EXTRA, MODEL_WIDTH), BF16),
            jax.ShapeDtypeStruct((BLOCKS // 2, ROWS + EXTRA, MODEL_WIDTH), BF16),
            jax.ShapeDtypeStruct(
                (SIDE * SIDE, LOCAL_EXPERTS, MODEL_WIDTH // SIDE**2, 3 * FF), BF16
            ),
            jax.ShapeDtypeStruct((EXPERTS, ROWS), F32),
        ),
        in_specs=[
            pl.BlockSpec(memory_space=pltpu.SMEM),
            kept(table),
            kept((BLOCKS, EXPERTS, ROWS)),
            kept((EXPERTS, MODEL_WIDTH)),
        ]
        + [kept((ROWS, MODEL_WIDTH))] * (2 * BLOCKS)
        + [
            pl.BlockSpec((1, MODEL_WIDTH, 2 * FF), working),
            pl.BlockSpec((1, FF, MODEL_WIDTH), working),
        ],
        out_specs=(
            pl.BlockSpec(row_block, ending),
            pl.BlockSpec(row_block, ending),
            pl.BlockSpec((1, ROWS + EXTRA, MODEL_WIDTH), ending),
            pl.BlockSpec((1, ROWS + EXTRA, MODEL_WIDTH), ending),
            pl.BlockSpec(
                (SIDE * SIDE, 1, MODEL_WIDTH // SIDE**2, 3 * FF),
                lambda s: (0, jnp.clip(s - GATHER_STEPS, 0, LOCAL_EXPERTS - 1), 0, 0),
            ),
            whole((EXPERTS, ROWS)),
        ),
        scratch_shapes=[
            pltpu.VMEM((LOCAL_EXPERTS, BLOCKS, SLOTS, MODEL_WIDTH), BF16),
            pltpu.VMEM((LOCAL_EXPERTS, BLOCKS, SLOTS, MODEL_WIDTH), BF16),
            pltpu.VMEM((LOCAL_EXPERTS, BLOCKS, SLOTS, 1), F32),
            pltpu.VMEM((LOCAL_EXPERTS, BLOCKS, SLOTS, 1), F32),
        ],
        compiler_params=pltpu.CompilerParams(vmem_limit_bytes=60 * 2**20),
        cost_estimate=work(50),
        name="expert_layer",
    )(device, slots, all_slots, router, *normals, *grads, weight_one, weight_two)


def local(
    n_dp,
    tokens,
    cotangent,
    seq_lengths,
    position_map,
    routes,
    turn_order,
    norm_gain,
    ffn_gain,
    w_query,
    key_weight,
    value_weight,
    w_out,
    w_router,
    w_gate_up,
    w_down,
):
    group = Group(BLOCKS)
    index = lax.axis_index("expert")
    shard = w_query.shape[0]

    inputs_wide = tokens.astype(F32)
    scale_one = lax.rsqrt(jnp.mean(inputs_wide * inputs_wide, axis=-1, keepdims=True) + EPSILON)
    normal_one = (inputs_wide * scale_one * norm_gain).astype(BF16)
    by_heads = jnp.concatenate(
        [
            w_query.reshape(shard, BLOCKS, QUERY_COLS),
            key_weight.reshape(shard, BLOCKS, HEAD_SIZE),
            value_weight.reshape(shard, BLOCKS, HEAD_SIZE),
        ],
        2,
    )
    own_heads = after(lax.dynamic_index_in_dim(by_heads, index, 1, keepdims=False), normal_one)
    below, above = group.send(normal_one, 1), group.send(normal_one, -1)
    row = [own_heads] + [send_dp(own_heads, 0, -k) for k in range(1, SIDE)]
    own_slots = slot_table(routes, turn_order[0]).reshape(BLOCKS, LOCAL_EXPERTS, ROWS)
    own_slots = jnp.transpose(own_slots, (1, 0, 2)).astype(BF16).reshape(EXPERTS, ROWS)
    own_slots = jnp.concatenate([own_slots, jnp.zeros((SMALL - EXPERTS, ROWS), BF16)], 0)
    row, own_slots, below, above = lax.optimization_barrier((row, own_slots, below, above))
    row = stack(row)
    own_heads = [row] + [send_dp(row, -k, 0) for k in range(1, SIDE)]
    far = group.send(after(normal_one, row), 2)
    position_map, seq_lengths = after((position_map, seq_lengths), own_heads[2])

    lengths = seq_lengths[0]
    stream = group.to_blocks(position_map[0].reshape(BLOCKS, ROWS)).reshape(GROUP)
    ordered = jnp.arange(GROUP, dtype=jnp.int32)
    begin_ordered = stream_starts(lengths, ordered)
    cosine, sine = rotary(stream - stream_starts(lengths, stream))
    first = begin_ordered[::TILE] // TILE
    at_dp = lax.axis_index("dp")
    first_dp = jnp.concatenate([first, jnp.stack([at_dp // SIDE, at_dp % SIDE])])
    begin = jnp.tile(begin_ordered.reshape(TILES, 1, TILE), (1, 1, GROUPED))
    stream_row = stream[None, :]

    own_heads, far, below, above, cosine, sine, stream_row, begin, first_dp = (
        lax.optimization_barrier(
            (own_heads, far, below, above, cosine, sine, stream_row, begin, first_dp)
        )
    )
    normals = group.both_cores([normal_one, above, far, below])
    out_full = lax.all_gather(after(w_out, row), "dp", axis=0, tiled=True)

    late = after(cotangent, *normals)
    grads = [late, group.send(late, -1), None, group.send(late, 1)]
    made = attend(first_dp, normals, own_heads, cosine, sine, stream_row, begin, own_slots)
    made, grads[1], grads[3] = lax.optimization_barrier((made, grads[1], grads[3]))
    mixed, other, query, key, value, log_total, turned = made

    heads_full = lax.all_gather(
        after(by_heads, mixed).reshape(shard, BLOCKS * HEAD_COLS), "dp", axis=0, tiled=True
    )
    attended = group.exchange_pairs(mixed, other)
    out_full, attended, grads[0] = lax.optimization_barrier((out_full, attended, grads[0]))
    grads[2] = group.send(grads[0], 2)
    swapped = [group.swap(grads[kz]) for kz in (0, 1, 3)]
    place = jnp.stack([group.z, group.core])
    made = project(place, attended, out_full, tokens, ffn_gain[None])
    (hidden_one, scale_two, normal_two), swapped = lax.optimization_barrier((made, swapped))
    along = group.along_z(normal_two)
    ordered_late, begin_late = after((ordered, begin_ordered), normal_two)
    cosine_ordered, sine_ordered = rotary(ordered_late - begin_late)
    slots = jnp.stack([pair[:, ROWS : ROWS + EXPERTS] for pair in attended], 0)
    slots = slots.reshape(BLOCKS, EXPERTS, ROWS).astype(jnp.int32)
    attended = [pair[:, :ROWS] for pair in attended]
    own_slots = lax.dynamic_index_in_dim(
        slots.reshape(BLOCKS, LOCAL_EXPERTS, BLOCKS, ROWS), index, 2, keepdims=False
    )
    along, grads[2], slots, own_slots, cosine_ordered, sine_ordered = lax.optimization_barrier(
        (along, grads[2], slots, own_slots, cosine_ordered, sine_ordered)
    )
    own, above, below = swapped
    grads = [grads[0], own, grads[1], above, grads[2], group.swap(grads[2]), grads[3], below]
    normals_two = group.both_cores(along)

    attended = group.to_natural(jnp.stack(attended, 0).reshape(BLOCKS, ROWS, QUERY_COLS))
    attended = jnp.transpose(attended, (1, 0, 2)).reshape(ROWS, QUERY_HEADS * HEAD_SIZE)
    attended_all = group.along_z(after(attended, *normals_two))

    router = w_router.T.reshape(BLOCKS, LOCAL_EXPERTS, MODEL_WIDTH)
    router = jnp.transpose(router, (1, 0, 2)).reshape(EXPERTS, MODEL_WIDTH)
    made = expert_layer(
        index[None], own_slots, slots, router, normals_two, grads, w_gate_up, w_down
    )
    made, attended_all = lax.optimization_barrier((made, attended_all))
    mixture, mixture_other, grad_mixture, grad_mixture_other = made[:4]
    expert_grads, own_gates = made[4:]
    other = group.swap(grad_mixture_other)
    grad_terms = group.sum_cores(grad_mixture, other)
    grad_terms, mixture, mixture_other, attended_all = lax.optimization_barrier(
        (grad_terms, mixture, mixture_other, attended_all)
    )
    grad_terms = group.scatter_along_z(grad_terms)
    attended_all = group.both_cores(attended_all)
    mixture = group.sum_cores(mixture, group.swap(mixture_other))
    grad_terms, attended_all, mixture = lax.optimization_barrier(
        (grad_terms, attended_all, mixture)
    )
    expert_grads = lax.psum_scatter(expert_grads, "dp", scatter_dimension=0, tiled=True)[0]

    grad_hidden_one, mine, other, branch, branch_other, grad_logits, local_ffn_gain = branch_back(
        place,
        grad_terms,
        hidden_one,
        scale_two,
        ffn_gain[None],
        cotangent,
        own_gates,
        router,
        out_full,
    )
    attended_grad = group.exchange_pairs(mine, other)
    branch_other = group.swap(branch_other)
    messages = [jnp.concatenate([branch[kz], branch_other[kz]], 1) for kz in range(4)]
    attended_grad, messages, mixture = lax.optimization_barrier((attended_grad, messages, mixture))
    mixture[1], mixture[3] = group.send(mixture[1], 1), group.send(mixture[3], 3)
    messages = messages[:1] + [group.send(messages[4 - kz], 4 - kz) for kz in range(1, 4)]
    head_grads = attend_back(
        first,
        *attended_grad,
        query,
        key,
        value,
        log_total,
        turned,
        cosine_ordered,
        sine_ordered,
        stream_row,
        stream[:, None],
        begin,
    )
    head_grads, messages, mixture = lax.optimization_barrier((head_grads, messages, mixture))
    mine, other, head_grads = head_grads
    own_grads = group.exchange_pairs(mine, other)
    local_grads = attention_weights(first_dp, normals, attended_all, messages, head_grads)
    own_grads, local_grads = lax.optimization_barrier((own_grads, local_grads))
    by_x, by_y = list(local_grads[:SIDE]), list(local_grads[SIDE:])
    from_x = [send_dp(by_x[k], 0, k) for k in range(1, SIDE)]
    made = finish(
        place,
        own_grads,
        heads_full,
        tokens,
        norm_gain[None],
        grad_hidden_one,
        grad_logits,
        normal_two,
        local_ffn_gain,
    )
    from_y = [send_dp(by_y[k], k, 0) for k in range(1, SIDE)]
    from_x, made = lax.optimization_barrier((from_x, made))
    d_tokens, small, small_other = made
    small = group.exchange_pairs(small, small_other)
    sum_x = by_x[0].astype(F32) + sum(term.astype(F32) for term in from_x)
    from_x = [send_dp(sum_x[k].astype(BF16), k, 0) for k in range(1, SIDE)]
    from_x, from_y, small = lax.optimization_barrier((from_x, from_y, small))
    small = sum(pair[0] + pair[1] for pair in small)
    sum_y = by_y[0].astype(F32) + sum(term.astype(F32) for term in from_y)
    rest = jnp.zeros((2 * SMALL, HALF - ROWS), BF16)
    behind = jnp.concatenate([in_halves(small), rest], 1)
    from_y = [
        send_dp(jnp.concatenate([sum_y[k].astype(BF16), behind], 0), 0, k) for k in range(1, SIDE)
    ]
    from_y, expert_grads = lax.optimization_barrier((from_y, expert_grads))
    parts = jnp.concatenate(
        [
            sum_x[0] + sum(term.astype(F32) for term in from_x),
            sum_y[0] + sum(term[:shard].astype(F32) for term in from_y),
        ],
        1,
    )
    small = small + sum(from_halves(term[shard:, :ROWS]) for term in from_y)
    small = small + sum(send_dp(small, k, 0) for k in range(1, SIDE))
    parts = jnp.concatenate([parts.astype(BF16), in_halves(small)], 1)
    parts = group.gather_small(parts)
    small = from_halves(parts[:, :, 2 * HALF :])
    parts = parts[:, :, : 2 * HALF]
    grad_gate_up = expert_grads[:, :, : 2 * FF].astype(F32)
    grad_down = jnp.transpose(expert_grads[:, :, 2 * FF :], (0, 2, 1)).astype(F32)
    mixture[2] = group.send(after(mixture[2], small), 2)
    output = (hidden_one + sum(term.astype(F32) for term in mixture)).astype(BF16)
    small = jnp.transpose(small, (1, 0, 2)).reshape(SMALL, MODEL_WIDTH)
    grad_router = small[:EXPERTS].reshape(LOCAL_EXPERTS, BLOCKS, MODEL_WIDTH)
    grad_router = jnp.transpose(grad_router, (2, 1, 0)).reshape(MODEL_WIDTH, EXPERTS)

    parts = jnp.transpose(parts, (1, 0, 2)).astype(F32)
    grad_query = parts[:, :, :QUERY_COLS].reshape(shard, -1)
    grad_key = parts[:, :, QUERY_COLS : QUERY_COLS + HEAD_SIZE].reshape(shard, -1)
    grad_value = parts[:, :, QUERY_COLS + HEAD_SIZE : HEAD_COLS].reshape(shard, -1)
    grad_out = parts[:, :, HEAD_COLS:].reshape(shard, -1)

    return (
        output,
        d_tokens,
        small[EXPERTS + 1],
        small[EXPERTS],
        grad_query,
        grad_key,
        grad_value,
        grad_out,
        grad_router,
        grad_gate_up,
        grad_down,
    )


def solution(mesh):
    placed = (
        P(("dp", "expert"), None),
        P(("dp", "expert"), None),
        P("dp", None),
        P("dp", None),
        P(("dp", "expert"), None),
        P(("dp", "expert"), None),
        P(),
        P(),
        P("dp", None),
        P("dp", None),
        P("dp", None),
        P("dp", None),
        P(),
        P("expert", None, None),
        P("expert", None, None),
    )
    return jax.shard_map(
        functools.partial(local, mesh.shape["dp"]),
        mesh=mesh,
        in_specs=placed,
        out_specs=(
            P(("dp", "expert"), None),
            P(("dp", "expert"), None),
            P(),
            P(),
            P("dp", None),
            P("dp", None),
            P("dp", None),
            P("dp", None),
            P(),
            P("expert", "dp", None),
            P("expert", None, "dp"),
        ),
        check_vma=False,
    )
```

```python
import functools

import jax
import jax.numpy as jnp
from jax import lax
from jax.experimental import pallas as pl
from jax.experimental.pallas import tpu as pltpu
from jax.sharding import PartitionSpec as P

MODEL_WIDTH = 1536
QUERY_HEADS = 24
KEY_VALUE_HEADS = 8
HEAD_SIZE = 64
FF = 512
TOP = 8
EXPERTS = 40

EPSILON = 1e-06
MASKED = -1e30
EXACT = lax.Precision.HIGHEST
F32 = jnp.float32
BF16 = jnp.bfloat16

ROWS = 192
BLOCKS = 8
GROUP = ROWS * BLOCKS
TILE = 256
TILES = GROUP // TILE
GROUPED = QUERY_HEADS // KEY_VALUE_HEADS
QUERY_COLS = GROUPED * HEAD_SIZE
HEAD_COLS = QUERY_COLS + 2 * HEAD_SIZE
STACK = GROUPED * TILE
CAP = 43
SLOTS = 48
LOCAL_EXPERTS = EXPERTS // BLOCKS
EXPERT_ROWS = BLOCKS * SLOTS
SMALL = 48
HALF = (HEAD_COLS + QUERY_COLS) // 2
EXTRA = 16
TABLE_ROWS = EXPERTS * ROWS // MODEL_WIDTH
GATE_COLS = 256


def work(microseconds):
    return pl.CostEstimate(flops=int(microseconds * 1e9), bytes_accessed=0, transcendentals=0)


def dot(left, right, dims=((1,), (0,))):
    return lax.dot_general(left, right, (dims, ((), ())), preferred_element_type=F32)


def whole(shape):
    return pl.BlockSpec(shape, lambda *_: (0,) * len(shape))


class Group:
    def __init__(self, devices):
        self.count = devices
        self.along = devices // 2
        index = lax.axis_index("expert")
        self.z = index // 2
        self.core = index % 2

    def send(self, value, shift, flip=0):
        steps = [
            (z * 2 + c, ((z + shift) % self.along) * 2 + (c ^ flip))
            for z in range(self.along)
            for c in range(2)
        ]
        return lax.ppermute(value, "expert", steps)

    def swap(self, value):
        return self.send(value, 0, 1)

    def along_z(self, value):
        return [value] + [self.send(value, -kz) for kz in range(1, self.along)]

    def near_halves(self, low, high):
        below, above = self.send(low, 1), self.send(high, -1)
        return [below, self.send(high, 1), self.send(low, -1), above]

    def far_halves(self, near):
        return [self.send(near[0], 1), self.send(near[3], -1)]

    def all_halves(self, own, near, far, swapped):
        order = [own, near[2:], far, near[:2]]
        cores = [swapped[:2], swapped[4:6], swapped[6:], swapped[2:4]]
        return [half for pair in zip(order, cores) for halves in pair for half in halves]

    def both_cores(self, along):
        blocks = []
        for piece in along:
            blocks += [piece, self.swap(piece)]
        return blocks

    def exchange(self, mine, other):
        other = self.swap(other)
        pairs = [jnp.concatenate([mine[kz], other[kz]], 1) for kz in range(self.along)]
        return [pairs[0]] + [
            self.send(pairs[self.along - kz], self.along - kz) for kz in range(1, self.along)
        ]

    def sum_cores(self, mine, other):
        both = [mine[kz].astype(F32) + other[kz].astype(F32) for kz in range(self.along)]
        return [both[0]] + [one.astype(BF16) for one in both[1:]]

    def scatter_along_z(self, terms):
        return [terms[0]] + [self.send(terms[kz], kz) for kz in range(1, self.along)]

    def to_natural(self, stack):
        pairs = stack.reshape((self.along, 2) + stack.shape[1:])
        pairs = jnp.where(self.core == 1, pairs[:, ::-1], pairs)
        pairs = lax.dynamic_slice_in_dim(
            jnp.concatenate([pairs, pairs], 0), self.along - self.z, self.along, 0
        )
        return pairs.reshape(stack.shape)

    def to_blocks(self, stack):
        pairs = stack.reshape((self.along, 2) + stack.shape[1:])
        pairs = lax.dynamic_slice_in_dim(
            jnp.concatenate([pairs, pairs], 0), self.z, self.along, 0
        )
        return jnp.where(self.core == 1, pairs[:, ::-1], pairs).reshape(stack.shape)


def after(value, *events):
    return lax.optimization_barrier((value, events))[0]


SIDE = 4


def send_dp(value, up, right):
    steps = [
        (y * SIDE + x, ((y + up) % SIDE) * SIDE + (x + right) % SIDE)
        for y in range(SIDE)
        for x in range(SIDE)
    ]
    return lax.ppermute(value, "dp", steps)


def stack_kernel(*refs):
    for i, ref in enumerate(refs[:-1]):
        refs[-1][i] = ref[...]


def stack(pieces):
    return pl.pallas_call(
        stack_kernel,
        out_shape=jax.ShapeDtypeStruct((len(pieces),) + pieces[0].shape, pieces[0].dtype),
        in_specs=[pl.BlockSpec(memory_space=pltpu.VMEM)] * len(pieces),
        out_specs=pl.BlockSpec(memory_space=pltpu.VMEM),
        cost_estimate=work(1),
        name="stack",
    )(*pieces)


def in_halves(value):
    high = value.astype(BF16)
    return jnp.concatenate([high, (value - high.astype(F32)).astype(BF16)], 0)


def from_halves(value):
    rows = value.shape[-2] // 2
    return value[..., :rows, :].astype(F32) + value[..., rows:, :].astype(F32)


def rotary(position):
    half = HEAD_SIZE // 2
    frequency = 10000.0 ** (-(jnp.arange(half, dtype=F32) * 2.0) / (2.0 * half))
    angles = position.astype(F32)[:, None] * frequency[None, :]
    cosine = jnp.cos(angles)
    sine = jnp.sin(angles)
    return (
        jnp.concatenate([cosine] * 4, -1),
        jnp.concatenate([-sine, sine, -sine, sine], -1),
    )


def stream_starts(lengths, stream):
    starts = jnp.cumsum(lengths) - lengths
    sequence = jnp.sum((stream[:, None] >= starts[None, 1:]).astype(jnp.int32), axis=1)
    chosen = sequence[:, None] == jnp.arange(lengths.shape[0], dtype=jnp.int32)[None, :]
    return jnp.sum(jnp.where(chosen, starts[None, :], 0), axis=1)


def slot_table(route_rows, order):
    rows = route_rows.shape[0]
    pairs = rows * TOP
    turns = jnp.arange(pairs, dtype=jnp.int32)
    turn = jnp.sum(jnp.where(order[None, :] == turns[:, None], turns[None, :], 0), axis=1)
    turn = turn.reshape(rows, TOP)
    hits = jnp.arange(EXPERTS, dtype=jnp.int32)[:, None, None] == route_rows[None]
    used = jnp.any(hits, axis=2)
    turn_of = jnp.sum(jnp.where(hits, turn[None], 0), axis=2)
    earlier = used[:, None, :] & (turn_of[:, None, :] < turn_of[:, :, None])
    slot = jnp.sum(earlier.astype(jnp.int32), axis=2)
    return jnp.where(used, slot, -1)


def turn(values, cosine, signed_sine):
    lane = lax.broadcasted_iota(jnp.int32, values.shape, 1) % HEAD_SIZE
    half = HEAD_SIZE // 2
    width = values.shape[1]
    other = jnp.where(
        lane < half,
        pltpu.roll(values, width - half, 1),
        pltpu.roll(values, half, 1),
    )
    return values * cosine + other * signed_sine


def visible_keys(tile, key_tile, begin):
    key_at = lax.broadcasted_iota(jnp.int32, (TILE, STACK), 0) + key_tile * TILE
    query_at = lax.broadcasted_iota(jnp.int32, (TILE, STACK), 1) % TILE + tile * TILE
    return (key_at >= begin) & (key_at <= query_at)


def attend_kernel(
    first_ref,
    *refs,
):
    normal_refs, refs = refs[:BLOCKS], refs[BLOCKS:]
    weight_refs, refs = refs[:SIDE], refs[SIDE:]
    (
    cosine_ref,
    sine_ref,
    stream_ref,
    begin_ref,
    slots_ref,
    out_ref,
    other_ref,
    query_ref,
    key_ref,
    value_ref,
    total_ref,
    turned_ref,
    heads,
    place,
    weights,
    ) = refs
    y, x = first_ref[TILES], first_ref[TILES + 1]
    for ky in range(SIDE):
        for kx in range(SIDE):
            weights[((y + ky) % SIDE) * SIDE + (x + kx) % SIDE] = weight_refs[ky][kx]
    weight = weights[...].reshape(MODEL_WIDTH, HEAD_COLS)
    for b in range(BLOCKS):
        rows = pl.ds(b * ROWS, ROWS)
        cosine = cosine_ref[rows, :]
        sine = sine_ref[rows, :]
        made = dot(normal_refs[b][...], weight)
        one = turn(made[:, :128], cosine, sine)
        two = turn(made[:, 128:256], cosine, sine)
        heads[rows, :] = jnp.concatenate([one, two, made[:, 256:]], 1).astype(BF16)
    for i in range(TILES):
        rows = pl.ds(i * TILE, TILE)
        at = lax.broadcasted_iota(jnp.int32, (TILE, GROUP), 0) + i * TILE
        chosen = (stream_ref[...] == at).astype(F32).astype(BF16)
        place[rows, :] = chosen
        ordered = dot(chosen, heads[...])
        for h in range(GROUPED):
            part = ordered[:, h * HEAD_SIZE : (h + 1) * HEAD_SIZE] * (HEAD_SIZE**-0.5)
            query_ref[i, pl.ds(h * TILE, TILE), :] = part.astype(BF16)
        key_ref[rows, :] = ordered[:, QUERY_COLS : QUERY_COLS + HEAD_SIZE].astype(BF16)
        value_ref[rows, :] = ordered[:, QUERY_COLS + HEAD_SIZE :].astype(BF16)
    for i in range(TILES):
        query = query_ref[i]
        begin = begin_ref[i]

        def step(j, carry, query=query, begin=begin, i=i):
            top, total, mixed = carry
            rows = pl.ds(pl.multiple_of(j * TILE, TILE), TILE)
            scores = dot(key_ref[rows, :], query, ((1,), (1,)))
            scores = jnp.where(visible_keys(i, j, begin), scores, MASKED)
            new_top = jnp.maximum(top, jnp.max(scores, axis=0, keepdims=True))
            weight = jnp.exp(scores - new_top)
            fade = jnp.exp(top - new_top)
            total = total * fade + jnp.sum(weight, axis=0, keepdims=True)
            mixed = mixed * fade + dot(value_ref[rows, :], weight.astype(BF16), ((0,), (0,)))
            return new_top, total, mixed

        top, total, mixed = lax.fori_loop(
            first_ref[i],
            i + 1,
            step,
            (
                jnp.full((1, STACK), MASKED, F32),
                jnp.zeros((1, STACK), F32),
                jnp.zeros((HEAD_SIZE, STACK), F32),
            ),
        )
        total_ref[i] = top + jnp.log(total)
        mixed = mixed / total
        for h in range(GROUPED):
            turned_ref[pl.ds(h * HEAD_SIZE, HEAD_SIZE), pl.ds(i * TILE, TILE)] = mixed[
                :, h * TILE : (h + 1) * TILE
            ].astype(BF16)
    mixed = dot(turned_ref[...], place[...]).T.astype(BF16)
    for b in range(BLOCKS):
        to = (out_ref, other_ref)[b % 2]
        to[b // 2, :ROWS, :] = mixed[b * ROWS : (b + 1) * ROWS]
        to[b // 2, ROWS:, :] = slots_ref[...]


def attend(first, normals, weights, cosine, sine, stream, begin, slots):
    return pl.pallas_call(
        attend_kernel,
        out_shape=(
            jax.ShapeDtypeStruct((BLOCKS // 2, ROWS + SMALL, QUERY_COLS), BF16),
            jax.ShapeDtypeStruct((BLOCKS // 2, ROWS + SMALL, QUERY_COLS), BF16),
            jax.ShapeDtypeStruct((TILES, STACK, HEAD_SIZE), BF16),
            jax.ShapeDtypeStruct((GROUP, HEAD_SIZE), BF16),
            jax.ShapeDtypeStruct((GROUP, HEAD_SIZE), BF16),
            jax.ShapeDtypeStruct((TILES, 1, STACK), F32),
            jax.ShapeDtypeStruct((QUERY_COLS, GROUP), BF16),
        ),
        in_specs=[pl.BlockSpec(memory_space=pltpu.SMEM)]
        + [pl.BlockSpec(memory_space=pltpu.VMEM)] * (BLOCKS + SIDE + 5),
        out_specs=tuple([pl.BlockSpec(memory_space=pltpu.VMEM)] * 7),
        scratch_shapes=[
            pltpu.VMEM((GROUP, HEAD_COLS), BF16),
            pltpu.VMEM((GROUP, GROUP), BF16),
            pltpu.VMEM((SIDE * SIDE, MODEL_WIDTH // SIDE**2, HEAD_COLS), BF16),
        ],
        compiler_params=pltpu.CompilerParams(vmem_limit_bytes=60 * 2**20),
        cost_estimate=work(20),
        name="attend",
    )(first, *normals, *weights, cosine, sine, stream, begin, slots)


def attend_back_kernel(
    first_ref,
    grad_0_ref,
    grad_1_ref,
    grad_2_ref,
    grad_3_ref,
    query_ref,
    key_ref,
    value_ref,
    total_ref,
    turned_ref,
    cosine_ref,
    sine_ref,
    stream_row_ref,
    stream_ref,
    begin_ref,
    *refs,
):
    out_refs, (whole_ref, grad_key, grad_value, grad_heads) = refs[:2], refs[2:]
    pairs = (grad_0_ref, grad_1_ref, grad_2_ref, grad_3_ref)
    grads = jnp.concatenate(
        [
            pair[:, kc * QUERY_COLS : (kc + 1) * QUERY_COLS]
            for pair in pairs
            for kc in range(2)
        ],
        0,
    )
    grad_key[...] = jnp.zeros_like(grad_key)
    grad_value[...] = jnp.zeros_like(grad_value)
    for i in range(TILES):
        query = query_ref[i]
        begin = begin_ref[i]
        total = total_ref[i]
        at = lax.broadcasted_iota(jnp.int32, (TILE, GROUP), 0) + i * TILE
        chosen = (stream_row_ref[...] == at).astype(F32).astype(BF16)
        grad = dot(chosen, grads)
        grad_turned = grad.T
        product = grad_turned * turned_ref[:, pl.ds(i * TILE, TILE)].astype(F32)
        inner = jnp.concatenate(
            [
                jnp.sum(product[h * HEAD_SIZE : (h + 1) * HEAD_SIZE], axis=0, keepdims=True)
                for h in range(GROUPED)
            ],
            1,
        )
        grad = jnp.concatenate(
            [grad[:, h * HEAD_SIZE : (h + 1) * HEAD_SIZE] for h in range(GROUPED)], 0
        ).astype(BF16)

        def step(j, grad_query, query=query, begin=begin, total=total, inner=inner, grad=grad, i=i):
            rows = pl.ds(pl.multiple_of(j * TILE, TILE), TILE)
            key = key_ref[rows, :]
            scores = dot(key, query, ((1,), (1,)))
            scores = jnp.where(visible_keys(i, j, begin), scores, MASKED)
            weight = jnp.exp(scores - total)
            grad_weight = dot(value_ref[rows, :], grad, ((1,), (1,)))
            grad_scores = (weight * (grad_weight - inner)).astype(BF16)
            grad_value[rows, :] += dot(weight.astype(BF16), grad)
            grad_key[rows, :] += dot(grad_scores, query)
            return grad_query + dot(key, grad_scores, ((0,), (0,)))

        grad_query = lax.fori_loop(
            first_ref[i], i + 1, step, jnp.zeros((HEAD_SIZE, STACK), F32)
        )
        grad_query = grad_query * (HEAD_SIZE**-0.5)
        for h in range(GROUPED):
            grad_heads[pl.ds(i * TILE, TILE), h * HEAD_SIZE : (h + 1) * HEAD_SIZE] = grad_query[
                :, h * TILE : (h + 1) * TILE
            ].T.astype(F32)
    grad_heads[:, QUERY_COLS : QUERY_COLS + HEAD_SIZE] = grad_key[...]
    ready = []
    for i in range(TILES):
        rows = pl.ds(i * TILE, TILE)
        cosine = cosine_ref[rows, :]
        sine = -sine_ref[rows, :]
        one = turn(grad_heads[rows, :128], cosine, sine)
        two = turn(grad_heads[rows, 128:256], cosine, sine)
        ready.append(jnp.concatenate([one, two, grad_value[rows, :]], 1).astype(BF16))
    ready = jnp.concatenate(ready, 0)
    for b in range(BLOCKS):
        rows = pl.ds(b * ROWS, ROWS)
        at = lax.broadcasted_iota(jnp.int32, (ROWS, GROUP), 1)
        chosen = (stream_ref[rows, :] == at).astype(F32).astype(BF16)
        found = dot(chosen, ready).astype(BF16)
        out_refs[b % 2][b // 2] = found
        whole_ref[b] = found


def attend_back(*operands):
    return pl.pallas_call(
        attend_back_kernel,
        out_shape=tuple([jax.ShapeDtypeStruct((4, ROWS, HEAD_COLS), BF16)] * 2)
        + (jax.ShapeDtypeStruct((BLOCKS, ROWS, HEAD_COLS), BF16),),
        in_specs=[pl.BlockSpec(memory_space=pltpu.SMEM)]
        + [pl.BlockSpec(memory_space=pltpu.VMEM)] * 14,
        out_specs=tuple([pl.BlockSpec(memory_space=pltpu.VMEM)] * 3),
        scratch_shapes=[
            pltpu.VMEM((GROUP, HEAD_SIZE), F32),
            pltpu.VMEM((GROUP, HEAD_SIZE), F32),
            pltpu.VMEM((GROUP, 4 * HEAD_SIZE), F32),
        ],
        compiler_params=pltpu.CompilerParams(vmem_limit_bytes=60 * 2**20),
        cost_estimate=work(22),
        name="attend_back",
    )(*operands)


def project_kernel(place_ref, *refs):
    pairs, refs = refs[:4], refs[4:]
    weight_ref, inputs_ref, gain_ref, hidden_ref, scale_ref, low_ref, high_ref = refs
    z, core = place_ref[0], place_ref[1]
    hidden = inputs_ref[...].astype(F32)
    for kz in range(4):
        for kc in range(2):
            device = ((z + kz) % 4) * 2 + (core + kc) % 2
            rows = pl.ds(pl.multiple_of(device * QUERY_COLS, QUERY_COLS), QUERY_COLS)
            part = pairs[kz][:ROWS, kc * QUERY_COLS : (kc + 1) * QUERY_COLS]
            hidden = hidden + dot(part, weight_ref[rows, :])
    hidden_ref[...] = hidden
    scale = lax.rsqrt(jnp.mean(hidden * hidden, axis=-1, keepdims=True) + EPSILON)
    scale_ref[...] = scale
    normal = (hidden * scale * gain_ref[...]).astype(BF16)
    low_ref[...] = normal[: ROWS // 2]
    high_ref[...] = normal[ROWS // 2 :]


def project(place, pairs, weight, inputs, gain):
    return pl.pallas_call(
        project_kernel,
        out_shape=(
            jax.ShapeDtypeStruct((ROWS, MODEL_WIDTH), F32),
            jax.ShapeDtypeStruct((ROWS, 1), F32),
            jax.ShapeDtypeStruct((ROWS // 2, MODEL_WIDTH), BF16),
            jax.ShapeDtypeStruct((ROWS // 2, MODEL_WIDTH), BF16),
        ),
        in_specs=[pl.BlockSpec(memory_space=pltpu.SMEM)]
        + [pl.BlockSpec(memory_space=pltpu.VMEM)] * 7,
        out_specs=tuple([pl.BlockSpec(memory_space=pltpu.VMEM)] * 4),
        compiler_params=pltpu.CompilerParams(vmem_limit_bytes=60 * 2**20),
        cost_estimate=work(3),
        name="project",
    )(place, *pairs, weight, inputs, gain)


def branch_kernel(place_ref, *refs):
    terms, refs = refs[:5], refs[5:]
    (
        hidden_ref,
        scale_ref,
        gain_ref,
        cotangent_ref,
        gates_ref,
        router_ref,
        weight_ref,
        grad_hidden_ref,
        grad_ref,
        grad_other_ref,
        branch_ref,
        branch_other_ref,
        grad_logits_ref,
        grad_gain_ref,
    ) = refs
    total = terms[0][...]
    for halves in (terms[1:3], terms[3:]):
        total = total + jnp.concatenate([half[...] for half in halves], 0).astype(F32)
    spread = total[ROWS : ROWS + BLOCKS] + total[ROWS + BLOCKS :]
    grad_gates = jnp.concatenate(
        [spread[:, e * GATE_COLS : e * GATE_COLS + ROWS] for e in range(LOCAL_EXPERTS)], 0
    )
    gates = gates_ref[...]
    grad_logits = gates * (grad_gates - jnp.sum(gates * grad_gates, axis=0, keepdims=True))
    grad_logits_ref[...] = grad_logits
    grad_normal = total[:ROWS] + lax.dot_general(
        grad_logits,
        router_ref[...].astype(F32),
        (((0,), (0,)), ((), ())),
        precision=EXACT,
        preferred_element_type=F32,
    )
    hidden, scale = hidden_ref[...], scale_ref[...]
    weighted = grad_normal * gain_ref[...]
    grad_gain_ref[...] = jnp.sum(grad_normal * hidden * scale, axis=0, keepdims=True)
    inner = jnp.mean(weighted * hidden, axis=-1, keepdims=True)
    grad_hidden = scale * weighted - hidden * (scale * scale * scale * inner)
    grad_hidden = grad_hidden + cotangent_ref[...].astype(F32)
    grad_hidden_ref[...] = grad_hidden
    branch = grad_hidden.astype(BF16)
    parts = [branch[:, n * QUERY_COLS : (n + 1) * QUERY_COLS] for n in range(BLOCKS)]
    z, core = place_ref[0], place_ref[1]
    for kz in range(4):
        for kc in range(2):
            device = ((z + kz) % 4) * 2 + (core + kc) % 2
            rows = pl.ds(pl.multiple_of(device * QUERY_COLS, QUERY_COLS), QUERY_COLS)
            grad = dot(branch, weight_ref[rows, :], ((1,), (1,)))
            (grad_ref, grad_other_ref)[kc][kz] = grad.astype(BF16)
            part = parts[0].astype(F32)
            for n in range(1, BLOCKS):
                part = jnp.where(device == n, parts[n].astype(F32), part)
            (branch_ref, branch_other_ref)[kc][kz] = part.astype(BF16)


def branch_back(place, terms, *operands):
    block = jax.ShapeDtypeStruct((BLOCKS // 2, ROWS, QUERY_COLS), BF16)
    return pl.pallas_call(
        branch_kernel,
        out_shape=(
            jax.ShapeDtypeStruct((ROWS, MODEL_WIDTH), F32),
            block,
            block,
            block,
            block,
            jax.ShapeDtypeStruct((EXPERTS, ROWS), F32),
            jax.ShapeDtypeStruct((1, MODEL_WIDTH), F32),
        ),
        in_specs=[pl.BlockSpec(memory_space=pltpu.SMEM)]
        + [pl.BlockSpec(memory_space=pltpu.VMEM)] * 12,
        out_specs=tuple([pl.BlockSpec(memory_space=pltpu.VMEM)] * 7),
        compiler_params=pltpu.CompilerParams(vmem_limit_bytes=60 * 2**20),
        cost_estimate=work(8),
        name="branch_back",
    )(place, *terms, *operands)


def attention_weight_kernel(place_ref, at_ref, *refs):
    normals, attended, refs = refs[:BLOCKS], refs[BLOCKS : 2 * BLOCKS], refs[2 * BLOCKS :]
    messages, weight_refs, refs = refs[:4], refs[4:8], refs[8:]
    heads_ref, logits_ref, low_ref, high_ref, gain_ref, *refs = refs
    out_refs, (small_ref, small_other_ref, made, weights) = refs[:SIDE], refs[SIDE:]
    y, x = place_ref[TILES], place_ref[TILES + 1]
    for ky in range(SIDE):
        for kx in range(SIDE):
            weights[((y + ky) % SIDE) * SIDE + (x + kx) % SIDE] = weight_refs[ky][kx]
    products = []
    branch = []
    for message in messages:
        branch += [message[:, :QUERY_COLS], message[:, QUERY_COLS:]]
    shard = made.shape[1]
    wide = 4 * shard
    for p in range(0, MODEL_WIDTH, wide):
        cols = slice(p, p + wide)
        one = two = None
        for b in range(BLOCKS):
            term = dot(normals[b][:, cols], heads_ref[b], ((0,), (0,)))
            one = term if b == 0 else one + term
            term = dot(attended[b][:, cols], branch[b], ((0,), (0,)))
            two = term if b == 0 else two + term
        weight = weights[p // shard : p // shard + 4].reshape(wide, HEAD_COLS).astype(F32)
        product = jnp.sum(one * weight, axis=1, keepdims=True)
        products.append(jnp.broadcast_to(product, (wide, 128)).T[:1])
        for q in range(4):
            rows = slice(q * shard, (q + 1) * shard)
            made[p // shard + q, :, :HEAD_COLS] = one[rows].astype(BF16)
            made[p // shard + q, :, HEAD_COLS:] = two[rows].astype(BF16)
    normal = jnp.concatenate([low_ref[...], high_ref[...]], 0)
    router = lax.dot_general(
        logits_ref[...],
        normal.astype(F32),
        (((1,), (0,)), ((), ())),
        precision=EXACT,
        preferred_element_type=F32,
    )
    rest = jnp.zeros((SMALL - EXPERTS - 2, MODEL_WIDTH), F32)
    small = jnp.concatenate([router, gain_ref[...], jnp.concatenate(products, 1), rest], 0)
    parts = [small[:, n * ROWS : (n + 1) * ROWS] for n in range(BLOCKS)]
    z, core = at_ref[0], at_ref[1]
    for b in range(BLOCKS):
        device = (z + b // 2) % 4 * 2 + (core + b) % 2
        part = parts[0]
        for n in range(1, BLOCKS):
            part = jnp.where(device == n, parts[n], part)
        (small_ref, small_other_ref)[b % 2][b // 2] = part
    for kx in range(SIDE):
        for ky in range(SIDE):
            part = made[((y + ky) % SIDE) * SIDE + (x + kx) % SIDE]
            out_refs[ky][kx] = part


def attention_weights(place, at, normals, attended, branch, weights, *operands):
    rows = MODEL_WIDTH // SIDE**2
    shape = (SIDE, rows, 2 * HALF)
    return pl.pallas_call(
        attention_weight_kernel,
        out_shape=tuple([jax.ShapeDtypeStruct(shape, BF16)] * SIDE)
        + tuple([jax.ShapeDtypeStruct((BLOCKS // 2, SMALL, ROWS), F32)] * 2),
        in_specs=[pl.BlockSpec(memory_space=pltpu.SMEM)] * 2
        + [pl.BlockSpec(memory_space=pltpu.VMEM)] * (2 * BLOCKS + 13),
        out_specs=tuple([pl.BlockSpec(memory_space=pltpu.VMEM)] * (SIDE + 2)),
        scratch_shapes=[
            pltpu.VMEM((SIDE * SIDE, rows, 2 * HALF), BF16),
            pltpu.VMEM((SIDE * SIDE, rows, HEAD_COLS), BF16),
        ],
        compiler_params=pltpu.CompilerParams(vmem_limit_bytes=60 * 2**20),
        cost_estimate=work(9),
        name="attention_weights",
    )(place, at, *normals, *attended, *branch, *weights, *operands)


def finish_kernel(place_ref, *refs):
    pairs, (weight_ref, tokens_ref, gain_ref, grad_hidden_ref, out_ref) = refs[:4], refs[4:]
    z, core = place_ref[0], place_ref[1]
    at = [((z + kz) % 4) * 2 + (core + kc) % 2 for kz in range(4) for kc in range(2)]
    parts = [
        pairs[b // 2][:, b % 2 * HEAD_COLS : (b % 2 + 1) * HEAD_COLS].astype(F32)
        for b in range(BLOCKS)
    ]
    natural = []
    for n in range(BLOCKS):
        part = parts[0]
        for b in range(1, BLOCKS):
            part = jnp.where(at[b] == n, parts[b], part)
        natural.append(part)
    natural = jnp.concatenate(natural, 1).astype(BF16)
    grad_normal = dot(natural, weight_ref[...], ((1,), (1,)))
    inputs = tokens_ref[...].astype(F32)
    scale = lax.rsqrt(jnp.mean(inputs * inputs, axis=-1, keepdims=True) + EPSILON)
    weighted = grad_normal * gain_ref[...]
    inner = jnp.mean(weighted * inputs, axis=-1, keepdims=True)
    grad_inputs = scale * weighted - inputs * (scale * scale * scale * inner)
    out_ref[...] = (grad_inputs + grad_hidden_ref[...]).astype(BF16)


def finish(place, pairs, *operands):
    return pl.pallas_call(
        finish_kernel,
        out_shape=jax.ShapeDtypeStruct((ROWS, MODEL_WIDTH), BF16),
        in_specs=[pl.BlockSpec(memory_space=pltpu.SMEM)]
        + [pl.BlockSpec(memory_space=pltpu.VMEM)] * 8,
        out_specs=pl.BlockSpec(memory_space=pltpu.VMEM),
        compiler_params=pltpu.CompilerParams(vmem_limit_bytes=60 * 2**20),
        cost_estimate=work(9),
        name="finish",
    )(place, *pairs, *operands)


def spread_kernel(at_ref, mine_ref, other_ref, *out_refs):
    z, core = at_ref[0], at_ref[1]
    begin = 0
    for n in range(BLOCKS):
        kz = (n // 2 + 4 - z) % 4
        block = jnp.where(core == n % 2, mine_ref[kz].astype(F32), other_ref[kz].astype(F32))
        begin = 0
        for out, wide in zip(out_refs, (QUERY_COLS, HEAD_SIZE, HEAD_SIZE, QUERY_COLS)):
            out[:, n * wide : (n + 1) * wide] = block[:, begin : begin + wide]
            begin += wide
        small = block[:, begin : begin + ROWS]
        out_refs[4][:, n * ROWS : (n + 1) * ROWS] = small[:SMALL] + small[SMALL:]


def spread(at, mine, other):
    rows = mine.shape[1]
    wide = (BLOCKS * QUERY_COLS, BLOCKS * HEAD_SIZE, BLOCKS * HEAD_SIZE, BLOCKS * QUERY_COLS)
    return pl.pallas_call(
        spread_kernel,
        out_shape=tuple(jax.ShapeDtypeStruct((rows, w), F32) for w in wide)
        + (jax.ShapeDtypeStruct((SMALL, MODEL_WIDTH), F32),),
        in_specs=[pl.BlockSpec(memory_space=pltpu.SMEM)]
        + [pl.BlockSpec(memory_space=pltpu.VMEM)] * 2,
        out_specs=tuple([pl.BlockSpec(memory_space=pltpu.VMEM)] * 5),
        compiler_params=pltpu.CompilerParams(vmem_limit_bytes=60 * 2**20),
        cost_estimate=work(3),
        name="spread",
    )(at, mine, other)


PER_STEP = 2
GATHER_STEPS = 1
EXPERT_STEPS = GATHER_STEPS + LOCAL_EXPERTS


def slots_hit(slot_ref, block):
    slot = lax.broadcasted_iota(jnp.int32, (SLOTS, ROWS), 0)
    slot = jnp.where(slot < CAP, slot, -2)
    return [slot_ref[block, e : e + 1, :] == slot for e in range(LOCAL_EXPERTS)]


def expert_kernel(device_ref, slot_ref, all_slots_ref, router_ref, *refs):
    normal_refs, refs = refs[: 2 * BLOCKS], refs[2 * BLOCKS :]
    grad_refs, refs = refs[: 2 * BLOCKS], refs[2 * BLOCKS :]
    (
        weight_one_ref,
        weight_two_ref,
        mixed_ref,
        mixed_other_ref,
        grad_mixed_ref,
        grad_mixed_other_ref,
        weights_ref,
        own_gates_ref,
        held,
        grad_held,
        gates,
        grad_gates,
    ) = refs
    step = pl.program_id(0)

    @pl.when(step < GATHER_STEPS)
    def _():
        device = device_ref[0]
        expert_at = lax.broadcasted_iota(jnp.int32, (EXPERTS, ROWS), 0)
        for block in range(BLOCKS):
            used = all_slots_ref[block] >= 0
            halves = slice(2 * block, 2 * block + 2)
            normal = jnp.concatenate([ref[...] for ref in normal_refs[halves]], 0)
            grads = jnp.concatenate([ref[...] for ref in grad_refs[halves]], 0)
            logits = dot(router_ref[...], normal, ((1,), (1,)))
            logits = jnp.where(used, logits, MASKED)
            gate = jnp.exp(logits - jnp.max(logits, axis=0, keepdims=True))
            gate = jnp.where(used, gate, 0.0)
            gate = gate / jnp.sum(gate, axis=0, keepdims=True)
            if block == 0:
                own_gates_ref[...] = gate
            hits = slots_hit(slot_ref, block)
            spread = []
            for e in range(LOCAL_EXPERTS):
                row = jnp.sum(
                    jnp.where(expert_at == e * BLOCKS + device, gate, 0.0), axis=0, keepdims=True
                )
                spread.append(jnp.sum(jnp.where(hits[e], row, 0.0), axis=1, keepdims=True))
            chosen = jnp.concatenate(hits, 0).astype(F32).astype(BF16)
            rows = dot(chosen, normal).astype(BF16)
            grads = dot(chosen, grads).astype(BF16)
            for e in range(LOCAL_EXPERTS):
                part = slice(e * SLOTS, (e + 1) * SLOTS)
                held[e, block] = rows[part]
                grad_held[e, block] = grads[part]
                gates[e, block] = spread[e]

    @pl.when((step >= GATHER_STEPS) & (step < EXPERT_STEPS))
    def _():
        e = step - GATHER_STEPS
        blocked = (BLOCKS, SLOTS, MODEL_WIDTH)
        rows = held[e].reshape(EXPERT_ROWS, MODEL_WIDTH)
        made = dot(rows, weight_one_ref[0])
        gate_part = made[:, :FF]
        up_part = made[:, FF:]
        sigmoid_gate = jax.nn.sigmoid(gate_part)
        activation = gate_part * sigmoid_gate
        hidden = (activation * up_part).astype(BF16)
        out = dot(hidden, weight_two_ref[0]).astype(BF16).astype(F32)
        gate = gates[e].reshape(EXPERT_ROWS, 1)
        grads = grad_held[e].reshape(EXPERT_ROWS, MODEL_WIDTH).astype(F32)
        grad_gates[e] = jnp.sum(out * grads, axis=1, keepdims=True).reshape(BLOCKS, SLOTS, 1)
        held[e] = (out * gate).astype(BF16).reshape(blocked)
        grad_out = (grads * gate).astype(BF16)
        grad_hidden = dot(grad_out, weight_two_ref[0], ((1,), (1,)))
        grad_gate = (
            grad_hidden * up_part * sigmoid_gate * (1.0 + gate_part * (1.0 - sigmoid_gate))
        )
        grad_up = grad_hidden * activation
        grad_made = jnp.concatenate([grad_gate, grad_up], 1).astype(BF16)
        grad_rows = dot(grad_made, weight_one_ref[0], ((1,), (1,))).astype(BF16)
        grad_held[e] = grad_rows.reshape(blocked)
        parts, _, wide, _ = weights_ref.shape
        for p in range(0, parts, 4):
            cols = slice(p * wide, (p + 4) * wide)
            one = dot(rows[:, cols], grad_made, ((0,), (0,))).astype(BF16)
            two = dot(grad_out[:, cols], hidden, ((0,), (0,))).astype(BF16)
            for q in range(4):
                weights_ref[p + q, 0, :, : 2 * FF] = one[q * wide : (q + 1) * wide]
                weights_ref[p + q, 0, :, 2 * FF :] = two[q * wide : (q + 1) * wide]

    @pl.when(step >= EXPERT_STEPS)
    def _():
        for b in range(PER_STEP):
            block = (step - EXPERT_STEPS) * PER_STEP + b
            hits = slots_hit(slot_ref, block)
            parts = []
            for e in range(LOCAL_EXPERTS):
                part = jnp.where(hits[e], grad_gates[e, block], 0.0)
                parts.append(jnp.sum(part, axis=0, keepdims=True))
                parts.append(jnp.zeros((1, GATE_COLS - ROWS), F32))
            parts.append(jnp.zeros((1, MODEL_WIDTH - LOCAL_EXPERTS * GATE_COLS), F32))
            row = jnp.concatenate(parts, 1)
            at = lax.broadcasted_iota(jnp.int32, (BLOCKS, MODEL_WIDTH), 0)
            row = jnp.where(at == device_ref[0], row, 0.0)
            high = row.astype(BF16).astype(F32)
            row = jnp.concatenate([high, row - high], 0).astype(BF16)
            chosen = jnp.concatenate(hits, 0).astype(F32).astype(BF16)
            mixed = jnp.concatenate([held[e, block] for e in range(LOCAL_EXPERTS)], 0)
            to = (mixed_ref, mixed_other_ref)[b]
            to[0] = dot(chosen, mixed, ((0,), (0,))).astype(BF16)
            mixed = jnp.concatenate([grad_held[e, block] for e in range(LOCAL_EXPERTS)], 0)
            to = (grad_mixed_ref, grad_mixed_other_ref)[b]
            to[0, :ROWS, :] = dot(chosen, mixed, ((0,), (0,))).astype(BF16)
            to[0, ROWS:, :] = row


def expert_layer(device, slots, all_slots, router, normals, grads, weight_one, weight_two):
    steps = EXPERT_STEPS + BLOCKS // PER_STEP

    def working(s):
        return (jnp.clip(s - GATHER_STEPS, 0, LOCAL_EXPERTS - 1), 0, 0)

    def ending(s):
        return (jnp.maximum(s - EXPERT_STEPS, 0), 0, 0)

    def kept(shape):
        return pl.BlockSpec(shape, lambda s: (0,) * len(shape), pipeline_mode=pl.Buffered(1))

    table = (BLOCKS, LOCAL_EXPERTS, ROWS)
    row_block = (1, ROWS, MODEL_WIDTH)
    return pl.pallas_call(
        expert_kernel,
        grid=(steps,),
        out_shape=(
            jax.ShapeDtypeStruct((BLOCKS // 2, ROWS, MODEL_WIDTH), BF16),
            jax.ShapeDtypeStruct((BLOCKS // 2, ROWS, MODEL_WIDTH), BF16),
            jax.ShapeDtypeStruct((BLOCKS // 2, ROWS + EXTRA, MODEL_WIDTH), BF16),
            jax.ShapeDtypeStruct((BLOCKS // 2, ROWS + EXTRA, MODEL_WIDTH), BF16),
            jax.ShapeDtypeStruct(
                (SIDE * SIDE, LOCAL_EXPERTS, MODEL_WIDTH // SIDE**2, 3 * FF), BF16
            ),
            jax.ShapeDtypeStruct((EXPERTS, ROWS), F32),
        ),
        in_specs=[
            pl.BlockSpec(memory_space=pltpu.SMEM),
            kept(table),
            kept((BLOCKS, EXPERTS, ROWS)),
            kept((EXPERTS, MODEL_WIDTH)),
        ]
        + [kept((ROWS // 2, MODEL_WIDTH))] * (4 * BLOCKS)
        + [
            pl.BlockSpec((1, MODEL_WIDTH, 2 * FF), working),
            pl.BlockSpec((1, FF, MODEL_WIDTH), working),
        ],
        out_specs=(
            pl.BlockSpec(row_block, ending),
            pl.BlockSpec(row_block, ending),
            pl.BlockSpec((1, ROWS + EXTRA, MODEL_WIDTH), ending),
            pl.BlockSpec((1, ROWS + EXTRA, MODEL_WIDTH), ending),
            pl.BlockSpec(
                (SIDE * SIDE, 1, MODEL_WIDTH // SIDE**2, 3 * FF),
                lambda s: (0, jnp.clip(s - GATHER_STEPS, 0, LOCAL_EXPERTS - 1), 0, 0),
            ),
            whole((EXPERTS, ROWS)),
        ),
        scratch_shapes=[
            pltpu.VMEM((LOCAL_EXPERTS, BLOCKS, SLOTS, MODEL_WIDTH), BF16),
            pltpu.VMEM((LOCAL_EXPERTS, BLOCKS, SLOTS, MODEL_WIDTH), BF16),
            pltpu.VMEM((LOCAL_EXPERTS, BLOCKS, SLOTS, 1), F32),
            pltpu.VMEM((LOCAL_EXPERTS, BLOCKS, SLOTS, 1), F32),
        ],
        compiler_params=pltpu.CompilerParams(vmem_limit_bytes=60 * 2**20),
        cost_estimate=work(50),
        name="expert_layer",
    )(device, slots, all_slots, router, *normals, *grads, weight_one, weight_two)


def local(
    n_dp,
    tokens,
    cotangent,
    seq_lengths,
    position_map,
    routes,
    turn_order,
    norm_gain,
    ffn_gain,
    w_query,
    key_weight,
    value_weight,
    w_out,
    w_router,
    w_gate_up,
    w_down,
):
    group = Group(BLOCKS)
    index = lax.axis_index("expert")
    shard = w_query.shape[0]

    inputs_wide = tokens.astype(F32)
    scale_one = lax.rsqrt(jnp.mean(inputs_wide * inputs_wide, axis=-1, keepdims=True) + EPSILON)
    normal_one = (inputs_wide * scale_one * norm_gain).astype(BF16)
    by_heads = jnp.concatenate(
        [
            w_query.reshape(shard, BLOCKS, QUERY_COLS),
            key_weight.reshape(shard, BLOCKS, HEAD_SIZE),
            value_weight.reshape(shard, BLOCKS, HEAD_SIZE),
        ],
        2,
    )
    own_heads = after(lax.dynamic_index_in_dim(by_heads, index, 1, keepdims=False), normal_one)
    below, above = group.send(normal_one, 1), group.send(normal_one, -1)
    row = [own_heads] + [send_dp(own_heads, 0, -k) for k in range(1, SIDE)]
    own_slots = slot_table(routes, turn_order[0]).reshape(BLOCKS, LOCAL_EXPERTS, ROWS)
    own_slots = jnp.transpose(own_slots, (1, 0, 2)).astype(BF16).reshape(EXPERTS, ROWS)
    own_slots = jnp.concatenate([own_slots, jnp.zeros((SMALL - EXPERTS, ROWS), BF16)], 0)
    row, own_slots, below, above = lax.optimization_barrier((row, own_slots, below, above))
    row = stack(row)
    own_heads = [row] + [send_dp(row, -k, 0) for k in range(1, SIDE)]
    far = group.send(after(normal_one, row), 2)
    position_map, seq_lengths = after((position_map, seq_lengths), own_heads[2])

    lengths = seq_lengths[0]
    stream = group.to_blocks(position_map[0].reshape(BLOCKS, ROWS)).reshape(GROUP)
    ordered = jnp.arange(GROUP, dtype=jnp.int32)
    begin_ordered = stream_starts(lengths, ordered)
    cosine, sine = rotary(stream - stream_starts(lengths, stream))
    first = begin_ordered[::TILE] // TILE
    at_dp = lax.axis_index("dp")
    first_dp = jnp.concatenate([first, jnp.stack([at_dp // SIDE, at_dp % SIDE])])
    begin = jnp.tile(begin_ordered.reshape(TILES, 1, TILE), (1, 1, GROUPED))
    stream_row = stream[None, :]

    own_heads, far, below, above, cosine, sine, stream_row, begin, first_dp = (
        lax.optimization_barrier(
            (own_heads, far, below, above, cosine, sine, stream_row, begin, first_dp)
        )
    )
    normals = group.both_cores([normal_one, above, far, below])
    out_full = lax.all_gather(after(w_out, row), "dp", axis=0, tiled=True)

    half = ROWS // 2
    grads = after([cotangent[:half], cotangent[half:]], *normals)
    grads_near = group.near_halves(*grads)
    made = attend(first_dp, normals, own_heads, cosine, sine, stream_row, begin, own_slots)
    made, grads_near = lax.optimization_barrier((made, grads_near))
    mixed, other, query, key, value, log_total, turned = made

    heads_full = lax.all_gather(
        after(by_heads, mixed).reshape(shard, BLOCKS * HEAD_COLS), "dp", axis=0, tiled=True
    )
    attended = group.exchange(mixed, other)
    out_full, attended, grads = lax.optimization_barrier((out_full, attended, grads))
    grads_far = group.far_halves(grads_near)
    grads_swapped = [group.swap(half) for half in grads + grads_near]
    place = jnp.stack([group.z, group.core])
    made = project(place, attended, out_full, tokens, ffn_gain[None])
    made, grads_far, grads_swapped = lax.optimization_barrier((made, grads_far, grads_swapped))
    hidden_one, scale_two, *normal_two = made
    near = group.near_halves(*normal_two)
    *own, near[0] = lax.optimization_barrier((*normal_two, near[0]))
    own = [group.swap(half) for half in own]
    far = group.far_halves(near)
    grads_swapped += [group.swap(half) for half in grads_far]
    grads = group.all_halves(grads, grads_near, grads_far, grads_swapped)
    ordered_late, begin_late = after((ordered, begin_ordered), *normal_two)
    cosine_ordered, sine_ordered = rotary(ordered_late - begin_late)
    blocks = [pair[:, c * ROWS : (c + 1) * ROWS] for pair in attended for c in range(2)]
    slots = jnp.stack([block[ROWS : ROWS + EXPERTS] for block in blocks], 0).astype(jnp.int32)
    attended = jnp.stack([block[:ROWS] for block in blocks], 0)
    own_slots = lax.dynamic_index_in_dim(
        slots.reshape(BLOCKS, LOCAL_EXPERTS, BLOCKS, ROWS), index, 2, keepdims=False
    )
    far, grads, slots, own_slots, cosine_ordered, sine_ordered = lax.optimization_barrier(
        (far, grads, slots, own_slots, cosine_ordered, sine_ordered)
    )
    swapped = own + [group.swap(half) for half in near + far]
    normals_two = group.all_halves(normal_two, near, far, swapped)

    attended = group.to_natural(attended)
    attended = jnp.transpose(attended, (1, 0, 2)).reshape(ROWS, QUERY_HEADS * HEAD_SIZE)
    attended_all = group.along_z(after(attended, *normals_two))

    router = w_router.T.reshape(BLOCKS, LOCAL_EXPERTS, MODEL_WIDTH)
    router = jnp.transpose(router, (1, 0, 2)).reshape(EXPERTS, MODEL_WIDTH)
    made = expert_layer(
        index[None], own_slots, slots, router, normals_two, grads, w_gate_up, w_down
    )
    made, attended_all = lax.optimization_barrier((made, attended_all))
    mixture, mixture_other, grad_mixture, grad_mixture_other = made[:4]
    expert_grads, own_gates = made[4:]
    other = group.swap(grad_mixture_other)
    def total(kz, begin, end):
        mine, theirs = grad_mixture[kz, begin:end], other[kz, begin:end]
        return mine.astype(F32) + theirs.astype(F32)

    end = ROWS + EXTRA
    far = [total(2, 0, half).astype(BF16), total(2, half, end).astype(BF16)]
    ready = [total(1, half, end).astype(BF16), total(3, 0, half).astype(BF16)]
    waiting = [total(1, 0, half), total(3, half, end), total(0, 0, end)]
    far, ready, waiting = lax.optimization_barrier((far, ready, waiting))
    far = [group.send(far[0], 1), group.send(far[1], -1)]
    ready = [group.send(ready[0], 1), group.send(ready[1], -1)]
    above, below = waiting[0] + far[0].astype(F32), waiting[1] + far[1].astype(F32)
    above, below = group.send(above.astype(BF16), 1), group.send(below.astype(BF16), -1)
    grad_terms = [waiting[2], above, ready[0], ready[1], below]
    expert_grads = lax.psum_scatter(expert_grads, "dp", scatter_dimension=0, tiled=True)[0]

    mixture_other, attended_all = after((mixture_other, attended_all), *grad_terms)
    mixture_other = group.swap(mixture_other)
    attended_all = group.both_cores(attended_all)
    made = branch_back(
        place,
        grad_terms,
        hidden_one,
        scale_two,
        ffn_gain[None],
        cotangent,
        own_gates,
        router,
        out_full,
    )
    made, mixture_other, attended_all = lax.optimization_barrier(
        (made, mixture_other, attended_all)
    )
    grad_hidden_one, mine, other, branch, branch_other, grad_logits, local_ffn_gain = made
    attended_grad = group.exchange(mine, other)
    mixture = group.sum_cores(mixture, after(mixture_other, mine))
    branch_other = group.swap(branch_other)
    messages = [jnp.concatenate([branch[kz], branch_other[kz]], 1) for kz in range(4)]
    attended_grad, messages, mixture = lax.optimization_barrier((attended_grad, messages, mixture))
    mixture[1], mixture[3] = group.send(mixture[1], 1), group.send(mixture[3], 3)
    messages = messages[:1] + [group.send(messages[4 - kz], 4 - kz) for kz in range(1, 4)]
    head_grads = attend_back(
        first,
        *attended_grad,
        query,
        key,
        value,
        log_total,
        turned,
        cosine_ordered,
        sine_ordered,
        stream_row,
        stream[:, None],
        begin,
    )
    head_grads, messages, mixture = lax.optimization_barrier((head_grads, messages, mixture))
    mine, other, head_grads = head_grads
    local_grads = attention_weights(
        first_dp,
        place,
        normals,
        attended_all,
        messages,
        own_heads,
        head_grads,
        grad_logits,
        *normal_two,
        local_ffn_gain,
    )
    *by_y, small, small_other = local_grads
    mine, other, *by_y = lax.optimization_barrier((mine, other, *by_y))
    from_y = [send_dp(by_y[k], k, 0) for k in range(1, SIDE)]
    small = group.exchange(small, small_other)
    own_grads = group.exchange(mine, other)
    from_y, small = lax.optimization_barrier((from_y, small))
    small = sum(pair[:, :ROWS] + pair[:, ROWS:] for pair in small)
    row = by_y[0].astype(F32) + sum(term.astype(F32) for term in from_y)
    rest = jnp.zeros((2 * SMALL, 2 * HALF - ROWS), BF16)
    behind = jnp.concatenate([in_halves(small), rest], 1)
    from_x = [
        send_dp(jnp.concatenate([row[k].astype(BF16), behind], 0), 0, k) for k in range(1, SIDE)
    ]
    d_tokens = finish(place, own_grads, heads_full, tokens, norm_gain[None], grad_hidden_one)
    from_x, d_tokens = lax.optimization_barrier((from_x, d_tokens))
    parts = row[0] + sum(term[:shard].astype(F32) for term in from_x)
    small = small + sum(from_halves(term[shard:, :ROWS]) for term in from_x)
    row = [send_dp(small, k, 0) for k in range(1, SIDE)]
    mixture[2] = group.send(mixture[2], 2)
    row, mixture, expert_grads = lax.optimization_barrier((row, mixture, expert_grads))
    small = small + sum(row)
    parts = jnp.concatenate([parts.astype(BF16), in_halves(small)], 1)
    parts = jnp.stack(group.along_z(parts), 0)
    grad_query, grad_key, grad_value, grad_out, small = spread(place, parts, group.swap(parts))
    grad_gate_up = expert_grads[:, :, : 2 * FF].astype(F32)
    grad_down = jnp.transpose(expert_grads[:, :, 2 * FF :], (0, 2, 1)).astype(F32)
    output = (hidden_one + sum(term.astype(F32) for term in mixture)).astype(BF16)
    grad_router = small[:EXPERTS].reshape(LOCAL_EXPERTS, BLOCKS, MODEL_WIDTH)
    grad_router = jnp.transpose(grad_router, (2, 1, 0)).reshape(MODEL_WIDTH, EXPERTS)

    return (
        output,
        d_tokens,
        small[EXPERTS + 1] / norm_gain,
        small[EXPERTS],
        grad_query,
        grad_key,
        grad_value,
        grad_out,
        grad_router,
        grad_gate_up,
        grad_down,
    )


def solution(mesh):
    placed = (
        P(("dp", "expert"), None),
        P(("dp", "expert"), None),
        P("dp", None),
        P("dp", None),
        P(("dp", "expert"), None),
        P(("dp", "expert"), None),
        P(),
        P(),
        P("dp", None),
        P("dp", None),
        P("dp", None),
        P("dp", None),
        P(),
        P("expert", None, None),
        P("expert", None, None),
    )
    return jax.shard_map(
        functools.partial(local, mesh.shape["dp"]),
        mesh=mesh,
        in_specs=placed,
        out_specs=(
            P(("dp", "expert"), None),
            P(("dp", "expert"), None),
            P(),
            P(),
            P("dp", None),
            P("dp", None),
            P("dp", None),
            P("dp", None),
            P(),
            P("expert", "dp", None),
            P("expert", None, "dp"),
        ),
        check_vma=False,
    )
```

```python
import functools

import jax
import jax.numpy as jnp
from jax import lax
from jax.experimental import pallas as pl
from jax.experimental.pallas import tpu as pltpu
from jax.sharding import PartitionSpec as P

MODEL_WIDTH = 1536
QUERY_HEADS = 24
KEY_VALUE_HEADS = 8
HEAD_SIZE = 64
FF = 512
TOP = 8
EXPERTS = 40

EPSILON = 1e-06
MASKED = -1e30
EXACT = lax.Precision.HIGHEST
F32 = jnp.float32
BF16 = jnp.bfloat16

ROWS = 192
BLOCKS = 8
GROUP = ROWS * BLOCKS
TILE = 256
TILES = GROUP // TILE
GROUPED = QUERY_HEADS // KEY_VALUE_HEADS
QUERY_COLS = GROUPED * HEAD_SIZE
HEAD_COLS = QUERY_COLS + 2 * HEAD_SIZE
STACK = GROUPED * TILE
CAP = 43
SLOTS = 48
LOCAL_EXPERTS = EXPERTS // BLOCKS
EXPERT_ROWS = BLOCKS * SLOTS
SMALL = 48
HALF = (HEAD_COLS + QUERY_COLS) // 2
EXTRA = 16
TABLE_ROWS = EXPERTS * ROWS // MODEL_WIDTH
GATE_COLS = 256


def work(microseconds):
    return pl.CostEstimate(flops=int(microseconds * 1e9), bytes_accessed=0, transcendentals=0)


def dot(left, right, dims=((1,), (0,))):
    return lax.dot_general(left, right, (dims, ((), ())), preferred_element_type=F32)


def whole(shape):
    return pl.BlockSpec(shape, lambda *_: (0,) * len(shape))


class Group:
    def __init__(self, devices):
        self.count = devices
        self.along = devices // 2
        index = lax.axis_index("expert")
        self.z = index // 2
        self.core = index % 2

    def send(self, value, shift, flip=0):
        steps = [
            (z * 2 + c, ((z + shift) % self.along) * 2 + (c ^ flip))
            for z in range(self.along)
            for c in range(2)
        ]
        return lax.ppermute(value, "expert", steps)

    def swap(self, value):
        return self.send(value, 0, 1)

    def along_z(self, value):
        return [value] + [self.send(value, -kz) for kz in range(1, self.along)]

    def near_halves(self, low, high):
        below, above = self.send(low, 1), self.send(high, -1)
        return [below, self.send(high, 1), self.send(low, -1), above]

    def far_halves(self, near):
        return [self.send(near[0], 1), self.send(near[3], -1)]

    def all_halves(self, own, near, far, swapped):
        order = [own, near[2:], far, near[:2]]
        cores = [swapped[:2], swapped[4:6], swapped[6:], swapped[2:4]]
        return [half for pair in zip(order, cores) for halves in pair for half in halves]

    def both_cores(self, along):
        blocks = []
        for piece in along:
            blocks += [piece, self.swap(piece)]
        return blocks

    def exchange(self, mine, other):
        other = self.swap(other)
        pairs = [jnp.concatenate([mine[kz], other[kz]], 1) for kz in range(self.along)]
        return [pairs[0]] + [
            self.send(pairs[self.along - kz], self.along - kz) for kz in range(1, self.along)
        ]

    def sum_cores(self, mine, other):
        both = [mine[kz].astype(F32) + other[kz].astype(F32) for kz in range(self.along)]
        return [both[0]] + [one.astype(BF16) for one in both[1:]]

    def scatter_along_z(self, terms):
        return [terms[0]] + [self.send(terms[kz], kz) for kz in range(1, self.along)]

    def to_natural(self, stack):
        pairs = stack.reshape((self.along, 2) + stack.shape[1:])
        pairs = jnp.where(self.core == 1, pairs[:, ::-1], pairs)
        pairs = lax.dynamic_slice_in_dim(
            jnp.concatenate([pairs, pairs], 0), self.along - self.z, self.along, 0
        )
        return pairs.reshape(stack.shape)

    def to_blocks(self, stack):
        pairs = stack.reshape((self.along, 2) + stack.shape[1:])
        pairs = lax.dynamic_slice_in_dim(
            jnp.concatenate([pairs, pairs], 0), self.z, self.along, 0
        )
        return jnp.where(self.core == 1, pairs[:, ::-1], pairs).reshape(stack.shape)


def after(value, *events):
    return lax.optimization_barrier((value, events))[0]


SIDE = 4


def send_dp(value, up, right):
    steps = [
        (y * SIDE + x, ((y + up) % SIDE) * SIDE + (x + right) % SIDE)
        for y in range(SIDE)
        for x in range(SIDE)
    ]
    return lax.ppermute(value, "dp", steps)


def stack_kernel(*refs):
    for i, ref in enumerate(refs[:-1]):
        refs[-1][i] = ref[...]


def stack(pieces):
    return pl.pallas_call(
        stack_kernel,
        out_shape=jax.ShapeDtypeStruct((len(pieces),) + pieces[0].shape, pieces[0].dtype),
        in_specs=[pl.BlockSpec(memory_space=pltpu.VMEM)] * len(pieces),
        out_specs=pl.BlockSpec(memory_space=pltpu.VMEM),
        cost_estimate=work(1),
        name="stack",
    )(*pieces)


def in_halves(value):
    high = value.astype(BF16)
    return jnp.concatenate([high, (value - high.astype(F32)).astype(BF16)], 0)


def from_halves(value):
    rows = value.shape[-2] // 2
    return value[..., :rows, :].astype(F32) + value[..., rows:, :].astype(F32)


def rotary(position):
    half = HEAD_SIZE // 2
    frequency = 10000.0 ** (-(jnp.arange(half, dtype=F32) * 2.0) / (2.0 * half))
    angles = position.astype(F32)[:, None] * frequency[None, :]
    cosine = jnp.cos(angles)
    sine = jnp.sin(angles)
    return (
        jnp.concatenate([cosine] * 4, -1),
        jnp.concatenate([-sine, sine, -sine, sine], -1),
    )


def stream_starts(lengths, stream):
    starts = jnp.cumsum(lengths) - lengths
    sequence = jnp.sum((stream[:, None] >= starts[None, 1:]).astype(jnp.int32), axis=1)
    chosen = sequence[:, None] == jnp.arange(lengths.shape[0], dtype=jnp.int32)[None, :]
    return jnp.sum(jnp.where(chosen, starts[None, :], 0), axis=1)


def slot_table(route_rows, order):
    rows = route_rows.shape[0]
    pairs = rows * TOP
    turns = jnp.arange(pairs, dtype=jnp.int32)
    turn = jnp.sum(jnp.where(order[None, :] == turns[:, None], turns[None, :], 0), axis=1)
    turn = turn.reshape(rows, TOP)
    hits = jnp.arange(EXPERTS, dtype=jnp.int32)[:, None, None] == route_rows[None]
    used = jnp.any(hits, axis=2)
    turn_of = jnp.sum(jnp.where(hits, turn[None], 0), axis=2)
    earlier = used[:, None, :] & (turn_of[:, None, :] < turn_of[:, :, None])
    slot = jnp.sum(earlier.astype(jnp.int32), axis=2)
    return jnp.where(used, slot, -1)


def turn(values, cosine, signed_sine):
    lane = lax.broadcasted_iota(jnp.int32, values.shape, 1) % HEAD_SIZE
    half = HEAD_SIZE // 2
    width = values.shape[1]
    other = jnp.where(
        lane < half,
        pltpu.roll(values, width - half, 1),
        pltpu.roll(values, half, 1),
    )
    return values * cosine + other * signed_sine


def visible_keys(tile, key_tile, begin):
    key_at = lax.broadcasted_iota(jnp.int32, (TILE, STACK), 0) + key_tile * TILE
    query_at = lax.broadcasted_iota(jnp.int32, (TILE, STACK), 1) % TILE + tile * TILE
    return (key_at >= begin) & (key_at <= query_at)


def attend_kernel(
    first_ref,
    *refs,
):
    normal_refs, refs = refs[:BLOCKS], refs[BLOCKS:]
    weight_refs, refs = refs[:SIDE], refs[SIDE:]
    (
    cosine_ref,
    sine_ref,
    stream_ref,
    begin_ref,
    slots_ref,
    out_ref,
    other_ref,
    query_ref,
    key_ref,
    value_ref,
    total_ref,
    turned_ref,
    heads,
    place,
    weights,
    ) = refs
    y, x = first_ref[TILES], first_ref[TILES + 1]
    for ky in range(SIDE):
        for kx in range(SIDE):
            weights[((y + ky) % SIDE) * SIDE + (x + kx) % SIDE] = weight_refs[ky][kx]
    weight = weights[...].reshape(MODEL_WIDTH, HEAD_COLS)
    for b in range(BLOCKS):
        rows = pl.ds(b * ROWS, ROWS)
        cosine = cosine_ref[rows, :]
        sine = sine_ref[rows, :]
        made = dot(normal_refs[b][...], weight)
        one = turn(made[:, :128], cosine, sine)
        two = turn(made[:, 128:256], cosine, sine)
        heads[rows, :] = jnp.concatenate([one, two, made[:, 256:]], 1).astype(BF16)
    for i in range(TILES):
        rows = pl.ds(i * TILE, TILE)
        at = lax.broadcasted_iota(jnp.int32, (TILE, GROUP), 0) + i * TILE
        chosen = (stream_ref[...] == at).astype(F32).astype(BF16)
        place[rows, :] = chosen
        ordered = dot(chosen, heads[...])
        for h in range(GROUPED):
            part = ordered[:, h * HEAD_SIZE : (h + 1) * HEAD_SIZE] * (HEAD_SIZE**-0.5)
            query_ref[i, pl.ds(h * TILE, TILE), :] = part.astype(BF16)
        key_ref[rows, :] = ordered[:, QUERY_COLS : QUERY_COLS + HEAD_SIZE].astype(BF16)
        value_ref[rows, :] = ordered[:, QUERY_COLS + HEAD_SIZE :].astype(BF16)
    for i in range(TILES):
        query = query_ref[i]
        begin = begin_ref[i]

        def step(j, carry, query=query, begin=begin, i=i):
            top, total, mixed = carry
            rows = pl.ds(pl.multiple_of(j * TILE, TILE), TILE)
            scores = dot(key_ref[rows, :], query, ((1,), (1,)))
            scores = jnp.where(visible_keys(i, j, begin), scores, MASKED)
            new_top = jnp.maximum(top, jnp.max(scores, axis=0, keepdims=True))
            weight = jnp.exp(scores - new_top)
            fade = jnp.exp(top - new_top)
            total = total * fade + jnp.sum(weight, axis=0, keepdims=True)
            mixed = mixed * fade + dot(value_ref[rows, :], weight.astype(BF16), ((0,), (0,)))
            return new_top, total, mixed

        top, total, mixed = lax.fori_loop(
            first_ref[i],
            i + 1,
            step,
            (
                jnp.full((1, STACK), MASKED, F32),
                jnp.zeros((1, STACK), F32),
                jnp.zeros((HEAD_SIZE, STACK), F32),
            ),
        )
        total_ref[i] = top + jnp.log(total)
        mixed = mixed / total
        for h in range(GROUPED):
            turned_ref[pl.ds(h * HEAD_SIZE, HEAD_SIZE), pl.ds(i * TILE, TILE)] = mixed[
                :, h * TILE : (h + 1) * TILE
            ].astype(BF16)
    mixed = dot(turned_ref[...], place[...]).T.astype(BF16)
    for b in range(BLOCKS):
        to = (out_ref, other_ref)[b % 2]
        to[b // 2, :ROWS, :] = mixed[b * ROWS : (b + 1) * ROWS]
        to[b // 2, ROWS:, :] = slots_ref[...]


def attend(first, normals, weights, cosine, sine, stream, begin, slots):
    return pl.pallas_call(
        attend_kernel,
        out_shape=(
            jax.ShapeDtypeStruct((BLOCKS // 2, ROWS + SMALL, QUERY_COLS), BF16),
            jax.ShapeDtypeStruct((BLOCKS // 2, ROWS + SMALL, QUERY_COLS), BF16),
            jax.ShapeDtypeStruct((TILES, STACK, HEAD_SIZE), BF16),
            jax.ShapeDtypeStruct((GROUP, HEAD_SIZE), BF16),
            jax.ShapeDtypeStruct((GROUP, HEAD_SIZE), BF16),
            jax.ShapeDtypeStruct((TILES, 1, STACK), F32),
            jax.ShapeDtypeStruct((QUERY_COLS, GROUP), BF16),
        ),
        in_specs=[pl.BlockSpec(memory_space=pltpu.SMEM)]
        + [pl.BlockSpec(memory_space=pltpu.VMEM)] * (BLOCKS + SIDE + 5),
        out_specs=tuple([pl.BlockSpec(memory_space=pltpu.VMEM)] * 7),
        scratch_shapes=[
            pltpu.VMEM((GROUP, HEAD_COLS), BF16),
            pltpu.VMEM((GROUP, GROUP), BF16),
            pltpu.VMEM((SIDE * SIDE, MODEL_WIDTH // SIDE**2, HEAD_COLS), BF16),
        ],
        compiler_params=pltpu.CompilerParams(vmem_limit_bytes=60 * 2**20),
        cost_estimate=work(20),
        name="attend",
    )(first, *normals, *weights, cosine, sine, stream, begin, slots)


def attend_back_kernel(
    first_ref,
    grad_0_ref,
    grad_1_ref,
    grad_2_ref,
    grad_3_ref,
    query_ref,
    key_ref,
    value_ref,
    total_ref,
    turned_ref,
    cosine_ref,
    sine_ref,
    stream_row_ref,
    stream_ref,
    begin_ref,
    *refs,
):
    out_refs, (whole_ref, grad_key, grad_value, grad_heads) = refs[:2], refs[2:]
    pairs = (grad_0_ref, grad_1_ref, grad_2_ref, grad_3_ref)
    grads = jnp.concatenate(
        [
            pair[:, kc * QUERY_COLS : (kc + 1) * QUERY_COLS]
            for pair in pairs
            for kc in range(2)
        ],
        0,
    )
    grad_key[...] = jnp.zeros_like(grad_key)
    grad_value[...] = jnp.zeros_like(grad_value)
    for i in range(TILES):
        query = query_ref[i]
        begin = begin_ref[i]
        total = total_ref[i]
        at = lax.broadcasted_iota(jnp.int32, (TILE, GROUP), 0) + i * TILE
        chosen = (stream_row_ref[...] == at).astype(F32).astype(BF16)
        grad = dot(chosen, grads)
        grad_turned = grad.T
        product = grad_turned * turned_ref[:, pl.ds(i * TILE, TILE)].astype(F32)
        inner = jnp.concatenate(
            [
                jnp.sum(product[h * HEAD_SIZE : (h + 1) * HEAD_SIZE], axis=0, keepdims=True)
                for h in range(GROUPED)
            ],
            1,
        )
        grad = jnp.concatenate(
            [grad[:, h * HEAD_SIZE : (h + 1) * HEAD_SIZE] for h in range(GROUPED)], 0
        ).astype(BF16)

        def step(j, grad_query, query=query, begin=begin, total=total, inner=inner, grad=grad, i=i):
            rows = pl.ds(pl.multiple_of(j * TILE, TILE), TILE)
            key = key_ref[rows, :]
            scores = dot(key, query, ((1,), (1,)))
            scores = jnp.where(visible_keys(i, j, begin), scores, MASKED)
            weight = jnp.exp(scores - total)
            grad_weight = dot(value_ref[rows, :], grad, ((1,), (1,)))
            grad_scores = (weight * (grad_weight - inner)).astype(BF16)
            grad_value[rows, :] += dot(weight.astype(BF16), grad)
            grad_key[rows, :] += dot(grad_scores, query)
            return grad_query + dot(key, grad_scores, ((0,), (0,)))

        grad_query = lax.fori_loop(
            first_ref[i], i + 1, step, jnp.zeros((HEAD_SIZE, STACK), F32)
        )
        grad_query = grad_query * (HEAD_SIZE**-0.5)
        for h in range(GROUPED):
            grad_heads[pl.ds(i * TILE, TILE), h * HEAD_SIZE : (h + 1) * HEAD_SIZE] = grad_query[
                :, h * TILE : (h + 1) * TILE
            ].T.astype(F32)
    grad_heads[:, QUERY_COLS : QUERY_COLS + HEAD_SIZE] = grad_key[...]
    ready = []
    for i in range(TILES):
        rows = pl.ds(i * TILE, TILE)
        cosine = cosine_ref[rows, :]
        sine = -sine_ref[rows, :]
        one = turn(grad_heads[rows, :128], cosine, sine)
        two = turn(grad_heads[rows, 128:256], cosine, sine)
        ready.append(jnp.concatenate([one, two, grad_value[rows, :]], 1).astype(BF16))
    ready = jnp.concatenate(ready, 0)
    for b in range(BLOCKS):
        rows = pl.ds(b * ROWS, ROWS)
        at = lax.broadcasted_iota(jnp.int32, (ROWS, GROUP), 1)
        chosen = (stream_ref[rows, :] == at).astype(F32).astype(BF16)
        found = dot(chosen, ready).astype(BF16)
        out_refs[b % 2][b // 2] = found
        whole_ref[b] = found


def attend_back(*operands):
    return pl.pallas_call(
        attend_back_kernel,
        out_shape=tuple([jax.ShapeDtypeStruct((4, ROWS, HEAD_COLS), BF16)] * 2)
        + (jax.ShapeDtypeStruct((BLOCKS, ROWS, HEAD_COLS), BF16),),
        in_specs=[pl.BlockSpec(memory_space=pltpu.SMEM)]
        + [pl.BlockSpec(memory_space=pltpu.VMEM)] * 14,
        out_specs=tuple([pl.BlockSpec(memory_space=pltpu.VMEM)] * 3),
        scratch_shapes=[
            pltpu.VMEM((GROUP, HEAD_SIZE), F32),
            pltpu.VMEM((GROUP, HEAD_SIZE), F32),
            pltpu.VMEM((GROUP, 4 * HEAD_SIZE), F32),
        ],
        compiler_params=pltpu.CompilerParams(vmem_limit_bytes=60 * 2**20),
        cost_estimate=work(22),
        name="attend_back",
    )(*operands)


def project_kernel(place_ref, *refs):
    pairs, refs = refs[:4], refs[4:]
    weight_ref, inputs_ref, gain_ref, hidden_ref, scale_ref, low_ref, high_ref = refs
    z, core = place_ref[0], place_ref[1]
    hidden = inputs_ref[...].astype(F32)
    for kz in range(4):
        for kc in range(2):
            device = ((z + kz) % 4) * 2 + (core + kc) % 2
            rows = pl.ds(pl.multiple_of(device * QUERY_COLS, QUERY_COLS), QUERY_COLS)
            part = pairs[kz][:ROWS, kc * QUERY_COLS : (kc + 1) * QUERY_COLS]
            hidden = hidden + dot(part, weight_ref[rows, :])
    hidden_ref[...] = hidden
    scale = lax.rsqrt(jnp.mean(hidden * hidden, axis=-1, keepdims=True) + EPSILON)
    scale_ref[...] = scale
    normal = (hidden * scale * gain_ref[...]).astype(BF16)
    low_ref[...] = normal[: ROWS // 2]
    high_ref[...] = normal[ROWS // 2 :]


def project(place, pairs, weight, inputs, gain):
    return pl.pallas_call(
        project_kernel,
        out_shape=(
            jax.ShapeDtypeStruct((ROWS, MODEL_WIDTH), F32),
            jax.ShapeDtypeStruct((ROWS, 1), F32),
            jax.ShapeDtypeStruct((ROWS // 2, MODEL_WIDTH), BF16),
            jax.ShapeDtypeStruct((ROWS // 2, MODEL_WIDTH), BF16),
        ),
        in_specs=[pl.BlockSpec(memory_space=pltpu.SMEM)]
        + [pl.BlockSpec(memory_space=pltpu.VMEM)] * 7,
        out_specs=tuple([pl.BlockSpec(memory_space=pltpu.VMEM)] * 4),
        compiler_params=pltpu.CompilerParams(vmem_limit_bytes=60 * 2**20),
        cost_estimate=work(3),
        name="project",
    )(place, *pairs, weight, inputs, gain)


def branch_kernel(place_ref, *refs):
    terms, refs = refs[:5], refs[5:]
    (
        hidden_ref,
        scale_ref,
        gain_ref,
        cotangent_ref,
        gates_ref,
        router_ref,
        weight_ref,
        grad_hidden_ref,
        grad_ref,
        grad_other_ref,
        branch_ref,
        branch_other_ref,
        grad_logits_ref,
        grad_gain_ref,
    ) = refs
    total = terms[0][...]
    for halves in (terms[1:3], terms[3:]):
        total = total + jnp.concatenate([half[...] for half in halves], 0).astype(F32)
    spread = total[ROWS : ROWS + BLOCKS] + total[ROWS + BLOCKS :]
    grad_gates = jnp.concatenate(
        [spread[:, e * GATE_COLS : e * GATE_COLS + ROWS] for e in range(LOCAL_EXPERTS)], 0
    )
    gates = gates_ref[...]
    grad_logits = gates * (grad_gates - jnp.sum(gates * grad_gates, axis=0, keepdims=True))
    grad_logits_ref[...] = grad_logits
    grad_normal = total[:ROWS] + lax.dot_general(
        grad_logits,
        router_ref[...].astype(F32),
        (((0,), (0,)), ((), ())),
        precision=EXACT,
        preferred_element_type=F32,
    )
    hidden, scale = hidden_ref[...], scale_ref[...]
    weighted = grad_normal * gain_ref[...]
    grad_gain_ref[...] = jnp.sum(grad_normal * hidden * scale, axis=0, keepdims=True)
    inner = jnp.mean(weighted * hidden, axis=-1, keepdims=True)
    grad_hidden = scale * weighted - hidden * (scale * scale * scale * inner)
    grad_hidden = grad_hidden + cotangent_ref[...].astype(F32)
    grad_hidden_ref[...] = grad_hidden
    branch = grad_hidden.astype(BF16)
    parts = [branch[:, n * QUERY_COLS : (n + 1) * QUERY_COLS] for n in range(BLOCKS)]
    z, core = place_ref[0], place_ref[1]
    for kz in range(4):
        for kc in range(2):
            device = ((z + kz) % 4) * 2 + (core + kc) % 2
            rows = pl.ds(pl.multiple_of(device * QUERY_COLS, QUERY_COLS), QUERY_COLS)
            grad = dot(branch, weight_ref[rows, :], ((1,), (1,)))
            (grad_ref, grad_other_ref)[kc][kz] = grad.astype(BF16)
            part = parts[0].astype(F32)
            for n in range(1, BLOCKS):
                part = jnp.where(device == n, parts[n].astype(F32), part)
            (branch_ref, branch_other_ref)[kc][kz] = part.astype(BF16)


def branch_back(place, terms, *operands):
    block = jax.ShapeDtypeStruct((BLOCKS // 2, ROWS, QUERY_COLS), BF16)
    return pl.pallas_call(
        branch_kernel,
        out_shape=(
            jax.ShapeDtypeStruct((ROWS, MODEL_WIDTH), F32),
            block,
            block,
            block,
            block,
            jax.ShapeDtypeStruct((EXPERTS, ROWS), F32),
            jax.ShapeDtypeStruct((1, MODEL_WIDTH), F32),
        ),
        in_specs=[pl.BlockSpec(memory_space=pltpu.SMEM)]
        + [pl.BlockSpec(memory_space=pltpu.VMEM)] * 12,
        out_specs=tuple([pl.BlockSpec(memory_space=pltpu.VMEM)] * 7),
        compiler_params=pltpu.CompilerParams(vmem_limit_bytes=60 * 2**20),
        cost_estimate=work(8),
        name="branch_back",
    )(place, *terms, *operands)


def attention_weight_kernel(place_ref, at_ref, *refs):
    normals, attended, refs = refs[:BLOCKS], refs[BLOCKS : 2 * BLOCKS], refs[2 * BLOCKS :]
    messages, weight_refs, refs = refs[:4], refs[4:8], refs[8:]
    heads_ref, logits_ref, low_ref, high_ref, gain_ref, *refs = refs
    out_refs, (small_ref, small_other_ref, made, weights) = refs[:SIDE], refs[SIDE:]
    y, x = place_ref[TILES], place_ref[TILES + 1]
    for ky in range(SIDE):
        for kx in range(SIDE):
            weights[((y + ky) % SIDE) * SIDE + (x + kx) % SIDE] = weight_refs[ky][kx]
    products = []
    branch = []
    for message in messages:
        branch += [message[:, :QUERY_COLS], message[:, QUERY_COLS:]]
    shard = made.shape[1]
    wide = 4 * shard
    for p in range(0, MODEL_WIDTH, wide):
        cols = slice(p, p + wide)
        one = two = None
        for b in range(BLOCKS):
            term = dot(normals[b][:, cols], heads_ref[b], ((0,), (0,)))
            one = term if b == 0 else one + term
            term = dot(attended[b][:, cols], branch[b], ((0,), (0,)))
            two = term if b == 0 else two + term
        weight = weights[p // shard : p // shard + 4].reshape(wide, HEAD_COLS).astype(F32)
        product = jnp.sum(one * weight, axis=1, keepdims=True)
        products.append(jnp.broadcast_to(product, (wide, 128)).T[:1])
        for q in range(4):
            rows = slice(q * shard, (q + 1) * shard)
            made[p // shard + q, :, :HEAD_COLS] = one[rows].astype(BF16)
            made[p // shard + q, :, HEAD_COLS:] = two[rows].astype(BF16)
    normal = jnp.concatenate([low_ref[...], high_ref[...]], 0)
    router = lax.dot_general(
        logits_ref[...],
        normal.astype(F32),
        (((1,), (0,)), ((), ())),
        precision=EXACT,
        preferred_element_type=F32,
    )
    rest = jnp.zeros((SMALL - EXPERTS - 2, MODEL_WIDTH), F32)
    small = jnp.concatenate([router, gain_ref[...], jnp.concatenate(products, 1), rest], 0)
    parts = [small[:, n * ROWS : (n + 1) * ROWS] for n in range(BLOCKS)]
    z, core = at_ref[0], at_ref[1]
    for b in range(BLOCKS):
        device = (z + b // 2) % 4 * 2 + (core + b) % 2
        part = parts[0]
        for n in range(1, BLOCKS):
            part = jnp.where(device == n, parts[n], part)
        (small_ref, small_other_ref)[b % 2][b // 2] = part
    for kx in range(SIDE):
        for ky in range(SIDE):
            part = made[((y + ky) % SIDE) * SIDE + (x + kx) % SIDE]
            out_refs[ky][kx] = part


def attention_weights(place, at, normals, attended, branch, weights, *operands):
    rows = MODEL_WIDTH // SIDE**2
    shape = (SIDE, rows, 2 * HALF)
    return pl.pallas_call(
        attention_weight_kernel,
        out_shape=tuple([jax.ShapeDtypeStruct(shape, BF16)] * SIDE)
        + tuple([jax.ShapeDtypeStruct((BLOCKS // 2, SMALL, ROWS), F32)] * 2),
        in_specs=[pl.BlockSpec(memory_space=pltpu.SMEM)] * 2
        + [pl.BlockSpec(memory_space=pltpu.VMEM)] * (2 * BLOCKS + 13),
        out_specs=tuple([pl.BlockSpec(memory_space=pltpu.VMEM)] * (SIDE + 2)),
        scratch_shapes=[
            pltpu.VMEM((SIDE * SIDE, rows, 2 * HALF), BF16),
            pltpu.VMEM((SIDE * SIDE, rows, HEAD_COLS), BF16),
        ],
        compiler_params=pltpu.CompilerParams(vmem_limit_bytes=60 * 2**20),
        cost_estimate=work(9),
        name="attention_weights",
    )(place, at, *normals, *attended, *branch, *weights, *operands)


def finish_kernel(place_ref, *refs):
    pairs, (weight_ref, tokens_ref, gain_ref, grad_hidden_ref, out_ref) = refs[:4], refs[4:]
    z, core = place_ref[0], place_ref[1]
    at = [((z + kz) % 4) * 2 + (core + kc) % 2 for kz in range(4) for kc in range(2)]
    parts = [
        pairs[b // 2][:, b % 2 * HEAD_COLS : (b % 2 + 1) * HEAD_COLS].astype(F32)
        for b in range(BLOCKS)
    ]
    natural = []
    for n in range(BLOCKS):
        part = parts[0]
        for b in range(1, BLOCKS):
            part = jnp.where(at[b] == n, parts[b], part)
        natural.append(part)
    natural = jnp.concatenate(natural, 1).astype(BF16)
    grad_normal = dot(natural, weight_ref[...], ((1,), (1,)))
    inputs = tokens_ref[...].astype(F32)
    scale = lax.rsqrt(jnp.mean(inputs * inputs, axis=-1, keepdims=True) + EPSILON)
    weighted = grad_normal * gain_ref[...]
    inner = jnp.mean(weighted * inputs, axis=-1, keepdims=True)
    grad_inputs = scale * weighted - inputs * (scale * scale * scale * inner)
    out_ref[...] = (grad_inputs + grad_hidden_ref[...]).astype(BF16)


def finish(place, pairs, *operands):
    return pl.pallas_call(
        finish_kernel,
        out_shape=jax.ShapeDtypeStruct((ROWS, MODEL_WIDTH), BF16),
        in_specs=[pl.BlockSpec(memory_space=pltpu.SMEM)]
        + [pl.BlockSpec(memory_space=pltpu.VMEM)] * 8,
        out_specs=pl.BlockSpec(memory_space=pltpu.VMEM),
        compiler_params=pltpu.CompilerParams(vmem_limit_bytes=60 * 2**20),
        cost_estimate=work(9),
        name="finish",
    )(place, *pairs, *operands)


def spread_kernel(at_ref, mine_ref, other_ref, *out_refs):
    z, core = at_ref[0], at_ref[1]
    begin = 0
    for n in range(BLOCKS):
        kz = (n // 2 + 4 - z) % 4
        block = jnp.where(core == n % 2, mine_ref[kz].astype(F32), other_ref[kz].astype(F32))
        begin = 0
        for out, wide in zip(out_refs, (QUERY_COLS, HEAD_SIZE, HEAD_SIZE, QUERY_COLS)):
            out[:, n * wide : (n + 1) * wide] = block[:, begin : begin + wide]
            begin += wide
        small = block[:, begin : begin + ROWS]
        out_refs[4][:, n * ROWS : (n + 1) * ROWS] = small[:SMALL] + small[SMALL:]


def spread(at, mine, other):
    rows = mine.shape[1]
    wide = (BLOCKS * QUERY_COLS, BLOCKS * HEAD_SIZE, BLOCKS * HEAD_SIZE, BLOCKS * QUERY_COLS)
    return pl.pallas_call(
        spread_kernel,
        out_shape=tuple(jax.ShapeDtypeStruct((rows, w), F32) for w in wide)
        + (jax.ShapeDtypeStruct((SMALL, MODEL_WIDTH), F32),),
        in_specs=[pl.BlockSpec(memory_space=pltpu.SMEM)]
        + [pl.BlockSpec(memory_space=pltpu.VMEM)] * 2,
        out_specs=tuple([pl.BlockSpec(memory_space=pltpu.VMEM)] * 5),
        compiler_params=pltpu.CompilerParams(vmem_limit_bytes=60 * 2**20),
        cost_estimate=work(3),
        name="spread",
    )(at, mine, other)


PER_STEP = 2
GATHER_STEPS = 1
EXPERT_STEPS = GATHER_STEPS + LOCAL_EXPERTS


def slots_hit(slot_ref, block):
    slot = lax.broadcasted_iota(jnp.int32, (SLOTS, ROWS), 0)
    slot = jnp.where(slot < CAP, slot, -2)
    return [slot_ref[block, e : e + 1, :] == slot for e in range(LOCAL_EXPERTS)]


def expert_kernel(device_ref, slot_ref, all_slots_ref, router_ref, *refs):
    normal_refs, refs = refs[: 2 * BLOCKS], refs[2 * BLOCKS :]
    grad_refs, refs = refs[: 2 * BLOCKS], refs[2 * BLOCKS :]
    (
        weight_one_ref,
        weight_two_ref,
        mixed_ref,
        mixed_other_ref,
        grad_mixed_ref,
        grad_mixed_other_ref,
        weights_ref,
        own_gates_ref,
        held,
        grad_held,
        gates,
        grad_gates,
    ) = refs
    step = pl.program_id(0)

    @pl.when(step < GATHER_STEPS)
    def _():
        device = device_ref[0]
        expert_at = lax.broadcasted_iota(jnp.int32, (EXPERTS, ROWS), 0)
        for block in range(BLOCKS):
            used = all_slots_ref[block] >= 0
            halves = slice(2 * block, 2 * block + 2)
            normal = jnp.concatenate([ref[...] for ref in normal_refs[halves]], 0)
            grads = jnp.concatenate([ref[...] for ref in grad_refs[halves]], 0)
            logits = dot(router_ref[...], normal, ((1,), (1,)))
            logits = jnp.where(used, logits, MASKED)
            gate = jnp.exp(logits - jnp.max(logits, axis=0, keepdims=True))
            gate = jnp.where(used, gate, 0.0)
            gate = gate / jnp.sum(gate, axis=0, keepdims=True)
            if block == 0:
                own_gates_ref[...] = gate
            hits = slots_hit(slot_ref, block)
            spread = []
            for e in range(LOCAL_EXPERTS):
                row = jnp.sum(
                    jnp.where(expert_at == e * BLOCKS + device, gate, 0.0), axis=0, keepdims=True
                )
                spread.append(jnp.sum(jnp.where(hits[e], row, 0.0), axis=1, keepdims=True))
            chosen = jnp.concatenate(hits, 0).astype(F32).astype(BF16)
            rows = dot(chosen, normal).astype(BF16)
            grads = dot(chosen, grads).astype(BF16)
            for e in range(LOCAL_EXPERTS):
                part = slice(e * SLOTS, (e + 1) * SLOTS)
                held[e, block] = rows[part]
                grad_held[e, block] = grads[part]
                gates[e, block] = spread[e]

    @pl.when((step >= GATHER_STEPS) & (step < EXPERT_STEPS))
    def _():
        e = step - GATHER_STEPS
        blocked = (BLOCKS, SLOTS, MODEL_WIDTH)
        rows = held[e].reshape(EXPERT_ROWS, MODEL_WIDTH)
        made = dot(rows, weight_one_ref[0])
        gate_part = made[:, :FF]
        up_part = made[:, FF:]
        sigmoid_gate = jax.nn.sigmoid(gate_part)
        activation = gate_part * sigmoid_gate
        hidden = (activation * up_part).astype(BF16)
        out = dot(hidden, weight_two_ref[0]).astype(BF16).astype(F32)
        gate = gates[e].reshape(EXPERT_ROWS, 1)
        grads = grad_held[e].reshape(EXPERT_ROWS, MODEL_WIDTH).astype(F32)
        grad_gates[e] = jnp.sum(out * grads, axis=1, keepdims=True).reshape(BLOCKS, SLOTS, 1)
        held[e] = (out * gate).astype(BF16).reshape(blocked)
        grad_out = (grads * gate).astype(BF16)
        grad_hidden = dot(grad_out, weight_two_ref[0], ((1,), (1,)))
        grad_gate = (
            grad_hidden * up_part * sigmoid_gate * (1.0 + gate_part * (1.0 - sigmoid_gate))
        )
        grad_up = grad_hidden * activation
        grad_made = jnp.concatenate([grad_gate, grad_up], 1).astype(BF16)
        grad_rows = dot(grad_made, weight_one_ref[0], ((1,), (1,))).astype(BF16)
        grad_held[e] = grad_rows.reshape(blocked)
        parts, _, wide, _ = weights_ref.shape
        for p in range(0, parts, 4):
            cols = slice(p * wide, (p + 4) * wide)
            one = dot(rows[:, cols], grad_made, ((0,), (0,))).astype(BF16)
            two = dot(grad_out[:, cols], hidden, ((0,), (0,))).astype(BF16)
            for q in range(4):
                weights_ref[p + q, 0, :, : 2 * FF] = one[q * wide : (q + 1) * wide]
                weights_ref[p + q, 0, :, 2 * FF :] = two[q * wide : (q + 1) * wide]

    @pl.when(step >= EXPERT_STEPS)
    def _():
        for b in range(PER_STEP):
            block = (step - EXPERT_STEPS) * PER_STEP + b
            hits = slots_hit(slot_ref, block)
            parts = []
            for e in range(LOCAL_EXPERTS):
                part = jnp.where(hits[e], grad_gates[e, block], 0.0)
                parts.append(jnp.sum(part, axis=0, keepdims=True))
                parts.append(jnp.zeros((1, GATE_COLS - ROWS), F32))
            parts.append(jnp.zeros((1, MODEL_WIDTH - LOCAL_EXPERTS * GATE_COLS), F32))
            row = jnp.concatenate(parts, 1)
            at = lax.broadcasted_iota(jnp.int32, (BLOCKS, MODEL_WIDTH), 0)
            row = jnp.where(at == device_ref[0], row, 0.0)
            high = row.astype(BF16).astype(F32)
            row = jnp.concatenate([high, row - high], 0).astype(BF16)
            chosen = jnp.concatenate(hits, 0).astype(F32).astype(BF16)
            mixed = jnp.concatenate([held[e, block] for e in range(LOCAL_EXPERTS)], 0)
            to = (mixed_ref, mixed_other_ref)[b]
            to[0] = dot(chosen, mixed, ((0,), (0,))).astype(BF16)
            mixed = jnp.concatenate([grad_held[e, block] for e in range(LOCAL_EXPERTS)], 0)
            to = (grad_mixed_ref, grad_mixed_other_ref)[b]
            to[0, :ROWS, :] = dot(chosen, mixed, ((0,), (0,))).astype(BF16)
            to[0, ROWS:, :] = row


def expert_layer(device, slots, all_slots, router, normals, grads, weight_one, weight_two):
    steps = EXPERT_STEPS + BLOCKS // PER_STEP

    def working(s):
        return (jnp.clip(s - GATHER_STEPS, 0, LOCAL_EXPERTS - 1), 0, 0)

    def ending(s):
        return (jnp.maximum(s - EXPERT_STEPS, 0), 0, 0)

    def kept(shape):
        return pl.BlockSpec(shape, lambda s: (0,) * len(shape), pipeline_mode=pl.Buffered(1))

    table = (BLOCKS, LOCAL_EXPERTS, ROWS)
    row_block = (1, ROWS, MODEL_WIDTH)
    return pl.pallas_call(
        expert_kernel,
        grid=(steps,),
        out_shape=(
            jax.ShapeDtypeStruct((BLOCKS // 2, ROWS, MODEL_WIDTH), BF16),
            jax.ShapeDtypeStruct((BLOCKS // 2, ROWS, MODEL_WIDTH), BF16),
            jax.ShapeDtypeStruct((BLOCKS // 2, ROWS + EXTRA, MODEL_WIDTH), BF16),
            jax.ShapeDtypeStruct((BLOCKS // 2, ROWS + EXTRA, MODEL_WIDTH), BF16),
            jax.ShapeDtypeStruct(
                (SIDE * SIDE, LOCAL_EXPERTS, MODEL_WIDTH // SIDE**2, 3 * FF), BF16
            ),
            jax.ShapeDtypeStruct((EXPERTS, ROWS), F32),
        ),
        in_specs=[
            pl.BlockSpec(memory_space=pltpu.SMEM),
            kept(table),
            kept((BLOCKS, EXPERTS, ROWS)),
            kept((EXPERTS, MODEL_WIDTH)),
        ]
        + [kept((ROWS // 2, MODEL_WIDTH))] * (4 * BLOCKS)
        + [
            pl.BlockSpec((1, MODEL_WIDTH, 2 * FF), working),
            pl.BlockSpec((1, FF, MODEL_WIDTH), working),
        ],
        out_specs=(
            pl.BlockSpec(row_block, ending),
            pl.BlockSpec(row_block, ending),
            pl.BlockSpec((1, ROWS + EXTRA, MODEL_WIDTH), ending),
            pl.BlockSpec((1, ROWS + EXTRA, MODEL_WIDTH), ending),
            pl.BlockSpec(
                (SIDE * SIDE, 1, MODEL_WIDTH // SIDE**2, 3 * FF),
                lambda s: (0, jnp.clip(s - GATHER_STEPS, 0, LOCAL_EXPERTS - 1), 0, 0),
            ),
            whole((EXPERTS, ROWS)),
        ),
        scratch_shapes=[
            pltpu.VMEM((LOCAL_EXPERTS, BLOCKS, SLOTS, MODEL_WIDTH), BF16),
            pltpu.VMEM((LOCAL_EXPERTS, BLOCKS, SLOTS, MODEL_WIDTH), BF16),
            pltpu.VMEM((LOCAL_EXPERTS, BLOCKS, SLOTS, 1), F32),
            pltpu.VMEM((LOCAL_EXPERTS, BLOCKS, SLOTS, 1), F32),
        ],
        compiler_params=pltpu.CompilerParams(vmem_limit_bytes=60 * 2**20),
        cost_estimate=work(50),
        name="expert_layer",
    )(device, slots, all_slots, router, *normals, *grads, weight_one, weight_two)


def local(
    n_dp,
    tokens,
    cotangent,
    seq_lengths,
    position_map,
    routes,
    turn_order,
    norm_gain,
    ffn_gain,
    w_query,
    key_weight,
    value_weight,
    w_out,
    w_router,
    w_gate_up,
    w_down,
):
    group = Group(BLOCKS)
    index = lax.axis_index("expert")
    shard = w_query.shape[0]

    inputs_wide = tokens.astype(F32)
    scale_one = lax.rsqrt(jnp.mean(inputs_wide * inputs_wide, axis=-1, keepdims=True) + EPSILON)
    normal_one = (inputs_wide * scale_one * norm_gain).astype(BF16)
    by_heads = jnp.concatenate(
        [
            w_query.reshape(shard, BLOCKS, QUERY_COLS),
            key_weight.reshape(shard, BLOCKS, HEAD_SIZE),
            value_weight.reshape(shard, BLOCKS, HEAD_SIZE),
        ],
        2,
    )
    own_heads = after(lax.dynamic_index_in_dim(by_heads, index, 1, keepdims=False), normal_one)
    below, above = group.send(normal_one, 1), group.send(normal_one, -1)
    row = [own_heads] + [send_dp(own_heads, 0, -k) for k in range(1, SIDE)]
    own_slots = slot_table(routes, turn_order[0]).reshape(BLOCKS, LOCAL_EXPERTS, ROWS)
    own_slots = jnp.transpose(own_slots, (1, 0, 2)).astype(BF16).reshape(EXPERTS, ROWS)
    own_slots = jnp.concatenate([own_slots, jnp.zeros((SMALL - EXPERTS, ROWS), BF16)], 0)
    row, own_slots, below, above = lax.optimization_barrier((row, own_slots, below, above))
    row = stack(row)
    own_heads = [row] + [send_dp(row, -k, 0) for k in range(1, SIDE)]
    far = group.send(after(normal_one, row), 2)
    position_map, seq_lengths = after((position_map, seq_lengths), own_heads[2])

    lengths = seq_lengths[0]
    stream = group.to_blocks(position_map[0].reshape(BLOCKS, ROWS)).reshape(GROUP)
    ordered = jnp.arange(GROUP, dtype=jnp.int32)
    begin_ordered = stream_starts(lengths, ordered)
    cosine, sine = rotary(stream - stream_starts(lengths, stream))
    first = begin_ordered[::TILE] // TILE
    at_dp = lax.axis_index("dp")
    first_dp = jnp.concatenate([first, jnp.stack([at_dp // SIDE, at_dp % SIDE])])
    begin = jnp.tile(begin_ordered.reshape(TILES, 1, TILE), (1, 1, GROUPED))
    stream_row = stream[None, :]

    own_heads, far, below, above, cosine, sine, stream_row, begin, first_dp = (
        lax.optimization_barrier(
            (own_heads, far, below, above, cosine, sine, stream_row, begin, first_dp)
        )
    )
    normals = group.both_cores([normal_one, above, far, below])
    out_full = lax.all_gather(after(w_out, row), "dp", axis=0, tiled=True)

    half = ROWS // 2
    grads = after([cotangent[:half], cotangent[half:]], *normals)
    grads_near = group.near_halves(*grads)
    made = attend(first_dp, normals, own_heads, cosine, sine, stream_row, begin, own_slots)
    made, grads_near = lax.optimization_barrier((made, grads_near))
    mixed, other, query, key, value, log_total, turned = made

    heads_full = lax.all_gather(
        after(by_heads, mixed).reshape(shard, BLOCKS * HEAD_COLS), "dp", axis=0, tiled=True
    )
    attended = group.exchange(mixed, other)
    out_full, attended, grads = lax.optimization_barrier((out_full, attended, grads))
    grads_far = group.far_halves(grads_near)
    grads_swapped = [group.swap(half) for half in grads_near[:3]]
    place = jnp.stack([group.z, group.core])
    made = project(place, attended, out_full, tokens, ffn_gain[None])
    made, grads_far, grads_swapped = lax.optimization_barrier((made, grads_far, grads_swapped))
    hidden_one, scale_two, *normal_two = made
    near = group.near_halves(*normal_two)
    own, grads, late, grads_far, near[1], near[2] = lax.optimization_barrier(
        (normal_two, grads, grads_near[3], grads_far, near[1], near[2])
    )
    own = [group.swap(half) for half in own]
    far = group.far_halves(near)
    grads_swapped = [group.swap(half) for half in grads] + grads_swapped
    grads_swapped += [group.swap(half) for half in [late] + grads_far]
    grads = group.all_halves(grads, grads_near, grads_far, grads_swapped)
    ordered_late, begin_late = after((ordered, begin_ordered), *normal_two)
    cosine_ordered, sine_ordered = rotary(ordered_late - begin_late)
    blocks = [pair[:, c * ROWS : (c + 1) * ROWS] for pair in attended for c in range(2)]
    slots = jnp.stack([block[ROWS : ROWS + EXPERTS] for block in blocks], 0).astype(jnp.int32)
    attended = jnp.stack([block[:ROWS] for block in blocks], 0)
    own_slots = lax.dynamic_index_in_dim(
        slots.reshape(BLOCKS, LOCAL_EXPERTS, BLOCKS, ROWS), index, 2, keepdims=False
    )
    far, grads, slots, own_slots, cosine_ordered, sine_ordered = lax.optimization_barrier(
        (far, grads, slots, own_slots, cosine_ordered, sine_ordered)
    )
    swapped = own + [group.swap(half) for half in near + far]
    normals_two = group.all_halves(normal_two, near, far, swapped)

    attended = group.to_natural(attended)
    attended = jnp.transpose(attended, (1, 0, 2)).reshape(ROWS, QUERY_HEADS * HEAD_SIZE)
    attended_all = group.along_z(after(attended, *normals_two))

    router = w_router.T.reshape(BLOCKS, LOCAL_EXPERTS, MODEL_WIDTH)
    router = jnp.transpose(router, (1, 0, 2)).reshape(EXPERTS, MODEL_WIDTH)
    made = expert_layer(
        index[None], own_slots, slots, router, normals_two, grads, w_gate_up, w_down
    )
    made, attended_all = lax.optimization_barrier((made, attended_all))
    mixture, mixture_other, grad_mixture, grad_mixture_other = made[:4]
    expert_grads, own_gates = made[4:]
    other = group.swap(grad_mixture_other)
    def total(kz, begin, end):
        mine, theirs = grad_mixture[kz, begin:end], other[kz, begin:end]
        return mine.astype(F32) + theirs.astype(F32)

    end = ROWS + EXTRA
    far = [total(2, 0, half).astype(BF16), total(2, half, end).astype(BF16)]
    ready = [total(1, half, end).astype(BF16), total(3, 0, half).astype(BF16)]
    waiting = [total(1, 0, half), total(3, half, end), total(0, 0, end)]
    far, ready, waiting = lax.optimization_barrier((far, ready, waiting))
    far = [group.send(far[0], 1), group.send(far[1], -1)]
    ready = [group.send(ready[0], 1), group.send(ready[1], -1)]
    above, below = waiting[0] + far[0].astype(F32), waiting[1] + far[1].astype(F32)
    above, below = group.send(above.astype(BF16), 1), group.send(below.astype(BF16), -1)
    grad_terms = [waiting[2], above, ready[0], ready[1], below]
    expert_grads = lax.psum_scatter(expert_grads, "dp", scatter_dimension=0, tiled=True)[0]

    mixture_other, attended_all = after((mixture_other, attended_all), *grad_terms)
    mixture_other = group.swap(mixture_other)
    attended_all = group.both_cores(attended_all)
    made = branch_back(
        place,
        grad_terms,
        hidden_one,
        scale_two,
        ffn_gain[None],
        cotangent,
        own_gates,
        router,
        out_full,
    )
    made, mixture_other, attended_all = lax.optimization_barrier(
        (made, mixture_other, attended_all)
    )
    grad_hidden_one, mine, other, branch, branch_other, grad_logits, local_ffn_gain = made
    attended_grad = group.exchange(mine, other)
    mixture = group.sum_cores(mixture, after(mixture_other, mine))
    branch_other = group.swap(branch_other)
    messages = [jnp.concatenate([branch[kz], branch_other[kz]], 1) for kz in range(4)]
    attended_grad, messages, mixture = lax.optimization_barrier((attended_grad, messages, mixture))
    mixture[1], mixture[3] = group.send(mixture[1], 1), group.send(mixture[3], 3)
    messages = messages[:1] + [group.send(messages[4 - kz], 4 - kz) for kz in range(1, 4)]
    head_grads = attend_back(
        first,
        *attended_grad,
        query,
        key,
        value,
        log_total,
        turned,
        cosine_ordered,
        sine_ordered,
        stream_row,
        stream[:, None],
        begin,
    )
    head_grads, messages, mixture = lax.optimization_barrier((head_grads, messages, mixture))
    mine, other, head_grads = head_grads
    local_grads = attention_weights(
        first_dp,
        place,
        normals,
        attended_all,
        messages,
        own_heads,
        head_grads,
        grad_logits,
        *normal_two,
        local_ffn_gain,
    )
    *by_y, small, small_other = local_grads
    mine, other, *by_y = lax.optimization_barrier((mine, other, *by_y))
    from_y = [send_dp(by_y[k], k, 0) for k in range(1, SIDE)]
    small = group.exchange(small, small_other)
    own_grads = group.exchange(mine, other)
    from_y, small = lax.optimization_barrier((from_y, small))
    small = sum(pair[:, :ROWS] + pair[:, ROWS:] for pair in small)
    row = by_y[0].astype(F32) + sum(term.astype(F32) for term in from_y)
    rest = jnp.zeros((2 * SMALL, 2 * HALF - ROWS), BF16)
    behind = jnp.concatenate([in_halves(small), rest], 1)
    from_x = [
        send_dp(jnp.concatenate([row[k].astype(BF16), behind], 0), 0, k) for k in range(1, SIDE)
    ]
    d_tokens = finish(place, own_grads, heads_full, tokens, norm_gain[None], grad_hidden_one)
    from_x, d_tokens = lax.optimization_barrier((from_x, d_tokens))
    parts = row[0] + sum(term[:shard].astype(F32) for term in from_x)
    small = small + sum(from_halves(term[shard:, :ROWS]) for term in from_x)
    row = [send_dp(small, k, 0) for k in range(1, SIDE)]
    mixture[2] = group.send(mixture[2], 2)
    row, mixture, expert_grads = lax.optimization_barrier((row, mixture, expert_grads))
    small = small + sum(row)
    parts = jnp.concatenate([parts.astype(BF16), in_halves(small)], 1)
    parts = jnp.stack(group.along_z(parts), 0)
    grad_query, grad_key, grad_value, grad_out, small = spread(place, parts, group.swap(parts))
    grad_gate_up = expert_grads[:, :, : 2 * FF].astype(F32)
    grad_down = jnp.transpose(expert_grads[:, :, 2 * FF :], (0, 2, 1)).astype(F32)
    output = (hidden_one + sum(term.astype(F32) for term in mixture)).astype(BF16)
    grad_router = small[:EXPERTS].reshape(LOCAL_EXPERTS, BLOCKS, MODEL_WIDTH)
    grad_router = jnp.transpose(grad_router, (2, 1, 0)).reshape(MODEL_WIDTH, EXPERTS)

    return (
        output,
        d_tokens,
        small[EXPERTS + 1] / norm_gain,
        small[EXPERTS],
        grad_query,
        grad_key,
        grad_value,
        grad_out,
        grad_router,
        grad_gate_up,
        grad_down,
    )


def solution(mesh):
    placed = (
        P(("dp", "expert"), None),
        P(("dp", "expert"), None),
        P("dp", None),
        P("dp", None),
        P(("dp", "expert"), None),
        P(("dp", "expert"), None),
        P(),
        P(),
        P("dp", None),
        P("dp", None),
        P("dp", None),
        P("dp", None),
        P(),
        P("expert", None, None),
        P("expert", None, None),
    )
    return jax.shard_map(
        functools.partial(local, mesh.shape["dp"]),
        mesh=mesh,
        in_specs=placed,
        out_specs=(
            P(("dp", "expert"), None),
            P(("dp", "expert"), None),
            P(),
            P(),
            P("dp", None),
            P("dp", None),
            P("dp", None),
            P("dp", None),
            P(),
            P("expert", "dp", None),
            P("expert", None, "dp"),
        ),
        check_vma=False,
    )
```
